32 devices in a mesh: parts: 2 (over x), dp: 16 (over z, y, core).
Axes of the slice: x: 2, y: 2, z: 4, core: 2. Of those that a mesh axis runs over, the one named last changes fastest.
Arguments:
- activations: bfloat16 [4096, 8192], P(('parts', 'dp')), parts along dimension 0, may hold values from -6 to 6
- out_grads: bfloat16 [4096, 28672], P(('parts', 'dp')), parts along dimension 0, may hold values from -6 to 6
- in_basis: bfloat16 [8192, 64], P('dp'), may hold values from -0.0625 to 0.0625
- out_basis: bfloat16 [28672, 64], P('dp'), may hold values from -0.03125 to 0.03125
- preconditioner: bfloat16 [4096, 4096], P('dp'), may hold values from -0.09375 to 0.09375
- queries: bfloat16 [128, 4096], P('dp'), may hold values from -6 to 6
Outputs:
- scores: float32 [4, 128], P('parts', 'dp'), parts along dimension 0
The draws below stay inside these ranges and needn't reach their ends.
There are 2 independent parts, one for each index of `parts`. The reference program is written for one: setup_inputs(seed, part) draws one part's arguments, and reference() takes and returns one part's arrays. A program takes and returns all parts, laid end to end along the dimension named above; an argument that names none is the same for every part. Nothing has to cross between parts.
All inputs are finite; a program needn't handle non-finite values.
Results may differ from the reference program's by a relative error of at most 0.0061.
Values may be sent and summed in bfloat16 or wider, within the bound.
No kernel may reach another device: no remote copies, remote signals or barrier semaphores. Data moves between devices by JAX's collectives and lax.ppermute only.
A program may use at most 64 MiB of HBM per device.

```python
import math
import jax
import jax.numpy as jnp
from jax import lax

D = 8192
FF = 28672
R = 64
LEN = 1024
RR = 4096
SEQS = 2
TOKENS = 2048
QUERIES = 128


def block_scale(stream_key, extent, pieces, low, high):
    def one(position, shards_of):
        draws = jax.random.uniform(jax.random.fold_in(jax.random.fold_in(stream_key, 6), position), (shards_of,), jnp.float32, low / len(pieces), high / len(pieces))
        return jnp.repeat(jnp.exp(draws), extent[position] // shards_of).reshape((-1,) + (1,) * (len(extent) - position - 1))

    gain = one(*pieces[0])
    for cut in pieces[1:]:
        gain = gain * one(*cut)
    return gain


def gaussian(own_key, shape, deviation, bound, split=(), dtype=jnp.bfloat16):
    factor_of = block_scale(own_key, shape, split, -0.22, 0.18) if split else 1.0
    drawn = jax.random.normal(own_key, shape, jnp.float32) * deviation * factor_of
    return jnp.minimum(jnp.maximum(drawn, -bound), bound).astype(dtype)


def setup_inputs(seed: int = 0, part: int = 0) -> dict:
    keys = jax.random.split(jax.random.key(seed), 7)
    part_keys = jax.random.split(jax.random.fold_in(keys[6], part), 7)
    activations = gaussian(part_keys[0], (TOKENS, D), 1.0, 6.0, ((0, 16),))
    out_grads = gaussian(part_keys[1], (TOKENS, FF), 1.0, 6.0, ((0, 16),))
    in_basis = gaussian(keys[2], (D, R), D ** -0.5, 0.0625, ((0, 16),))
    out_basis = gaussian(keys[3], (FF, R), FF ** -0.5, 0.03125, ((0, 16),))
    preconditioner = gaussian(keys[4], (RR, RR), RR ** -0.5, 0.09375, ((0, 16),))
    queries = gaussian(keys[5], (QUERIES, RR), 1.0, 6.0, ((0, 16),))
    return dict(activations=activations, out_grads=out_grads, in_basis=in_basis, out_basis=out_basis, preconditioner=preconditioner, queries=queries)


def reference(activations, out_grads, in_basis, out_basis, preconditioner, queries):
    act_proj = jnp.dot(activations, in_basis, preferred_element_type=jnp.float32).astype(jnp.bfloat16)
    grad_proj = jnp.dot(out_grads, out_basis, preferred_element_type=jnp.float32).astype(jnp.bfloat16)
    act_seq = act_proj.astype(jnp.float32).reshape(SEQS, LEN, R)
    grad_seq = grad_proj.astype(jnp.float32).reshape(SEQS, LEN, R)
    raw_features = jnp.einsum('sti,stj->sij', grad_seq, act_seq).reshape(SEQS, R * R)
    raw_features = raw_features * (1.0 / math.sqrt(LEN))
    features = raw_features.astype(jnp.bfloat16)
    conditioned = lax.dot_general(features, preconditioner, (((1,), (1,)), ((), ())), preferred_element_type=jnp.float32).astype(jnp.bfloat16)
    scores = lax.dot_general(conditioned, queries, (((1,), (1,)), ((), ())), preferred_element_type=jnp.float32)
    return scores * (1.0 / R)
```

```python
import functools
import math

import jax
import jax.numpy as jnp
from jax import lax
from jax.experimental import pallas as pl
from jax.experimental.pallas import tpu as pltpu
from jax.sharding import PartitionSpec as P

LEN = 1024
NT = (((1,), (1,)), ((), ()))
TN = (((0,), (0,)), ((), ()))


def dot(a, b, dims):
    return lax.dot_general(a, b, dims, preferred_element_type=jnp.float32)


def factors(n):
    rest = n // 2
    inner = 1
    while inner * inner * 4 <= rest:
        inner *= 2
    return rest // inner, inner, 2


def shift(x, sizes, steps):
    pairs = []
    for a in range(sizes[0]):
        for b in range(sizes[1]):
            for c in range(sizes[2]):
                to = [(i + s) % m for i, s, m in zip((a, b, c), steps, sizes)]
                pairs.append(
                    ((a * sizes[1] + b) * sizes[2] + c, (to[0] * sizes[1] + to[1]) * sizes[2] + to[2])
                )
    return lax.ppermute(x, "dp", pairs)


def owner(sizes, steps):
    me = lax.axis_index("dp")
    c = lax.rem(me, sizes[2])
    b = lax.rem(me // sizes[2], sizes[1])
    a = me // (sizes[1] * sizes[2])
    a, b, c = (lax.rem(i + m - s, m) for i, s, m in zip((a, b, c), steps, sizes))
    return (a * sizes[1] + b) * sizes[2] + c


def project_kernel(sizes, steps, width, carry, *refs):
    count = len(steps)
    act, grad = refs[:2]
    pieces = refs[2 : 2 + count]
    refs = refs[2 + count :]
    if carry:
        a_in, g_in = refs[:2]
        refs = refs[2:]
    a_out, g_out, a_buf, g_buf, sems = refs
    g_width = pieces[0].shape[1] - width
    copies = []
    for i, step in enumerate(steps):
        index = owner(sizes, step)
        a_copy = pltpu.make_async_copy(
            act.at[:, pl.ds(pl.multiple_of(index * width, 128), width)], a_buf.at[i], sems.at[0, i]
        )
        g_copy = pltpu.make_async_copy(
            grad.at[:, pl.ds(pl.multiple_of(index * g_width, 128), g_width)], g_buf.at[i], sems.at[1, i]
        )
        a_copy.start()
        g_copy.start()
        copies.append((a_copy, g_copy))
    if carry:
        a_sum, g_sum = a_in[...], g_in[...]
    else:
        a_sum = g_sum = jnp.zeros(a_out.shape, jnp.float32)
    for i, (a_copy, g_copy) in enumerate(copies):
        a_copy.wait()
        a_sum += dot(a_buf[i], pieces[i][:, :width], NT)
        g_copy.wait()
        g_sum += dot(g_buf[i], pieces[i][:, width:], NT)
    a_out[...] = a_sum
    g_out[...] = g_sum


def project(act, grad, pieces, steps, sizes, width, rank, carry=None):
    rows = act.shape[0]
    count = len(pieces)
    g_width = pieces[0].shape[1] - width
    vmem = pl.BlockSpec(memory_space=pltpu.VMEM)
    hbm = pl.BlockSpec(memory_space=pl.ANY)
    total = jax.ShapeDtypeStruct((rows, rank), jnp.float32)
    carried = () if carry is None else carry
    return pl.pallas_call(
        functools.partial(project_kernel, sizes, steps, width, carry is not None),
        out_shape=(total, total),
        in_specs=[hbm, hbm] + [vmem] * (count + len(carried)),
        out_specs=(vmem, vmem),
        scratch_shapes=[
            pltpu.VMEM((count, rows, width), act.dtype),
            pltpu.VMEM((count, rows, g_width), act.dtype),
            pltpu.SemaphoreType.DMA((2, count)),
        ],
        compiler_params=pltpu.CompilerParams(vmem_limit_bytes=32 * 2**20),
        cost_estimate=pl.CostEstimate(
            flops=2 * count * rows * rank * (width + g_width),
            bytes_accessed=count * (rows + rank) * (width + g_width) * 2,
            transcendentals=0,
        ),
    )(act, grad, *pieces, *carried)


def projections(activations, out_grads, in_basis, out_basis, sizes):
    width, rank = in_basis.shape
    run = functools.partial(project, activations, out_grads, sizes=sizes, width=width, rank=rank)
    own = jnp.concatenate([in_basis.T, out_basis.T], axis=1)
    level = [((a, 0, 0), own if a == 0 else shift(own, sizes, (a, 0, 0))) for a in range(sizes[0])]
    level2 = [((s[0], b, 0), shift(x, sizes, (0, b, 0))) for b in range(1, sizes[1]) for s, x in level]
    level3 = [((s[0], s[1], 1), shift(x, sizes, (0, 0, 1))) for s, x in level + level2]
    carry = None
    for group in (level, level2, level3):
        steps, pieces = zip(*group)
        carry = run(pieces=pieces, steps=steps, carry=carry)
    return carry


def spread(x, sizes, one_level):
    return [
        (s, x if s == (0, 0, 0) else shift(x, sizes, s))
        for s in one_level
    ]


def local(activations, out_grads, in_basis, out_basis, preconditioner, queries):
    rows = activations.shape[0]
    width, rank = in_basis.shape
    n = activations.shape[1] // width
    sizes = factors(n)
    split = LEN // rows
    act_sum, grad_sum = projections(activations, out_grads, in_basis, out_basis, sizes)
    raw = dot(grad_sum.astype(jnp.bfloat16), act_sum.astype(jnp.bfloat16), TN)
    raw = raw.reshape(1, rank * rank) * (1.0 / math.sqrt(LEN))
    group = sizes[1] * sizes[2]
    inner = [(0, b, c) for b in range(sizes[1]) for c in range(sizes[2])]
    outer = [(a, 0, 0) for a in range(sizes[0])]
    summed = sum(x for _, x in spread(raw, sizes, inner))
    blocks = spread(summed, sizes, outer)
    sequences = n // split
    rows_of = lax.broadcasted_iota(jnp.int32, (sequences, 1), 0)
    features = sum(
        jnp.where(owner(sizes, s) // split == rows_of, x, 0.0) for s, x in blocks
    ).astype(jnp.bfloat16)
    conditioned = dot(features, preconditioner, NT).astype(jnp.bfloat16)
    out = preconditioner.shape[0]
    steps = [(a, b, c) for a, _, _ in outer for _, b, c in inner]
    terms = [
        dot(x, lax.dynamic_slice_in_dim(queries, owner(sizes, s) * out, out, axis=1), NT)
        for s, x in spread(conditioned, sizes, steps)
    ]
    return sum(terms) * (1.0 / rank)


def local_gathered(activations, out_grads, in_basis, out_basis, preconditioner, queries):
    rows = activations.shape[0]
    rank = in_basis.shape[1]
    act_proj = jnp.dot(
        activations,
        lax.all_gather(in_basis, "dp", axis=0, tiled=True),
        preferred_element_type=jnp.float32,
    ).astype(jnp.bfloat16)
    grad_proj = jnp.dot(
        out_grads,
        lax.all_gather(out_basis, "dp", axis=0, tiled=True),
        preferred_element_type=jnp.float32,
    ).astype(jnp.bfloat16)
    raw = dot(grad_proj, act_proj, TN).reshape(1, rank * rank) * (1.0 / math.sqrt(LEN))
    gathered = lax.all_gather(raw, "dp", axis=0, tiled=True)
    features = gathered.reshape(-1, LEN // rows, rank * rank).sum(axis=1).astype(jnp.bfloat16)
    conditioned = dot(features, preconditioner, NT).astype(jnp.bfloat16)
    scores = dot(lax.all_gather(conditioned, "dp", axis=1, tiled=True), queries, NT)
    return scores * (1.0 / rank)


def solution(mesh):
    n = mesh.shape["dp"]

    def body(activations, out_grads, in_basis, out_basis, preconditioner, queries):
        aligned = in_basis.shape[0] % 128 == 0 and out_basis.shape[0] % 128 == 0
        regular = aligned and (LEN // activations.shape[0]) % (factors(n)[1] * 2) == 0
        form = local if regular else local_gathered
        return form(activations, out_grads, in_basis, out_basis, preconditioner, queries)

    return jax.shard_map(
        body,
        mesh=mesh,
        in_specs=(
            P(("parts", "dp"), None),
            P(("parts", "dp"), None),
            P("dp", None),
            P("dp", None),
            P("dp", None),
            P("dp", None),
        ),
        out_specs=P("parts", "dp"),
        check_vma=False,
    )
```

```python
import functools
import math

import jax
import jax.numpy as jnp
from jax import lax
from jax.experimental import pallas as pl
from jax.experimental.pallas import tpu as pltpu
from jax.sharding import PartitionSpec as P

LEN = 1024
NT = (((1,), (1,)), ((), ()))
TN = (((0,), (0,)), ((), ()))


def dot(a, b, dims):
    return lax.dot_general(a, b, dims, preferred_element_type=jnp.float32)


def chip_at(place, chips):
    half = chips // 2
    return jnp.where(place < half, 2 * place, 2 * (chips - 1 - place) + 1)


def block_at(offset, chips):
    me = lax.axis_index("dp")
    chip = me >> 1
    z, y = chip >> 1, chip & 1
    place = jnp.where(y == 0, z, chips - 1 - z)
    return chip_at((place - offset) & (chips - 1), chips) * 2 + (me & 1)


def ring(x, step, chips):
    half = chips // 2
    chip = [2 * p if p < half else 2 * (chips - 1 - p) + 1 for p in range(chips)]
    pairs = [
        (chip[p] * 2 + c, chip[(p + step) % chips] * 2 + c) for p in range(chips) for c in range(2)
    ]
    return lax.ppermute(x, "dp", pairs)


def swap(x, bit, n):
    return lax.ppermute(x, "dp", [(i, i ^ bit) for i in range(n)])


def project_kernel(chips, offsets, halves, carry, *refs):
    tokens, refs = refs[:4], refs[4:]
    blocks = []
    for half in halves:
        blocks.append(refs[: 1 + half])
        refs = refs[1 + half :]
    if carry:
        carried, refs = refs[0], refs[1:]
    out, a_buf, g_buf, b_buf, sems = refs
    rows = tokens[0].shape[0]
    a_width, g_width = a_buf.shape[2], g_buf.shape[2]
    rank = b_buf.shape[1]
    copies = []
    for i, (offset, parts) in enumerate(zip(offsets, blocks)):
        index = block_at(offset, chips)
        mine = []
        for core in range(2):
            for which, (buf, width) in enumerate(((a_buf, a_width), (g_buf, g_width))):
                mine.append(
                    pltpu.make_async_copy(
                        tokens[2 * which + core].at[:, pl.ds(pl.multiple_of(index * width, 128), width)],
                        buf.at[i, pl.ds(core * rows, rows)],
                        sems.at[i, 2 * which + core],
                    )
                )
        for k, part in enumerate(parts):
            size = rank // len(parts)
            mine.append(
                pltpu.make_async_copy(part, b_buf.at[i, pl.ds(k * size, size)], sems.at[i, 4 + k])
            )
        for copy in mine:
            copy.start()
        copies.append(mine)
    if carry:
        a_sum, g_sum = carried[:, :rank], carried[:, rank:]
    else:
        a_sum = g_sum = jnp.zeros((2 * rows, rank), jnp.float32)
    for i, mine in enumerate(copies):
        for copy in mine:
            copy.wait()
        a_sum += dot(a_buf[i], b_buf[i, :, :a_width], NT)
        g_sum += dot(g_buf[i], b_buf[i, :, a_width:], NT)
    out[:, :rank] = a_sum
    out[:, rank:] = g_sum


def project(tokens, blocks, offsets, chips, a_width, carry=None):
    rows = tokens[0].shape[0]
    count = len(offsets)
    blocks = [b if isinstance(b, tuple) else (b,) for b in blocks]
    halves = [len(b) - 1 for b in blocks]
    flat = [x for b in blocks for x in b]
    width = flat[0].shape[1]
    rank = sum(x.shape[0] for x in blocks[0])
    vmem = pl.BlockSpec(memory_space=pltpu.VMEM)
    anywhere = pl.BlockSpec(memory_space=pl.ANY)
    carried = () if carry is None else (carry,)
    return pl.pallas_call(
        functools.partial(project_kernel, chips, offsets, halves, carry is not None),
        out_shape=jax.ShapeDtypeStruct((2 * rows, 2 * rank), jnp.float32),
        in_specs=[anywhere] * (4 + len(flat)) + [vmem] * len(carried),
        out_specs=vmem,
        scratch_shapes=[
            pltpu.VMEM((count, 2 * rows, a_width), jnp.bfloat16),
            pltpu.VMEM((count, 2 * rows, width - a_width), jnp.bfloat16),
            pltpu.VMEM((count, rank, width), jnp.bfloat16),
            pltpu.SemaphoreType.DMA((count, 6)),
        ],
        compiler_params=pltpu.CompilerParams(vmem_limit_bytes=24 * 2**20),
        cost_estimate=pl.CostEstimate(
            flops=4 * count * rows * rank * width,
            bytes_accessed=count * (2 * rows + rank) * width * 2,
            transcendentals=0,
        ),
    )(*tokens, *flat, *carried)


def ordered_kernel(count, x, out):
    me = lax.axis_index("dp")
    width = x.shape[1] // count
    for j in range(count):
        out[:, j * width : (j + 1) * width] = x[:, pl.ds(pl.multiple_of((me ^ j) * width, 128), width)]


def local(activations, out_grads, in_basis, out_basis, preconditioner, queries):
    rows = activations.shape[0]
    a_width, rank = in_basis.shape
    n = activations.shape[1] // a_width
    chips = n // 2
    split = LEN // rows
    me = lax.axis_index("dp")

    own = jnp.concatenate([in_basis.T, out_basis.T], axis=1)
    up, down = [own], [own]
    for _ in range(chips // 2 - 1):
        up.append(ring(up[-1], 1, chips))
        down.append(ring(down[-1], -1, chips))
    tokens = (activations, swap(activations, 1, n), out_grads, swap(out_grads, 1, n))
    preconditioner_2 = swap(preconditioner, 1, n)

    run = functools.partial(project, tokens, chips=chips, a_width=a_width)
    early, offsets = [own], [0]
    for i in range(1, chips // 2 - 1):
        early += [up[i], down[i]]
        offsets += [i, -i]
    last = chips // 2 - 1
    total = run(early, offsets)
    total, up_last, down_last = lax.optimization_barrier((total, up[last], down[last]))
    half = rank // 2
    far = (ring(up_last[:half], 1, chips), ring(down_last[half:], -1, chips))
    total = run([up_last, down_last], [last, -last], carry=total)
    total = run([far], [chips // 2], carry=total)
    theirs = swap(total, 1, n)
    total = (total + jnp.concatenate([theirs[rows:], theirs[:rows]], axis=0)).astype(jnp.bfloat16)

    raw = dot(total[:, rank:], total[:, :rank], TN)
    raw = raw.reshape(1, rank * rank) * (1.0 / math.sqrt(LEN))
    bit = 2
    while bit < n:
        other = swap(raw, bit, n)
        if bit < split:
            raw = raw + other
        else:
            raw = jnp.where(
                (me & bit) == 0,
                jnp.concatenate([raw, other], axis=0),
                jnp.concatenate([other, raw], axis=0),
            )
        bit *= 2
    features = raw.astype(jnp.bfloat16)

    conditioned = jnp.concatenate(
        [dot(features, m, NT) for m in (preconditioner, preconditioner_2)], axis=1
    ).astype(jnp.bfloat16)
    bit = 2
    while bit < n:
        conditioned = jnp.concatenate([conditioned, swap(conditioned, bit, n)], axis=1)
        bit *= 2
    arranged = pl.pallas_call(
        functools.partial(ordered_kernel, n),
        out_shape=jax.ShapeDtypeStruct(queries.shape, queries.dtype),
    )(queries)
    return dot(conditioned, arranged, NT) * (1.0 / rank)


def local_gathered(activations, out_grads, in_basis, out_basis, preconditioner, queries):
    rows = activations.shape[0]
    rank = in_basis.shape[1]
    act_proj = jnp.dot(
        activations,
        lax.all_gather(in_basis, "dp", axis=0, tiled=True),
        preferred_element_type=jnp.float32,
    ).astype(jnp.bfloat16)
    grad_proj = jnp.dot(
        out_grads,
        lax.all_gather(out_basis, "dp", axis=0, tiled=True),
        preferred_element_type=jnp.float32,
    ).astype(jnp.bfloat16)
    raw = dot(grad_proj, act_proj, TN).reshape(1, rank * rank) * (1.0 / math.sqrt(LEN))
    gathered = lax.all_gather(raw, "dp", axis=0, tiled=True)
    features = gathered.reshape(-1, LEN // rows, rank * rank).sum(axis=1).astype(jnp.bfloat16)
    conditioned = dot(features, preconditioner, NT).astype(jnp.bfloat16)
    scores = dot(lax.all_gather(conditioned, "dp", axis=1, tiled=True), queries, NT)
    return scores * (1.0 / rank)


def power_of_two(x):
    return x > 0 and x & (x - 1) == 0


def solution(mesh):
    n = mesh.shape["dp"]

    def body(activations, out_grads, in_basis, out_basis, preconditioner, queries):
        aligned = all(x.shape[0] % 128 == 0 for x in (in_basis, out_basis, preconditioner))
        split = LEN // activations.shape[0]
        regular = aligned and n >= 8 and power_of_two(n) and power_of_two(split) and 4 <= split <= n
        form = local if regular else local_gathered
        return form(activations, out_grads, in_basis, out_basis, preconditioner, queries)

    return jax.shard_map(
        body,
        mesh=mesh,
        in_specs=(
            P(("parts", "dp"), None),
            P(("parts", "dp"), None),
            P("dp", None),
            P("dp", None),
            P("dp", None),
            P("dp", None),
        ),
        out_specs=P("parts", "dp"),
        check_vma=False,
    )
```

```python
import functools
import math

import jax
import jax.numpy as jnp
from jax import lax
from jax.experimental import pallas as pl
from jax.experimental.pallas import tpu as pltpu
from jax.sharding import PartitionSpec as P

LEN = 1024
LIMIT = 48
NT = (((1,), (1,)), ((), ()))
TN = (((0,), (0,)), ((), ()))
VMEM = pl.BlockSpec(memory_space=pltpu.VMEM)
HBM = pl.BlockSpec(memory_space=pltpu.HBM)


def dot(a, b, dims):
    return lax.dot_general(a, b, dims, preferred_element_type=jnp.float32)


def chip_behind(offset, chips):
    chip = lax.axis_index("dp") >> 1
    z, y = chip >> 1, chip & 1
    place = (jnp.where(y == 0, z, chips - 1 - z) - offset) & (chips - 1)
    return jnp.where(place < chips // 2, 2 * place, 2 * (chips - 1 - place) + 1)


def ring(x, step, chips):
    half = chips // 2
    chip = [2 * p if p < half else 2 * (chips - 1 - p) + 1 for p in range(chips)]
    pairs = [
        (chip[p] * 2 + c, chip[(p + step) % chips] * 2 + c) for p in range(chips) for c in range(2)
    ]
    return lax.ppermute(x, "dp", pairs)


def swap(x, bit, n):
    return lax.ppermute(x, "dp", [(i, i ^ bit) for i in range(n)])


def project_kernel(chips, offsets, widths, carry, fetch, *refs):
    tokens, refs = refs[:4], refs[4:]
    blocks, refs = refs[: 2 * len(offsets)], refs[2 * len(offsets) :]
    if carry:
        carried, refs = refs[0], refs[1:]
    out, refs = refs[0], refs[1:]
    if fetch is not None:
        fetched, refs = refs[0], refs[1:]
    buf, sems = refs
    rows = tokens[0].shape[0]
    rank, cut = blocks[0].shape
    a_width, g_width = widths
    core = lax.axis_index("dp") & 1
    copies = []
    for i, offset in enumerate(offsets + ([] if fetch is None else [fetch])):
        index = chip_behind(offset, chips) * 2 + core
        to = buf.at[i] if i < len(offsets) else fetched
        for k, ref in enumerate(tokens):
            width, start = (a_width, 0) if k < 2 else (g_width, a_width)
            copies.append(
                pltpu.make_async_copy(
                    ref.at[:, pl.ds(pl.multiple_of(index * width, 128), width)],
                    to.at[pl.ds(k % 2 * rows, rows), pl.ds(start, width)],
                    sems.at[i, k],
                )
            )
    for copy in copies:
        copy.start()
    if carry:
        a_sum, g_sum = carried[:, :rank], carried[:, rank:]
    else:
        a_sum = g_sum = jnp.zeros((out.shape[0], rank), jnp.float32)
    for i in range(len(offsets)):
        for copy in copies[4 * i : 4 * i + 4]:
            copy.wait()
        a_sum += dot(buf[i, :, :a_width], blocks[2 * i][:, :a_width], NT)
        g_sum += dot(buf[i, :, a_width:cut], blocks[2 * i][:, a_width:], NT)
        g_sum += dot(buf[i, :, cut:], blocks[2 * i + 1][...], NT)
    out[:, :rank] = a_sum
    out[:, rank:] = g_sum
    for copy in copies[4 * len(offsets) :]:
        copy.wait()


def project(tokens, blocks, offsets, widths, chips, carry=None, fetch=None):
    rows = tokens[0].shape[0]
    count = len(offsets)
    rank = blocks[0][0].shape[0]
    width = sum(widths)
    flat = [x for block in blocks for x in block]
    carried = () if carry is None else (carry,)
    out_shape = [jax.ShapeDtypeStruct((2 * rows, 2 * rank), jnp.float32)]
    if fetch is not None:
        out_shape.append(jax.ShapeDtypeStruct((2 * rows, width), tokens[0].dtype))
    return pl.pallas_call(
        functools.partial(project_kernel, chips, offsets, widths, carry is not None, fetch),
        out_shape=out_shape,
        in_specs=[HBM] * 4 + [VMEM] * (len(flat) + len(carried)),
        out_specs=[VMEM] * len(out_shape),
        scratch_shapes=[
            pltpu.VMEM((count, 2 * rows, width), tokens[0].dtype),
            pltpu.SemaphoreType.DMA((count + 1, 4)),
        ],
        compiler_params=pltpu.CompilerParams(vmem_limit_bytes=LIMIT * 2**20),
        cost_estimate=pl.CostEstimate(
            flops=4 * count * rows * rank * width,
            bytes_accessed=count * (2 * rows + rank) * width * 2,
            transcendentals=0,
        ),
    )(*tokens, *flat, *carried)


def finish_kernel(a_width, tokens, first, second, carried, out):
    rank, cut = first.shape
    out[:, :rank] = carried[:, :rank] + dot(tokens[:, :a_width], first[:, :a_width], NT)
    out[:, rank:] = (
        carried[:, rank:]
        + dot(tokens[:, a_width:cut], first[:, a_width:], NT)
        + dot(tokens[:, cut:], second[...], NT)
    )


def finish(tokens, block, a_width, carry):
    return pl.pallas_call(
        functools.partial(finish_kernel, a_width),
        out_shape=jax.ShapeDtypeStruct(carry.shape, carry.dtype),
        in_specs=[VMEM] * 4,
        out_specs=VMEM,
        compiler_params=pltpu.CompilerParams(vmem_limit_bytes=16 * 2**20),
    )(tokens, *block, carry)


def to_all(x, groups):
    copies = jnp.broadcast_to(x[None], (len(groups[0]),) + x.shape)
    return lax.all_to_all(copies, "dp", 0, 0, axis_index_groups=groups, tiled=True)


def local(activations, out_grads, in_basis, out_basis, preconditioner, queries):
    rows = activations.shape[0]
    a_width, rank = in_basis.shape
    n = activations.shape[1] // a_width
    chips = n // 2
    split = LEN // rows

    width = a_width + out_basis.shape[0]
    cut = width // 256 * 128
    in_rows, out_rows = in_basis.T, out_basis.T
    own = (
        jnp.concatenate([in_rows, out_rows[:, : cut - a_width]], axis=1),
        out_rows[:, cut - a_width :],
    )
    up, down = [own], [own]
    for _ in range(chips // 2 - 1):
        up.append(tuple(ring(x, 1, chips) for x in up[-1]))
        down.append(tuple(ring(x, -1, chips) for x in down[-1]))
    tokens = (activations, swap(activations, 1, n), out_grads, swap(out_grads, 1, n))

    widths = (a_width, width - a_width)
    run = functools.partial(project, tokens, widths=widths, chips=chips)
    (total,) = run([own, up[1], down[1]], [0, 1, -1])
    total, far_up, far_down = lax.optimization_barrier((total, up[-1][0], down[-1][1]))
    far = (ring(far_up, 1, chips), ring(far_down, -1, chips))
    for i in range(2, chips // 2 - 1):
        (total,) = run([up[i], down[i]], [i, -i], carry=total)
    i = chips // 2 - 1
    total, far_tokens = run([up[i], down[i]], [i, -i], carry=total, fetch=chips // 2)
    total = finish(far_tokens, far, a_width, total)
    theirs = swap(total, 1, n)
    total = (total + jnp.concatenate([theirs[rows:], theirs[:rows]], axis=0)).astype(jnp.bfloat16)

    raw = dot(total[:, rank:], total[:, :rank], TN)
    raw = raw.reshape(1, rank * rank) * (1.0 / math.sqrt(LEN))
    planes = [[2 * i + c for i in range(chips)] for c in range(2)]
    raw = to_all(raw, planes).reshape(-1, split // 2, rank * rank)
    features = raw.sum(axis=1).astype(jnp.bfloat16)

    conditioned = dot(features, preconditioner, NT).astype(jnp.bfloat16)
    conditioned = to_all(conditioned, [list(range(n))])
    conditioned = conditioned.transpose(1, 0, 2).reshape(-1, queries.shape[1])
    return dot(conditioned, queries, NT) * (1.0 / rank)


def local_gathered(activations, out_grads, in_basis, out_basis, preconditioner, queries):
    rows = activations.shape[0]
    rank = in_basis.shape[1]
    act_proj = jnp.dot(
        activations,
        lax.all_gather(in_basis, "dp", axis=0, tiled=True),
        preferred_element_type=jnp.float32,
    ).astype(jnp.bfloat16)
    grad_proj = jnp.dot(
        out_grads,
        lax.all_gather(out_basis, "dp", axis=0, tiled=True),
        preferred_element_type=jnp.float32,
    ).astype(jnp.bfloat16)
    raw = dot(grad_proj, act_proj, TN).reshape(1, rank * rank) * (1.0 / math.sqrt(LEN))
    gathered = lax.all_gather(raw, "dp", axis=0, tiled=True)
    features = gathered.reshape(-1, LEN // rows, rank * rank).sum(axis=1).astype(jnp.bfloat16)
    conditioned = dot(features, preconditioner, NT).astype(jnp.bfloat16)
    scores = dot(lax.all_gather(conditioned, "dp", axis=1, tiled=True), queries, NT)
    return scores * (1.0 / rank)


def power_of_two(x):
    return x > 0 and x & (x - 1) == 0


def solution(mesh):
    n = mesh.shape["dp"]

    def body(activations, out_grads, in_basis, out_basis, preconditioner, queries):
        aligned = all(x.shape[0] % 128 == 0 for x in (in_basis, out_basis, preconditioner))
        split = LEN // activations.shape[0]
        regular = aligned and n >= 8 and power_of_two(n) and power_of_two(split) and 4 <= split <= n
        form = local if regular else local_gathered
        return form(activations, out_grads, in_basis, out_basis, preconditioner, queries)

    return jax.shard_map(
        body,
        mesh=mesh,
        in_specs=(
            P(("parts", "dp"), None),
            P(("parts", "dp"), None),
            P("dp", None),
            P("dp", None),
            P("dp", None),
            P("dp", None),
        ),
        out_specs=P("parts", "dp"),
        check_vma=False,
    )
```

```python
import functools
import math

import jax
import jax.numpy as jnp
from jax import lax
from jax.experimental import pallas as pl
from jax.experimental.pallas import tpu as pltpu
from jax.sharding import PartitionSpec as P

LEN = 1024
LIMIT = 48
NT = (((1,), (1,)), ((), ()))
TN = (((0,), (0,)), ((), ()))
VMEM = pl.BlockSpec(memory_space=pltpu.VMEM)
HBM = pl.BlockSpec(memory_space=pltpu.HBM)


def dot(a, b, dims):
    return lax.dot_general(a, b, dims, preferred_element_type=jnp.float32)


def chip_behind(offset, chips):
    chip = lax.axis_index("dp") >> 1
    z, y = chip >> 1, chip & 1
    place = (jnp.where(y == 0, z, chips - 1 - z) - offset) & (chips - 1)
    return jnp.where(place < chips // 2, 2 * place, 2 * (chips - 1 - place) + 1)


def ring(x, step, chips):
    half = chips // 2
    chip = [2 * p if p < half else 2 * (chips - 1 - p) + 1 for p in range(chips)]
    pairs = [
        (chip[p] * 2 + c, chip[(p + step) % chips] * 2 + c) for p in range(chips) for c in range(2)
    ]
    return lax.ppermute(x, "dp", pairs)


def swap(x, bit, n):
    return lax.ppermute(x, "dp", [(i, i ^ bit) for i in range(n)])


def project_kernel(chips, offsets, widths, carry, fetch, *refs):
    tokens, refs = refs[:4], refs[4:]
    blocks, refs = refs[: 2 * len(offsets)], refs[2 * len(offsets) :]
    if carry:
        carried, refs = refs[0], refs[1:]
    out, refs = refs[0], refs[1:]
    if fetch is not None:
        fetched, refs = refs[0], refs[1:]
    buf, sems = refs
    rows = tokens[0].shape[0]
    rank, cut = blocks[0].shape
    a_width, g_width = widths
    core = lax.axis_index("dp") & 1
    copies = []
    for i, offset in enumerate(offsets + ([] if fetch is None else [fetch])):
        index = chip_behind(offset, chips) * 2 + core
        to = buf.at[i] if i < len(offsets) else fetched
        for k, ref in enumerate(tokens):
            width, start = (a_width, 0) if k < 2 else (g_width, a_width)
            copies.append(
                pltpu.make_async_copy(
                    ref.at[:, pl.ds(pl.multiple_of(index * width, 128), width)],
                    to.at[pl.ds(k % 2 * rows, rows), pl.ds(start, width)],
                    sems.at[i, k],
                )
            )
    for copy in copies:
        copy.start()
    if carry:
        a_sum, g_sum = carried[:, :rank], carried[:, rank:]
    else:
        a_sum = g_sum = jnp.zeros((out.shape[0], rank), jnp.float32)
    for i in range(len(offsets)):
        for copy in copies[4 * i : 4 * i + 4]:
            copy.wait()
        a_sum += dot(buf[i, :, :a_width], blocks[2 * i][:, :a_width], NT)
        g_sum += dot(buf[i, :, a_width:cut], blocks[2 * i][:, a_width:], NT)
        g_sum += dot(buf[i, :, cut:], blocks[2 * i + 1][...], NT)
    out[:, :rank] = a_sum
    out[:, rank:] = g_sum
    for copy in copies[4 * len(offsets) :]:
        copy.wait()


def project(tokens, blocks, offsets, widths, chips, carry=None, fetch=None):
    rows = tokens[0].shape[0]
    count = len(offsets)
    rank = blocks[0][0].shape[0]
    width = sum(widths)
    flat = [x for block in blocks for x in block]
    carried = () if carry is None else (carry,)
    out_shape = [jax.ShapeDtypeStruct((2 * rows, 2 * rank), jnp.float32)]
    if fetch is not None:
        out_shape.append(jax.ShapeDtypeStruct((2 * rows, width), tokens[0].dtype))
    return pl.pallas_call(
        functools.partial(project_kernel, chips, offsets, widths, carry is not None, fetch),
        out_shape=out_shape,
        in_specs=[HBM] * 4 + [VMEM] * (len(flat) + len(carried)),
        out_specs=[VMEM] * len(out_shape),
        scratch_shapes=[
            pltpu.VMEM((count, 2 * rows, width), tokens[0].dtype),
            pltpu.SemaphoreType.DMA((count + 1, 4)),
        ],
        compiler_params=pltpu.CompilerParams(vmem_limit_bytes=LIMIT * 2**20),
        cost_estimate=pl.CostEstimate(
            flops=4 * count * rows * rank * width,
            bytes_accessed=count * (2 * rows + rank) * width * 2,
            transcendentals=0,
        ),
    )(*tokens, *flat, *carried)


def finish_kernel(a_width, tokens, first, second, carried, out):
    rank, cut = first.shape
    out[:, :rank] = carried[:, :rank] + dot(tokens[:, :a_width], first[:, :a_width], NT)
    out[:, rank:] = (
        carried[:, rank:]
        + dot(tokens[:, a_width:cut], first[:, a_width:], NT)
        + dot(tokens[:, cut:], second[...], NT)
    )


def finish(tokens, block, a_width, carry):
    return pl.pallas_call(
        functools.partial(finish_kernel, a_width),
        out_shape=jax.ShapeDtypeStruct(carry.shape, carry.dtype),
        in_specs=[VMEM] * 4,
        out_specs=VMEM,
        compiler_params=pltpu.CompilerParams(vmem_limit_bytes=16 * 2**20),
    )(tokens, *block, carry)


def to_all(x, groups):
    copies = jnp.broadcast_to(x[None], (len(groups[0]),) + x.shape)
    return lax.all_to_all(copies, "dp", 0, 0, axis_index_groups=groups, tiled=True)


def local(activations, out_grads, in_basis, out_basis, preconditioner, queries):
    rows = activations.shape[0]
    a_width, rank = in_basis.shape
    n = activations.shape[1] // a_width
    chips = n // 2
    split = LEN // rows

    width = a_width + out_basis.shape[0]
    cut = width // 256 * 128
    in_rows, out_rows = in_basis.T, out_basis.T
    own = (
        jnp.concatenate([in_rows, out_rows[:, : cut - a_width]], axis=1),
        out_rows[:, cut - a_width :],
    )
    activations_2 = swap(activations, 1, n)
    out_grads_2 = swap(out_grads, 1, n)
    up, down = [own], [own]
    for i in range(chips // 2 - 1):
        if i == 1:
            first, activations_2 = lax.optimization_barrier((up[-1][0], activations_2))
            up[-1] = (first, up[-1][1])
        up.append(tuple(ring(x, 1, chips) for x in up[-1]))
        down.append(tuple(ring(x, -1, chips) for x in down[-1]))
    tokens = (activations, activations_2, out_grads, out_grads_2)

    widths = (a_width, width - a_width)
    run = functools.partial(project, tokens, widths=widths, chips=chips)
    (total,) = run([own, up[1], down[1]], [0, 1, -1])
    total, far_up, far_down = lax.optimization_barrier((total, up[-1][0], down[-1][1]))
    far = (ring(far_up, 1, chips), ring(far_down, -1, chips))
    for i in range(2, chips // 2 - 1):
        (total,) = run([up[i], down[i]], [i, -i], carry=total)
    i = chips // 2 - 1
    total, far_tokens = run([up[i], down[i]], [i, -i], carry=total, fetch=chips // 2)
    total = finish(far_tokens, far, a_width, total)
    theirs = swap(total, 1, n)
    total = (total + jnp.concatenate([theirs[rows:], theirs[:rows]], axis=0)).astype(jnp.bfloat16)

    raw = dot(total[:, rank:], total[:, :rank], TN)
    raw = (raw * (1.0 / math.sqrt(LEN))).astype(jnp.bfloat16).reshape(-1, 128)
    planes = [[2 * i + c for i in range(chips)] for c in range(2)]
    raw = to_all(raw, planes).astype(jnp.float32)
    features = raw.reshape((-1, split // 2) + raw.shape[1:]).sum(axis=1)
    features = features.astype(jnp.bfloat16).reshape(-1, rank * rank)

    conditioned = dot(features, preconditioner, NT).astype(jnp.bfloat16)
    conditioned = to_all(conditioned, [list(range(n))])
    conditioned = conditioned.transpose(1, 0, 2).reshape(-1, queries.shape[1])
    return dot(conditioned, queries, NT) * (1.0 / rank)


def local_gathered(activations, out_grads, in_basis, out_basis, preconditioner, queries):
    rows = activations.shape[0]
    rank = in_basis.shape[1]
    act_proj = jnp.dot(
        activations,
        lax.all_gather(in_basis, "dp", axis=0, tiled=True),
        preferred_element_type=jnp.float32,
    ).astype(jnp.bfloat16)
    grad_proj = jnp.dot(
        out_grads,
        lax.all_gather(out_basis, "dp", axis=0, tiled=True),
        preferred_element_type=jnp.float32,
    ).astype(jnp.bfloat16)
    raw = dot(grad_proj, act_proj, TN).reshape(1, rank * rank) * (1.0 / math.sqrt(LEN))
    gathered = lax.all_gather(raw, "dp", axis=0, tiled=True)
    features = gathered.reshape(-1, LEN // rows, rank * rank).sum(axis=1).astype(jnp.bfloat16)
    conditioned = dot(features, preconditioner, NT).astype(jnp.bfloat16)
    scores = dot(lax.all_gather(conditioned, "dp", axis=1, tiled=True), queries, NT)
    return scores * (1.0 / rank)


def power_of_two(x):
    return x > 0 and x & (x - 1) == 0


def solution(mesh):
    n = mesh.shape["dp"]

    def body(activations, out_grads, in_basis, out_basis, preconditioner, queries):
        aligned = all(x.shape[0] % 128 == 0 for x in (in_basis, out_basis, preconditioner))
        split = LEN // activations.shape[0]
        regular = aligned and n >= 8 and power_of_two(n) and power_of_two(split) and 4 <= split <= n
        form = local if regular else local_gathered
        return form(activations, out_grads, in_basis, out_basis, preconditioner, queries)

    return jax.shard_map(
        body,
        mesh=mesh,
        in_specs=(
            P(("parts", "dp"), None),
            P(("parts", "dp"), None),
            P("dp", None),
            P("dp", None),
            P("dp", None),
            P("dp", None),
        ),
        out_specs=P("parts", "dp"),
        check_vma=False,
    )
```

```python
import functools
import math

import jax
import jax.numpy as jnp
from jax import lax
from jax.experimental import pallas as pl
from jax.experimental.pallas import tpu as pltpu
from jax.sharding import PartitionSpec as P

LEN = 1024
LIMIT = 46
NT = (((1,), (1,)), ((), ()))
TN = (((0,), (0,)), ((), ()))
VMEM = pl.BlockSpec(memory_space=pltpu.VMEM)
HBM = pl.BlockSpec(memory_space=pltpu.HBM)


def dot(a, b, dims):
    return lax.dot_general(a, b, dims, preferred_element_type=jnp.float32)


def chip_behind(offset, chips):
    chip = lax.axis_index("dp") >> 1
    z, y = chip >> 1, chip & 1
    place = (jnp.where(y == 0, z, chips - 1 - z) - offset) & (chips - 1)
    return jnp.where(place < chips // 2, 2 * place, 2 * (chips - 1 - place) + 1)


def ring(x, step, chips):
    half = chips // 2
    chip = [2 * p if p < half else 2 * (chips - 1 - p) + 1 for p in range(chips)]
    pairs = [
        (chip[p] * 2 + c, chip[(p + step) % chips] * 2 + c) for p in range(chips) for c in range(2)
    ]
    return lax.ppermute(x, "dp", pairs)


def swap(x, bit, n):
    return lax.ppermute(x, "dp", [(i, i ^ bit) for i in range(n)])


def gather_kernel(chips, a_width, act, grad, out, sems):
    core = lax.axis_index("dp") & 1
    copies = []
    for chip in range(chips):
        block = 2 * chip + core
        for k, (ref, start, stop) in enumerate(((act, 0, a_width), (grad, a_width, out.shape[2]))):
            width = stop - start
            copies.append(
                pltpu.make_async_copy(
                    ref.at[:, pl.ds(pl.multiple_of(block * width, 128), width)],
                    out.at[chip, :, pl.ds(start, width)],
                    sems.at[chip, k],
                )
            )
    for copy in copies:
        copy.start()
    for copy in copies:
        copy.wait()


def gather_columns(act, grad, a_width, width, chips):
    rows = act.shape[0]
    return pl.pallas_call(
        functools.partial(gather_kernel, chips, a_width),
        out_shape=jax.ShapeDtypeStruct((chips, rows, width), act.dtype),
        in_specs=[HBM, HBM],
        out_specs=VMEM,
        scratch_shapes=[pltpu.SemaphoreType.DMA((chips, 2))],
        compiler_params=pltpu.CompilerParams(vmem_limit_bytes=LIMIT * 2**20),
        cost_estimate=pl.CostEstimate(
            flops=0, bytes_accessed=4 * chips * rows * width, transcendentals=0
        ),
    )(act, grad)


def project_kernel(chips, offsets, a_width, carry, *refs):
    mine, act, grad = refs[:3]
    blocks, refs = refs[3 : 3 + 2 * len(offsets)], refs[3 + 2 * len(offsets) :]
    out = refs[-1]
    rank, cut = blocks[0].shape
    width = mine.shape[2]
    g_width = width - a_width
    core = lax.axis_index("dp") & 1
    if carry:
        a_sum, g_sum = refs[0][:, :rank], refs[0][:, rank:]
    else:
        a_sum = g_sum = jnp.zeros((out.shape[0], rank), jnp.float32)
    for i, offset in enumerate(offsets):
        chip = chip_behind(offset, chips)
        block = chip * 2 + core
        a_at = pl.multiple_of(block * a_width, 128)
        g_at = pl.multiple_of(block * g_width, 128)

        def both(start, stop):
            if stop <= a_width:
                theirs = act[:, pl.ds(a_at + start, stop - start)]
            else:
                theirs = grad[:, pl.ds(g_at + start - a_width, stop - start)]
            return jnp.concatenate([mine[chip, :, start:stop], theirs], axis=0)

        a_sum += dot(both(0, a_width), blocks[2 * i][:, :a_width], NT)
        g_sum += dot(both(a_width, cut), blocks[2 * i][:, a_width:], NT)
        g_sum += dot(both(cut, width), blocks[2 * i + 1][...], NT)
    out[:, :rank] = a_sum
    out[:, rank:] = g_sum


def project(tokens, blocks, offsets, a_width, carry=None):
    chips, rows, width = tokens[0].shape
    count = len(offsets)
    rank = blocks[0][0].shape[0]
    flat = [x for block in blocks for x in block]
    carried = () if carry is None else (carry,)
    return pl.pallas_call(
        functools.partial(project_kernel, chips, offsets, a_width, carry is not None),
        out_shape=jax.ShapeDtypeStruct((2 * rows, 2 * rank), jnp.float32),
        in_specs=[VMEM] * (3 + len(flat) + len(carried)),
        out_specs=VMEM,
        compiler_params=pltpu.CompilerParams(vmem_limit_bytes=24 * 2**20),
        cost_estimate=pl.CostEstimate(
            flops=4 * count * rows * rank * width,
            bytes_accessed=count * (2 * rows + rank) * width * 2,
            transcendentals=0,
        ),
    )(*tokens, *flat, *carried)


def to_all(x, groups):
    copies = jnp.broadcast_to(x[None], (len(groups[0]),) + x.shape)
    return lax.all_to_all(copies, "dp", 0, 0, axis_index_groups=groups, tiled=True)


def local(activations, out_grads, in_basis, out_basis, preconditioner, queries):
    rows = activations.shape[0]
    a_width, rank = in_basis.shape
    n = activations.shape[1] // a_width
    chips = n // 2
    split = LEN // rows

    width = a_width + out_basis.shape[0]
    cut = width // 256 * 128
    in_rows, out_rows = in_basis.T, out_basis.T
    own = (
        jnp.concatenate([in_rows, out_rows[:, : cut - a_width]], axis=1),
        out_rows[:, cut - a_width :],
    )
    activations_2 = swap(activations, 1, n)
    out_grads_2 = swap(out_grads, 1, n)
    up, down = [own], [own]
    for i in range(chips // 2 - 1):
        if i == 1:
            mine = gather_columns(activations, out_grads, a_width, width, chips)
            first, activations_2, mine = lax.optimization_barrier((up[-1][0], activations_2, mine))
            up[-1] = (first, up[-1][1])
        up.append(tuple(ring(x, 1, chips) for x in up[-1]))
        down.append(tuple(ring(x, -1, chips) for x in down[-1]))
    run = functools.partial(project, (mine, activations_2, out_grads_2), a_width=a_width)
    near, offsets = [own], [0]
    for i in range(1, chips // 2 - 1):
        near += [up[i], down[i]]
        offsets += [i, -i]
    total = run(near, offsets)
    total, far_up, far_down = lax.optimization_barrier((total, up[-1][0], down[-1][1]))
    far = (ring(far_up, 1, chips), ring(far_down, -1, chips))
    last = chips // 2 - 1
    total = run([up[last], down[last]], [last, -last], carry=total)
    total = run([far], [chips // 2], carry=total)
    theirs = swap(total, 1, n)
    total = (total + jnp.concatenate([theirs[rows:], theirs[:rows]], axis=0)).astype(jnp.bfloat16)

    raw = dot(total[:, rank:], total[:, :rank], TN)
    raw = raw.reshape(1, rank * rank) * (1.0 / math.sqrt(LEN))
    planes = [[2 * i + c for i in range(chips)] for c in range(2)]
    raw = to_all(raw, planes).reshape(-1, split // 2, rank * rank)
    features = raw.sum(axis=1).astype(jnp.bfloat16)

    conditioned = dot(features, preconditioner, NT).astype(jnp.bfloat16)
    conditioned = to_all(conditioned, [list(range(n))])
    conditioned = conditioned.transpose(1, 0, 2).reshape(-1, queries.shape[1])
    return dot(conditioned, queries, NT) * (1.0 / rank)


def local_gathered(activations, out_grads, in_basis, out_basis, preconditioner, queries):
    rows = activations.shape[0]
    rank = in_basis.shape[1]
    act_proj = jnp.dot(
        activations,
        lax.all_gather(in_basis, "dp", axis=0, tiled=True),
        preferred_element_type=jnp.float32,
    ).astype(jnp.bfloat16)
    grad_proj = jnp.dot(
        out_grads,
        lax.all_gather(out_basis, "dp", axis=0, tiled=True),
        preferred_element_type=jnp.float32,
    ).astype(jnp.bfloat16)
    raw = dot(grad_proj, act_proj, TN).reshape(1, rank * rank) * (1.0 / math.sqrt(LEN))
    gathered = lax.all_gather(raw, "dp", axis=0, tiled=True)
    features = gathered.reshape(-1, LEN // rows, rank * rank).sum(axis=1).astype(jnp.bfloat16)
    conditioned = dot(features, preconditioner, NT).astype(jnp.bfloat16)
    scores = dot(lax.all_gather(conditioned, "dp", axis=1, tiled=True), queries, NT)
    return scores * (1.0 / rank)


def power_of_two(x):
    return x > 0 and x & (x - 1) == 0


def solution(mesh):
    n = mesh.shape["dp"]

    def body(activations, out_grads, in_basis, out_basis, preconditioner, queries):
        aligned = all(x.shape[0] % 128 == 0 for x in (in_basis, out_basis, preconditioner))
        split = LEN // activations.shape[0]
        regular = aligned and n >= 8 and power_of_two(n) and power_of_two(split) and 4 <= split <= n
        form = local if regular else local_gathered
        return form(activations, out_grads, in_basis, out_basis, preconditioner, queries)

    return jax.shard_map(
        body,
        mesh=mesh,
        in_specs=(
            P(("parts", "dp"), None),
            P(("parts", "dp"), None),
            P("dp", None),
            P("dp", None),
            P("dp", None),
            P("dp", None),
        ),
        out_specs=P("parts", "dp"),
        check_vma=False,
    )
```

```python
import functools
import math

import jax
import jax.numpy as jnp
from jax import lax
from jax.experimental import pallas as pl
from jax.experimental.pallas import tpu as pltpu
from jax.sharding import PartitionSpec as P

LEN = 1024
LIMIT = 42
NT = (((1,), (1,)), ((), ()))
TN = (((0,), (0,)), ((), ()))
VMEM = pl.BlockSpec(memory_space=pltpu.VMEM)
HBM = pl.BlockSpec(memory_space=pltpu.HBM)


def dot(a, b, dims):
    return lax.dot_general(a, b, dims, preferred_element_type=jnp.float32)


def chip_behind(offset, chips):
    chip = lax.axis_index("dp") >> 1
    z, y = chip >> 1, chip & 1
    place = (jnp.where(y == 0, z, chips - 1 - z) - offset) & (chips - 1)
    return jnp.where(place < chips // 2, 2 * place, 2 * (chips - 1 - place) + 1)


def ring(x, step, chips):
    half = chips // 2
    chip = [2 * p if p < half else 2 * (chips - 1 - p) + 1 for p in range(chips)]
    pairs = [
        (chip[p] * 2 + c, chip[(p + step) % chips] * 2 + c) for p in range(chips) for c in range(2)
    ]
    return lax.ppermute(x, "dp", pairs)


def swap(x, bit, n):
    return lax.ppermute(x, "dp", [(i, i ^ bit) for i in range(n)])


def gather_kernel(chips, a_width, act, grad, out, sems):
    core = lax.axis_index("dp") & 1
    copies = []
    for chip in range(chips):
        block = 2 * chip + core
        for k, (ref, start, stop) in enumerate(((act, 0, a_width), (grad, a_width, out.shape[2]))):
            width = stop - start
            copies.append(
                pltpu.make_async_copy(
                    ref.at[:, pl.ds(pl.multiple_of(block * width, 128), width)],
                    out.at[chip, :, pl.ds(start, width)],
                    sems.at[chip, k],
                )
            )
    for copy in copies:
        copy.start()
    for copy in copies:
        copy.wait()


def gather_columns(act, grad, a_width, width, chips):
    rows = act.shape[0]
    return pl.pallas_call(
        functools.partial(gather_kernel, chips, a_width),
        out_shape=jax.ShapeDtypeStruct((chips, rows, width), act.dtype),
        in_specs=[HBM, HBM],
        out_specs=VMEM,
        scratch_shapes=[pltpu.SemaphoreType.DMA((chips, 2))],
        compiler_params=pltpu.CompilerParams(vmem_limit_bytes=LIMIT * 2**20),
        cost_estimate=pl.CostEstimate(
            flops=0, bytes_accessed=4 * chips * rows * width, transcendentals=0
        ),
    )(act, grad)


def project_kernel(chips, offsets, a_width, carry, *refs):
    mine, act, grad = refs[:3]
    blocks, refs = refs[3 : 3 + 2 * len(offsets)], refs[3 + 2 * len(offsets) :]
    out = refs[-1]
    rank, cut = blocks[0].shape
    width = mine.shape[2]
    g_width = width - a_width
    core = lax.axis_index("dp") & 1
    if carry:
        a_sum, g_sum = refs[0][:, :rank], refs[0][:, rank:]
    else:
        a_sum = g_sum = jnp.zeros((out.shape[0], rank), jnp.float32)
    for i, offset in enumerate(offsets):
        chip = chip_behind(offset, chips)
        block = chip * 2 + core
        a_at = pl.multiple_of(block * a_width, 128)
        g_at = pl.multiple_of(block * g_width, 128)

        def both(start, stop):
            if stop <= a_width:
                theirs = act[:, pl.ds(a_at + start, stop - start)]
            else:
                theirs = grad[:, pl.ds(g_at + start - a_width, stop - start)]
            return jnp.concatenate([mine[chip, :, start:stop], theirs], axis=0)

        a_sum += dot(both(0, a_width), blocks[2 * i][:, :a_width], NT)
        g_sum += dot(both(a_width, cut), blocks[2 * i][:, a_width:], NT)
        g_sum += dot(both(cut, width), blocks[2 * i + 1][...], NT)
    out[:, :rank] = a_sum
    out[:, rank:] = g_sum


def project(tokens, blocks, offsets, a_width, carry=None):
    chips, rows, width = tokens[0].shape
    count = len(offsets)
    rank = blocks[0][0].shape[0]
    flat = [x for block in blocks for x in block]
    carried = () if carry is None else (carry,)
    return pl.pallas_call(
        functools.partial(project_kernel, chips, offsets, a_width, carry is not None),
        out_shape=jax.ShapeDtypeStruct((2 * rows, 2 * rank), jnp.float32),
        in_specs=[VMEM] * (3 + len(flat) + len(carried)),
        out_specs=VMEM,
        compiler_params=pltpu.CompilerParams(vmem_limit_bytes=24 * 2**20),
        cost_estimate=pl.CostEstimate(
            flops=4 * count * rows * rank * width,
            bytes_accessed=count * (2 * rows + rank) * width * 2,
            transcendentals=0,
        ),
    )(*tokens, *flat, *carried)


def to_all(x, groups):
    copies = jnp.broadcast_to(x[None], (len(groups[0]),) + x.shape)
    return lax.all_to_all(copies, "dp", 0, 0, axis_index_groups=groups, tiled=True)


def local(activations, out_grads, in_basis, out_basis, preconditioner, queries):
    rows = activations.shape[0]
    a_width, rank = in_basis.shape
    n = activations.shape[1] // a_width
    chips = n // 2
    split = LEN // rows

    width = a_width + out_basis.shape[0]
    cut = width // 256 * 128
    in_rows, out_rows = in_basis.T, out_basis.T
    own = (
        jnp.concatenate([in_rows, out_rows[:, : cut - a_width]], axis=1),
        out_rows[:, cut - a_width :],
    )
    activations_2 = swap(activations, 1, n)
    out_grads_2 = swap(out_grads, 1, n)
    up, down = [own], [own]
    for i in range(chips // 2 - 1):
        if i == 1:
            mine = gather_columns(activations, out_grads, a_width, width, chips)
            first, activations_2, mine = lax.optimization_barrier((up[-1][0], activations_2, mine))
            up[-1] = (first, up[-1][1])
        up.append(tuple(ring(x, 1, chips) for x in up[-1]))
        down.append(tuple(ring(x, -1, chips) for x in down[-1]))
    run = functools.partial(project, (mine, activations_2, out_grads_2), a_width=a_width)
    near, offsets = [own], [0]
    for i in range(1, chips // 2 - 1):
        near += [up[i], down[i]]
        offsets += [i, -i]
    total = run(near, offsets)
    total, far_up, far_down = lax.optimization_barrier((total, up[-1][0], down[-1][1]))
    far = (ring(far_up, 1, chips), ring(far_down, -1, chips))
    last = chips // 2 - 1
    total = run([up[last], down[last]], [last, -last], carry=total)
    total = run([far], [chips // 2], carry=total)
    theirs = swap(total, 1, n)
    total = (total + jnp.concatenate([theirs[rows:], theirs[:rows]], axis=0)).astype(jnp.bfloat16)

    raw = dot(total[:, rank:], total[:, :rank], TN)
    raw = raw.reshape(1, rank * rank) * (1.0 / math.sqrt(LEN))
    planes = [[2 * i + c for i in range(chips)] for c in range(2)]
    raw = to_all(raw, planes).reshape(-1, split // 2, rank * rank)
    features = raw.sum(axis=1).astype(jnp.bfloat16)

    conditioned = dot(features, preconditioner, NT).astype(jnp.bfloat16)
    conditioned = to_all(conditioned, [list(range(n))])
    conditioned = conditioned.transpose(1, 0, 2).reshape(-1, queries.shape[1])
    return dot(conditioned, queries, NT) * (1.0 / rank)


def local_gathered(activations, out_grads, in_basis, out_basis, preconditioner, queries):
    rows = activations.shape[0]
    rank = in_basis.shape[1]
    act_proj = jnp.dot(
        activations,
        lax.all_gather(in_basis, "dp", axis=0, tiled=True),
        preferred_element_type=jnp.float32,
    ).astype(jnp.bfloat16)
    grad_proj = jnp.dot(
        out_grads,
        lax.all_gather(out_basis, "dp", axis=0, tiled=True),
        preferred_element_type=jnp.float32,
    ).astype(jnp.bfloat16)
    raw = dot(grad_proj, act_proj, TN).reshape(1, rank * rank) * (1.0 / math.sqrt(LEN))
    gathered = lax.all_gather(raw, "dp", axis=0, tiled=True)
    features = gathered.reshape(-1, LEN // rows, rank * rank).sum(axis=1).astype(jnp.bfloat16)
    conditioned = dot(features, preconditioner, NT).astype(jnp.bfloat16)
    scores = dot(lax.all_gather(conditioned, "dp", axis=1, tiled=True), queries, NT)
    return scores * (1.0 / rank)


def power_of_two(x):
    return x > 0 and x & (x - 1) == 0


def solution(mesh):
    n = mesh.shape["dp"]

    def body(activations, out_grads, in_basis, out_basis, preconditioner, queries):
        aligned = all(x.shape[0] % 128 == 0 for x in (in_basis, out_basis, preconditioner))
        split = LEN // activations.shape[0]
        regular = aligned and n >= 8 and power_of_two(n) and power_of_two(split) and 4 <= split <= n
        form = local if regular else local_gathered
        return form(activations, out_grads, in_basis, out_basis, preconditioner, queries)

    return jax.shard_map(
        body,
        mesh=mesh,
        in_specs=(
            P(("parts", "dp"), None),
            P(("parts", "dp"), None),
            P("dp", None),
            P("dp", None),
            P("dp", None),
            P("dp", None),
        ),
        out_specs=P("parts", "dp"),
        check_vma=False,
    )
```

```python
import functools
import math

import jax
import jax.numpy as jnp
from jax import lax
from jax.experimental import pallas as pl
from jax.experimental.pallas import tpu as pltpu
from jax.sharding import PartitionSpec as P

LEN = 1024
LIMIT = 48
NT = (((1,), (1,)), ((), ()))
TN = (((0,), (0,)), ((), ()))
VMEM = pl.BlockSpec(memory_space=pltpu.VMEM)
HBM = pl.BlockSpec(memory_space=pltpu.HBM)


def dot(a, b, dims):
    return lax.dot_general(a, b, dims, preferred_element_type=jnp.float32)


def chip_behind(offset, chips):
    chip = lax.axis_index("dp") >> 1
    z, y = chip >> 1, chip & 1
    place = (jnp.where(y == 0, z, chips - 1 - z) - offset) & (chips - 1)
    return jnp.where(place < chips // 2, 2 * place, 2 * (chips - 1 - place) + 1)


def ring(x, step, chips):
    half = chips // 2
    chip = [2 * p if p < half else 2 * (chips - 1 - p) + 1 for p in range(chips)]
    pairs = [
        (chip[p] * 2 + c, chip[(p + step) % chips] * 2 + c) for p in range(chips) for c in range(2)
    ]
    return lax.ppermute(x, "dp", pairs)


def swap(x, bit, n):
    return lax.ppermute(x, "dp", [(i, i ^ bit) for i in range(n)])


def add_products(a_sum, g_sum, tokens, block):
    a_block, *g_block = block
    a_width = a_block.shape[1]
    g_block = jnp.concatenate([ref[...] for ref in g_block], axis=0)
    a_sum += dot(tokens[:, :a_width], a_block[...], NT)
    g_sum += dot(tokens[:, a_width:], g_block, NT)
    return a_sum, g_sum


def project_kernel(chips, offsets, carry, fetch, *refs):
    tokens, refs = refs[:4], refs[4:]
    blocks, refs = refs[: 2 * len(offsets)], refs[2 * len(offsets) :]
    carried, refs = (refs[0], refs[1:]) if carry else (None, refs)
    out, *fetched, buf, sems = refs
    rows = tokens[0].shape[0]
    rank, a_width = blocks[0].shape
    g_width = blocks[1].shape[1]
    core = lax.axis_index("dp") & 1
    copies = []
    for i, offset in enumerate(offsets + ([] if fetch is None else [fetch])):
        index = chip_behind(offset, chips) * 2 + core
        to = buf.at[i] if i < len(offsets) else fetched[0]
        for k, ref in enumerate(tokens):
            width, first = (a_width, 0) if k < 2 else (g_width, a_width)
            copies.append(
                pltpu.make_async_copy(
                    ref.at[:, pl.ds(pl.multiple_of(index * width, 128), width)],
                    to.at[pl.ds(k % 2 * rows, rows), pl.ds(first, width)],
                    sems.at[i, k],
                )
            )
    for copy in copies:
        copy.start()
    if carry:
        sums = carried[:, :rank], carried[:, rank:]
    else:
        sums = (jnp.zeros((out.shape[0], rank), jnp.float32),) * 2
    for i in range(len(offsets)):
        for copy in copies[4 * i : 4 * i + 4]:
            copy.wait()
        sums = add_products(*sums, buf.at[i], blocks[2 * i : 2 * i + 2])
    out[:, :rank], out[:, rank:] = sums
    for copy in copies[4 * len(offsets) :]:
        copy.wait()


def project(tokens, blocks, offsets, chips, carry=None, fetch=None):
    rows = tokens[0].shape[0]
    count = len(offsets)
    rank = blocks[0][0].shape[0]
    width = sum(x.shape[1] for x in blocks[0])
    flat = [x for block in blocks for x in block]
    carried = () if carry is None else (carry,)
    out_shape = [jax.ShapeDtypeStruct((2 * rows, 2 * rank), jnp.float32)]
    if fetch is not None:
        out_shape.append(jax.ShapeDtypeStruct((2 * rows, width), tokens[0].dtype))
    return pl.pallas_call(
        functools.partial(project_kernel, chips, offsets, carry is not None, fetch),
        out_shape=out_shape,
        in_specs=[HBM] * 4 + [VMEM] * (len(flat) + len(carried)),
        out_specs=[VMEM] * len(out_shape),
        scratch_shapes=[
            pltpu.VMEM((count, 2 * rows, width), tokens[0].dtype),
            pltpu.SemaphoreType.DMA((count + 1, 4)),
        ],
        compiler_params=pltpu.CompilerParams(vmem_limit_bytes=LIMIT * 2**20),
        cost_estimate=pl.CostEstimate(
            flops=4 * count * rows * rank * width,
            bytes_accessed=count * (2 * rows + rank) * width * 2,
            transcendentals=0,
        ),
    )(*tokens, *flat, *carried)


def finish_kernel(tokens, *refs):
    *block, carried, out = refs
    rank = block[0].shape[0]
    out[:, :rank], out[:, rank:] = add_products(
        carried[:, :rank], carried[:, rank:], tokens, block
    )


def finish(tokens, block, carry):
    return pl.pallas_call(
        finish_kernel,
        out_shape=jax.ShapeDtypeStruct(carry.shape, carry.dtype),
        in_specs=[VMEM] * (2 + len(block)),
        out_specs=VMEM,
        compiler_params=pltpu.CompilerParams(vmem_limit_bytes=16 * 2**20),
    )(tokens, *block, carry)


def to_all(x, groups):
    copies = jnp.broadcast_to(x[None], (len(groups[0]),) + x.shape)
    return lax.all_to_all(copies, "dp", 0, 0, axis_index_groups=groups, tiled=True)


def local(activations, out_grads, in_basis, out_basis, preconditioner, queries):
    rows = activations.shape[0]
    a_width, rank = in_basis.shape
    n = activations.shape[1] // a_width
    chips = n // 2
    split = LEN // rows

    own = (in_basis.T, out_basis.T)

    def step(block, way):
        return tuple(ring(x, way, chips) for x in block)

    activations_2 = swap(activations, 1, n)
    first, activations_2, send = lax.optimization_barrier(
        ((step(own, 1), step(own, -1)), activations_2, out_grads)
    )
    tokens = (activations, activations_2, out_grads, swap(send, 1, n))
    up, down = [own, first[0]], [own, first[1]]
    for _ in range(chips // 2 - 2):
        up.append(step(up[-1], 1))
        down.append(step(down[-1], -1))

    near, offsets = [own], [0]
    for i in range(1, chips // 2 - 1):
        near += [up[i], down[i]]
        offsets += [i, -i]
    (total,) = project(tokens, near, offsets, chips)
    last = chips // 2 - 1
    total, far_up, far_down = lax.optimization_barrier((total, up[last], down[last][1]))
    far = (
        ring(far_up[0], 1, chips),
        ring(far_up[1][: rank // 2], 1, chips),
        ring(far_down[rank // 2 :], -1, chips),
    )
    total, far_tokens = project(
        tokens, [up[last], down[last]], [last, -last], chips, carry=total, fetch=chips // 2
    )
    total = finish(far_tokens, far, total)
    theirs = swap(total, 1, n)
    total = (total + jnp.concatenate([theirs[rows:], theirs[:rows]], axis=0)).astype(jnp.bfloat16)

    raw = dot(total[:, rank:], total[:, :rank], TN)
    raw = raw.reshape(1, rank * rank) * (1.0 / math.sqrt(LEN))
    planes = [[2 * i + c for i in range(chips)] for c in range(2)]
    raw = to_all(raw, planes).reshape(-1, split // 2, rank * rank)
    features = raw.sum(axis=1).astype(jnp.bfloat16)

    conditioned = dot(features, preconditioner, NT).astype(jnp.bfloat16)
    conditioned = to_all(conditioned, [list(range(n))])
    conditioned = conditioned.transpose(1, 0, 2).reshape(-1, queries.shape[1])
    return dot(conditioned, queries, NT) * (1.0 / rank)


def local_gathered(activations, out_grads, in_basis, out_basis, preconditioner, queries):
    rows = activations.shape[0]
    rank = in_basis.shape[1]
    act_proj = jnp.dot(
        activations,
        lax.all_gather(in_basis, "dp", axis=0, tiled=True),
        preferred_element_type=jnp.float32,
    ).astype(jnp.bfloat16)
    grad_proj = jnp.dot(
        out_grads,
        lax.all_gather(out_basis, "dp", axis=0, tiled=True),
        preferred_element_type=jnp.float32,
    ).astype(jnp.bfloat16)
    raw = dot(grad_proj, act_proj, TN).reshape(1, rank * rank) * (1.0 / math.sqrt(LEN))
    gathered = lax.all_gather(raw, "dp", axis=0, tiled=True)
    features = gathered.reshape(-1, LEN // rows, rank * rank).sum(axis=1).astype(jnp.bfloat16)
    conditioned = dot(features, preconditioner, NT).astype(jnp.bfloat16)
    scores = dot(lax.all_gather(conditioned, "dp", axis=1, tiled=True), queries, NT)
    return scores * (1.0 / rank)


def power_of_two(x):
    return x > 0 and x & (x - 1) == 0


def solution(mesh):
    n = mesh.shape["dp"]

    def body(activations, out_grads, in_basis, out_basis, preconditioner, queries):
        aligned = all(x.shape[0] % 128 == 0 for x in (in_basis, out_basis, preconditioner))
        split = LEN // activations.shape[0]
        regular = aligned and n >= 8 and power_of_two(n) and power_of_two(split) and 4 <= split <= n
        form = local if regular else local_gathered
        return form(activations, out_grads, in_basis, out_basis, preconditioner, queries)

    return jax.shard_map(
        body,
        mesh=mesh,
        in_specs=(
            P(("parts", "dp"), None),
            P(("parts", "dp"), None),
            P("dp", None),
            P("dp", None),
            P("dp", None),
            P("dp", None),
        ),
        out_specs=P("parts", "dp"),
        check_vma=False,
    )
```

```python
import functools
import math

import jax
import jax.numpy as jnp
from jax import lax
from jax.experimental import pallas as pl
from jax.experimental.pallas import tpu as pltpu
from jax.sharding import PartitionSpec as P

LEN = 1024
NT = (((1,), (1,)), ((), ()))
TN = (((0,), (0,)), ((), ()))
VMEM = pl.BlockSpec(memory_space=pltpu.VMEM)
HBM = pl.BlockSpec(memory_space=pltpu.HBM)


def held(space, *arrays):
    return [pltpu.with_memory_space_constraint(x, space) for x in arrays]


def dot(a, b, dims):
    return lax.dot_general(a, b, dims, preferred_element_type=jnp.float32)


def chip_behind(offset, chips):
    chip = lax.axis_index("dp") >> 1
    z, y = chip >> 1, chip & 1
    place = (jnp.where(y == 0, z, chips - 1 - z) - offset) & (chips - 1)
    return jnp.where(place < chips // 2, 2 * place, 2 * (chips - 1 - place) + 1)


def ring(x, step, chips):
    half = chips // 2
    chip = [2 * p if p < half else 2 * (chips - 1 - p) + 1 for p in range(chips)]
    pairs = [
        (chip[p] * 2 + c, chip[(p + step) % chips] * 2 + c) for p in range(chips) for c in range(2)
    ]
    return lax.ppermute(x, "dp", pairs)


def swap(x, bit, n):
    return lax.ppermute(x, "dp", [(i, i ^ bit) for i in range(n)])


def start_kernel(chips, act, grad, in_rows, out_rows, first, second, keep, send, sems):
    core = lax.axis_index("dp") & 1
    a_width, g_width = in_rows.shape[1], out_rows.shape[1]
    cut = first.shape[1]
    pairs = [
        (in_rows, first.at[:, pl.ds(0, a_width)]),
        (out_rows.at[:, pl.ds(0, cut - a_width)], first.at[:, pl.ds(a_width, cut - a_width)]),
        (out_rows.at[:, pl.ds(cut - a_width, second.shape[1])], second),
    ]
    for out, owner in ((send, 1 - core), (keep, core)):
        for chip in range(chips):
            block = 2 * chip + owner
            for ref, at, width in ((act, 0, a_width), (grad, a_width, g_width)):
                columns = pl.ds(pl.multiple_of(block * width, 128), width)
                pairs.append((ref.at[:, columns], out.at[chip, :, pl.ds(at, width)]))
    copies = [pltpu.make_async_copy(*pair, sems.at[i]) for i, pair in enumerate(pairs)]
    for copy in copies:
        copy.start()
    for copy in copies:
        copy.wait()


def start(act, grad, in_rows, out_rows, chips):
    rows = act.shape[0]
    rank, width = in_rows.shape[0], in_rows.shape[1] + out_rows.shape[1]
    cut = width // 256 * 128
    shapes = [(rank, cut), (rank, width - cut)] + [(chips, rows, width)] * 2
    return pl.pallas_call(
        functools.partial(start_kernel, chips),
        out_shape=[pltpu.VMEM(shape, act.dtype) for shape in shapes],
        in_specs=[HBM] * 4,
        out_specs=[VMEM] * 4,
        scratch_shapes=[pltpu.SemaphoreType.DMA((3 + 4 * chips,))],
        compiler_params=pltpu.CompilerParams(vmem_limit_bytes=16 * 2**20),
        cost_estimate=pl.CostEstimate(
            flops=0, bytes_accessed=4 * (rank + 2 * chips * rows) * width, transcendentals=0
        ),
    )(*held(pltpu.HBM, act, grad, in_rows, out_rows))


def project_kernel(chips, offsets, a_width, carry, *refs):
    keep, theirs = refs[:2]
    blocks, refs = refs[2 : 2 + 2 * len(offsets)], refs[2 + 2 * len(offsets) :]
    out = refs[-1]
    rank, cut = blocks[0].shape
    width = keep.shape[2]
    if carry:
        a_sum, g_sum = refs[0][:, :rank], refs[0][:, rank:]
    else:
        a_sum = g_sum = jnp.zeros((out.shape[0], rank), jnp.float32)
    for i, offset in enumerate(offsets):
        chip = chip_behind(offset, chips)

        def tokens(first, last):
            return jnp.concatenate([ref[chip, :, first:last] for ref in (keep, theirs)], axis=0)

        a_sum += dot(tokens(0, a_width), blocks[2 * i][:, :a_width], NT)
        g_sum += dot(tokens(a_width, cut), blocks[2 * i][:, a_width:], NT)
        g_sum += dot(tokens(cut, width), blocks[2 * i + 1][...], NT)
    out[:, :rank] = a_sum
    out[:, rank:] = g_sum


def project(tokens, blocks, offsets, a_width, carry=None):
    chips, rows, width = tokens[0].shape
    count = len(offsets)
    rank = blocks[0][0].shape[0]
    flat = [x for block in blocks for x in block]
    carried = () if carry is None else (carry,)
    return pl.pallas_call(
        functools.partial(project_kernel, chips, offsets, a_width, carry is not None),
        out_shape=pltpu.VMEM((2 * rows, 2 * rank), jnp.float32),
        in_specs=[VMEM] * (2 + len(flat) + len(carried)),
        out_specs=VMEM,
        compiler_params=pltpu.CompilerParams(vmem_limit_bytes=16 * 2**20),
        cost_estimate=pl.CostEstimate(
            flops=4 * count * rows * rank * width,
            bytes_accessed=count * (2 * rows + rank) * width * 2,
            transcendentals=0,
        ),
    )(*held(pltpu.VMEM, *tokens, *flat, *carried))


def to_all(x, groups):
    copies = jnp.broadcast_to(x[None], (len(groups[0]),) + x.shape)
    return lax.all_to_all(copies, "dp", 0, 0, axis_index_groups=groups, tiled=True)


def local(activations, out_grads, in_basis, out_basis, preconditioner, queries):
    rows = activations.shape[0]
    a_width, rank = in_basis.shape
    n = activations.shape[1] // a_width
    chips = n // 2
    split = LEN // rows

    *own, keep, send = start(activations, out_grads, in_basis.T, out_basis.T, chips)
    tokens = (keep, swap(send, 1, n))
    up, down = [own], [own]
    for i in range(chips // 2 - 1):
        up.append(tuple(ring(x, 1, chips) for x in up[-1]))
        down.append(tuple(ring(x, -1, chips) for x in down[-1]))
    run = functools.partial(project, tokens, a_width=a_width)
    near, offsets = [own], [0]
    for i in range(1, chips // 2 - 1):
        near += [up[i], down[i]]
        offsets += [i, -i]
    total = run(near, offsets)
    total, far_up, far_down = lax.optimization_barrier((total, up[-1][0], down[-1][1]))
    far = (ring(far_up, 1, chips), ring(far_down, -1, chips))
    last = chips // 2 - 1
    total = run([up[last], down[last]], [last, -last], carry=total)
    total = run([far], [chips // 2], carry=total)
    theirs = swap(total, 1, n)
    total = (total + jnp.concatenate([theirs[rows:], theirs[:rows]], axis=0)).astype(jnp.bfloat16)

    raw = dot(total[:, rank:], total[:, :rank], TN)
    raw = raw.reshape(1, rank * rank) * (1.0 / math.sqrt(LEN))
    planes = [[2 * i + c for i in range(chips)] for c in range(2)]
    raw = to_all(raw, planes).reshape(-1, split // 2, rank * rank)
    features = raw.sum(axis=1).astype(jnp.bfloat16)

    conditioned = dot(features, preconditioner, NT).astype(jnp.bfloat16)
    conditioned = to_all(conditioned, [list(range(n))])
    conditioned = conditioned.transpose(1, 0, 2).reshape(-1, queries.shape[1])
    return dot(conditioned, queries, NT) * (1.0 / rank)


def local_gathered(activations, out_grads, in_basis, out_basis, preconditioner, queries):
    rows = activations.shape[0]
    rank = in_basis.shape[1]
    act_proj = jnp.dot(
        activations,
        lax.all_gather(in_basis, "dp", axis=0, tiled=True),
        preferred_element_type=jnp.float32,
    ).astype(jnp.bfloat16)
    grad_proj = jnp.dot(
        out_grads,
        lax.all_gather(out_basis, "dp", axis=0, tiled=True),
        preferred_element_type=jnp.float32,
    ).astype(jnp.bfloat16)
    raw = dot(grad_proj, act_proj, TN).reshape(1, rank * rank) * (1.0 / math.sqrt(LEN))
    gathered = lax.all_gather(raw, "dp", axis=0, tiled=True)
    features = gathered.reshape(-1, LEN // rows, rank * rank).sum(axis=1).astype(jnp.bfloat16)
    conditioned = dot(features, preconditioner, NT).astype(jnp.bfloat16)
    scores = dot(lax.all_gather(conditioned, "dp", axis=1, tiled=True), queries, NT)
    return scores * (1.0 / rank)


def power_of_two(x):
    return x > 0 and x & (x - 1) == 0


def solution(mesh):
    n = mesh.shape["dp"]

    def body(activations, out_grads, in_basis, out_basis, preconditioner, queries):
        aligned = all(x.shape[0] % 128 == 0 for x in (in_basis, out_basis, preconditioner))
        split = LEN // activations.shape[0]
        regular = aligned and n >= 8 and power_of_two(n) and power_of_two(split) and 4 <= split <= n
        form = local if regular else local_gathered
        return form(activations, out_grads, in_basis, out_basis, preconditioner, queries)

    return jax.shard_map(
        body,
        mesh=mesh,
        in_specs=(
            P(("parts", "dp"), None),
            P(("parts", "dp"), None),
            P("dp", None),
            P("dp", None),
            P("dp", None),
            P("dp", None),
        ),
        out_specs=P("parts", "dp"),
        check_vma=False,
    )
```

```python
import functools
import math

import jax
import jax.numpy as jnp
from jax import lax
from jax.experimental import pallas as pl
from jax.experimental.pallas import tpu as pltpu
from jax.sharding import PartitionSpec as P

LEN = 1024
NT = (((1,), (1,)), ((), ()))
TN = (((0,), (0,)), ((), ()))
VMEM = pl.BlockSpec(memory_space=pltpu.VMEM)
HBM = pl.BlockSpec(memory_space=pltpu.HBM)


def held(space, *arrays):
    return [pltpu.with_memory_space_constraint(x, space) for x in arrays]


def dot(a, b, dims):
    return lax.dot_general(a, b, dims, preferred_element_type=jnp.float32)


def chip_behind(offset, chips):
    chip = lax.axis_index("dp") >> 1
    z, y = chip >> 1, chip & 1
    place = (jnp.where(y == 0, z, chips - 1 - z) - offset) & (chips - 1)
    return jnp.where(place < chips // 2, 2 * place, 2 * (chips - 1 - place) + 1)


def ring(x, step, chips):
    half = chips // 2
    chip = [2 * p if p < half else 2 * (chips - 1 - p) + 1 for p in range(chips)]
    pairs = [
        (chip[p] * 2 + c, chip[(p + step) % chips] * 2 + c) for p in range(chips) for c in range(2)
    ]
    return lax.ppermute(x, "dp", pairs)


def swap(x, bit, n):
    return lax.ppermute(x, "dp", [(i, i ^ bit) for i in range(n)])


def column_copies(chips, core, act, grad, out, sems):
    a_width = act.shape[1] // (2 * chips)
    g_width = grad.shape[1] // (2 * chips)
    copies = []
    for chip in range(chips):
        block = 2 * chip + core
        for k, (ref, at, width) in enumerate(((act, 0, a_width), (grad, a_width, g_width))):
            columns = pl.ds(pl.multiple_of(block * width, 128), width)
            copies.append(
                pltpu.make_async_copy(
                    ref.at[:, columns], out.at[chip, :, pl.ds(at, width)], sems.at[chip, k]
                )
            )
    return copies


def run_copies(copies):
    for copy in copies:
        copy.start()
    for copy in copies:
        copy.wait()


def start_kernel(chips, act, grad, in_rows, out_rows, first, second, send, sems, send_sems):
    core = lax.axis_index("dp") & 1
    a_width = in_rows.shape[1]
    cut = first.shape[1]
    pairs = [
        (in_rows, first.at[:, pl.ds(0, a_width)]),
        (out_rows.at[:, pl.ds(0, cut - a_width)], first.at[:, pl.ds(a_width, cut - a_width)]),
        (out_rows.at[:, pl.ds(cut - a_width, second.shape[1])], second),
    ]
    copies = [pltpu.make_async_copy(*pair, sems.at[i]) for i, pair in enumerate(pairs)]
    run_copies(copies + column_copies(chips, 1 - core, act, grad, send, send_sems))


def start(act, grad, in_rows, out_rows, chips):
    rows = act.shape[0]
    rank, width = in_rows.shape[0], in_rows.shape[1] + out_rows.shape[1]
    cut = width // 256 * 128
    shapes = (rank, cut), (rank, width - cut), (chips, rows, width)
    return pl.pallas_call(
        functools.partial(start_kernel, chips),
        out_shape=[pltpu.VMEM(shape, act.dtype) for shape in shapes],
        in_specs=[HBM] * 4,
        out_specs=[VMEM] * 3,
        scratch_shapes=[pltpu.SemaphoreType.DMA((3,)), pltpu.SemaphoreType.DMA((chips, 2))],
        compiler_params=pltpu.CompilerParams(vmem_limit_bytes=16 * 2**20),
        cost_estimate=pl.CostEstimate(
            flops=0, bytes_accessed=4 * (rank + chips * rows) * width, transcendentals=0
        ),
    )(*held(pltpu.HBM, act, grad, in_rows, out_rows))


def keep_kernel(chips, act, grad, keep, sems):
    core = lax.axis_index("dp") & 1
    run_copies(column_copies(chips, core, act, grad, keep, sems))


def keep_columns(act, grad, chips):
    rows, width = act.shape[0], (act.shape[1] + grad.shape[1]) // (2 * chips)
    return pl.pallas_call(
        functools.partial(keep_kernel, chips),
        out_shape=pltpu.VMEM((chips, rows, width), act.dtype),
        in_specs=[HBM] * 2,
        out_specs=VMEM,
        scratch_shapes=[pltpu.SemaphoreType.DMA((chips, 2))],
        compiler_params=pltpu.CompilerParams(vmem_limit_bytes=16 * 2**20),
        cost_estimate=pl.CostEstimate(
            flops=0, bytes_accessed=4 * chips * rows * width, transcendentals=0
        ),
    )(*held(pltpu.HBM, act, grad))


def project_kernel(chips, offsets, a_width, carry, *refs):
    keep, theirs = refs[:2]
    blocks, refs = refs[2 : 2 + 2 * len(offsets)], refs[2 + 2 * len(offsets) :]
    out = refs[-1]
    rank, cut = blocks[0].shape
    width = keep.shape[2]
    if carry:
        a_sum, g_sum = refs[0][:, :rank], refs[0][:, rank:]
    else:
        a_sum = g_sum = jnp.zeros((out.shape[0], rank), jnp.float32)
    for i, offset in enumerate(offsets):
        chip = chip_behind(offset, chips)

        def tokens(first, last):
            return jnp.concatenate([ref[chip, :, first:last] for ref in (keep, theirs)], axis=0)

        a_sum += dot(tokens(0, a_width), blocks[2 * i][:, :a_width], NT)
        g_sum += dot(tokens(a_width, cut), blocks[2 * i][:, a_width:], NT)
        g_sum += dot(tokens(cut, width), blocks[2 * i + 1][...], NT)
    out[:, :rank] = a_sum
    out[:, rank:] = g_sum


def project(tokens, blocks, offsets, a_width, carry=None):
    chips, rows, width = tokens[0].shape
    count = len(offsets)
    rank = blocks[0][0].shape[0]
    flat = [x for block in blocks for x in block]
    carried = () if carry is None else (carry,)
    return pl.pallas_call(
        functools.partial(project_kernel, chips, offsets, a_width, carry is not None),
        out_shape=pltpu.VMEM((2 * rows, 2 * rank), jnp.float32),
        in_specs=[VMEM] * (2 + len(flat) + len(carried)),
        out_specs=VMEM,
        compiler_params=pltpu.CompilerParams(vmem_limit_bytes=16 * 2**20),
        cost_estimate=pl.CostEstimate(
            flops=4 * count * rows * rank * width,
            bytes_accessed=count * (2 * rows + rank) * width * 2,
            transcendentals=0,
        ),
    )(*held(pltpu.VMEM, *tokens, *flat, *carried))


def to_all(x, groups):
    copies = jnp.broadcast_to(x[None], (len(groups[0]),) + x.shape)
    return lax.all_to_all(copies, "dp", 0, 0, axis_index_groups=groups, tiled=True)


def local(activations, out_grads, in_basis, out_basis, preconditioner, queries):
    rows = activations.shape[0]
    a_width, rank = in_basis.shape
    n = activations.shape[1] // a_width
    chips = n // 2
    split = LEN // rows

    *own, send = start(activations, out_grads, in_basis.T, out_basis.T, chips)
    theirs = swap(send, 1, n)
    up, down = [own], [own]
    for _ in range(chips // 2 - 1):
        up.append([ring(x, 1, chips) for x in up[-1]])
        down.append([ring(x, -1, chips) for x in down[-1]])
    last = chips // 2 - 1
    keep = keep_columns(activations, out_grads, chips)
    keep, far_up, far_down = lax.optimization_barrier((keep, up[last][0], down[last][1]))
    far = (ring(far_up, 1, chips), ring(far_down, -1, chips))

    run = functools.partial(project, (keep, theirs), a_width=a_width)
    near, offsets = [own], [0]
    for i in range(1, last):
        near += [up[i], down[i]]
        offsets += [i, -i]
    total = run(near, offsets)
    total = run([up[last], down[last]], [last, -last], carry=total)
    total = run([far], [chips // 2], carry=total)
    theirs = swap(total, 1, n)
    total = (total + jnp.concatenate([theirs[rows:], theirs[:rows]], axis=0)).astype(jnp.bfloat16)

    raw = dot(total[:, rank:], total[:, :rank], TN)
    raw = raw.reshape(1, rank * rank) * (1.0 / math.sqrt(LEN))
    planes = [[2 * i + c for i in range(chips)] for c in range(2)]
    raw = to_all(raw, planes).reshape(-1, split // 2, rank * rank)
    features = raw.sum(axis=1).astype(jnp.bfloat16)

    conditioned = dot(features, preconditioner, NT).astype(jnp.bfloat16)
    conditioned = to_all(conditioned, [list(range(n))])
    conditioned = conditioned.transpose(1, 0, 2).reshape(-1, queries.shape[1])
    return dot(conditioned, queries, NT) * (1.0 / rank)


def local_gathered(activations, out_grads, in_basis, out_basis, preconditioner, queries):
    rows = activations.shape[0]
    rank = in_basis.shape[1]
    act_proj = jnp.dot(
        activations,
        lax.all_gather(in_basis, "dp", axis=0, tiled=True),
        preferred_element_type=jnp.float32,
    ).astype(jnp.bfloat16)
    grad_proj = jnp.dot(
        out_grads,
        lax.all_gather(out_basis, "dp", axis=0, tiled=True),
        preferred_element_type=jnp.float32,
    ).astype(jnp.bfloat16)
    raw = dot(grad_proj, act_proj, TN).reshape(1, rank * rank) * (1.0 / math.sqrt(LEN))
    gathered = lax.all_gather(raw, "dp", axis=0, tiled=True)
    features = gathered.reshape(-1, LEN // rows, rank * rank).sum(axis=1).astype(jnp.bfloat16)
    conditioned = dot(features, preconditioner, NT).astype(jnp.bfloat16)
    scores = dot(lax.all_gather(conditioned, "dp", axis=1, tiled=True), queries, NT)
    return scores * (1.0 / rank)


def power_of_two(x):
    return x > 0 and x & (x - 1) == 0


def solution(mesh):
    n = mesh.shape["dp"]

    def body(activations, out_grads, in_basis, out_basis, preconditioner, queries):
        aligned = all(x.shape[0] % 128 == 0 for x in (in_basis, out_basis, preconditioner))
        split = LEN // activations.shape[0]
        regular = aligned and n >= 8 and power_of_two(n) and power_of_two(split) and 4 <= split <= n
        form = local if regular else local_gathered
        return form(activations, out_grads, in_basis, out_basis, preconditioner, queries)

    return jax.shard_map(
        body,
        mesh=mesh,
        in_specs=(
            P(("parts", "dp"), None),
            P(("parts", "dp"), None),
            P("dp", None),
            P("dp", None),
            P("dp", None),
            P("dp", None),
        ),
        out_specs=P("parts", "dp"),
        check_vma=False,
    )
```

```python
import functools
import math

import jax
import jax.numpy as jnp
from jax import lax
from jax.experimental import pallas as pl
from jax.experimental.pallas import tpu as pltpu
from jax.sharding import PartitionSpec as P

LEN = 1024
NT = (((1,), (1,)), ((), ()))
TN = (((0,), (0,)), ((), ()))
VMEM = pl.BlockSpec(memory_space=pltpu.VMEM)
HBM = pl.BlockSpec(memory_space=pltpu.HBM)


def held(space, *arrays):
    return [pltpu.with_memory_space_constraint(x, space) for x in arrays]


def dot(a, b, dims):
    return lax.dot_general(a, b, dims, preferred_element_type=jnp.float32)


def chip_behind(offset, chips):
    chip = lax.axis_index("dp") >> 1
    z, y = chip >> 1, chip & 1
    place = (jnp.where(y == 0, z, chips - 1 - z) - offset) & (chips - 1)
    return jnp.where(place < chips // 2, 2 * place, 2 * (chips - 1 - place) + 1)


def ring(x, step, chips):
    half = chips // 2
    chip = [2 * p if p < half else 2 * (chips - 1 - p) + 1 for p in range(chips)]
    pairs = [
        (chip[p] * 2 + c, chip[(p + step) % chips] * 2 + c) for p in range(chips) for c in range(2)
    ]
    return lax.ppermute(x, "dp", pairs)


def swap(x, bit, n):
    return lax.ppermute(x, "dp", [(i, i ^ bit) for i in range(n)])


def column_copies(chips, core, act, grad, out, sems):
    a_width = act.shape[1] // (2 * chips)
    g_width = grad.shape[1] // (2 * chips)
    copies = []
    for chip in range(chips):
        block = 2 * chip + core
        for k, (ref, at, width) in enumerate(((act, 0, a_width), (grad, a_width, g_width))):
            columns = pl.ds(pl.multiple_of(block * width, 128), width)
            copies.append(
                pltpu.make_async_copy(
                    ref.at[:, columns], out.at[chip, :, pl.ds(at, width)], sems.at[chip, k]
                )
            )
    return copies


def run_copies(copies):
    for copy in copies:
        copy.start()
    for copy in copies:
        copy.wait()


def start_kernel(chips, act, grad, in_rows, out_rows, first, second, send, sems, send_sems):
    core = lax.axis_index("dp") & 1
    a_width = in_rows.shape[1]
    cut = first.shape[1]
    pairs = [
        (in_rows, first.at[:, pl.ds(0, a_width)]),
        (out_rows.at[:, pl.ds(0, cut - a_width)], first.at[:, pl.ds(a_width, cut - a_width)]),
        (out_rows.at[:, pl.ds(cut - a_width, second.shape[1])], second),
    ]
    copies = [pltpu.make_async_copy(*pair, sems.at[i]) for i, pair in enumerate(pairs)]
    run_copies(copies + column_copies(chips, 1 - core, act, grad, send, send_sems))


def start(act, grad, in_rows, out_rows, chips):
    rows = act.shape[0]
    rank, width = in_rows.shape[0], in_rows.shape[1] + out_rows.shape[1]
    cut = width // 256 * 128
    shapes = (rank, cut), (rank, width - cut), (chips, rows, width)
    return pl.pallas_call(
        functools.partial(start_kernel, chips),
        out_shape=[pltpu.VMEM(shape, act.dtype) for shape in shapes],
        in_specs=[HBM] * 4,
        out_specs=[VMEM] * 3,
        scratch_shapes=[pltpu.SemaphoreType.DMA((3,)), pltpu.SemaphoreType.DMA((chips, 2))],
        compiler_params=pltpu.CompilerParams(vmem_limit_bytes=16 * 2**20),
        cost_estimate=pl.CostEstimate(
            flops=0, bytes_accessed=4 * (rank + chips * rows) * width, transcendentals=0
        ),
    )(*held(pltpu.HBM, act, grad, in_rows, out_rows))


def keep_kernel(chips, act, grad, keep, sems):
    core = lax.axis_index("dp") & 1
    run_copies(column_copies(chips, core, act, grad, keep, sems))


def keep_columns(act, grad, chips):
    rows, width = act.shape[0], (act.shape[1] + grad.shape[1]) // (2 * chips)
    return pl.pallas_call(
        functools.partial(keep_kernel, chips),
        out_shape=pltpu.VMEM((chips, rows, width), act.dtype),
        in_specs=[HBM] * 2,
        out_specs=VMEM,
        scratch_shapes=[pltpu.SemaphoreType.DMA((chips, 2))],
        compiler_params=pltpu.CompilerParams(vmem_limit_bytes=16 * 2**20),
        cost_estimate=pl.CostEstimate(
            flops=0, bytes_accessed=4 * chips * rows * width, transcendentals=0
        ),
    )(*held(pltpu.HBM, act, grad))


def project_kernel(chips, offsets, parts, a_width, cut, carry, *refs):
    keep, theirs = refs[:2]
    chunks, refs = refs[2 : 2 + len(parts)], refs[2 + len(parts) :]
    out = refs[-1]
    rank = chunks[0].shape[0]
    width = keep.shape[2]
    if carry:
        a_sum, g_sum = refs[0][:, :rank], refs[0][:, rank:]
    else:
        a_sum = g_sum = jnp.zeros((out.shape[0], rank), jnp.float32)
    for offset, part, chunk in zip(offsets, parts, chunks):
        chip = chip_behind(offset, chips)

        def tokens(first, last):
            return jnp.concatenate([ref[chip, :, first:last] for ref in (keep, theirs)], axis=0)

        if part == 0:
            a_sum += dot(tokens(0, a_width), chunk[:, :a_width], NT)
            g_sum += dot(tokens(a_width, cut), chunk[:, a_width:], NT)
        else:
            g_sum += dot(tokens(cut, width), chunk[...], NT)
    out[:, :rank] = a_sum
    out[:, rank:] = g_sum


def project(tokens, chunks, a_width, cut, carry=None):
    chips, rows, width = tokens[0].shape
    offsets, parts, flat = zip(*chunks)
    rank = flat[0].shape[0]
    carried = () if carry is None else (carry,)
    columns = sum(x.shape[1] for x in flat)
    return pl.pallas_call(
        functools.partial(project_kernel, chips, offsets, parts, a_width, cut, carry is not None),
        out_shape=pltpu.VMEM((2 * rows, 2 * rank), jnp.float32),
        in_specs=[VMEM] * (2 + len(flat) + len(carried)),
        out_specs=VMEM,
        compiler_params=pltpu.CompilerParams(vmem_limit_bytes=16 * 2**20),
        cost_estimate=pl.CostEstimate(
            flops=4 * rows * rank * columns,
            bytes_accessed=(2 * rows + rank) * columns * 2,
            transcendentals=0,
        ),
    )(*held(pltpu.VMEM, *tokens, *flat, *carried))


def score_kernel(scale, conditioned, queries, out):
    width = conditioned.shape[2]
    total = jnp.zeros(out.shape, jnp.float32)
    for i in range(conditioned.shape[0]):
        total += dot(conditioned[i], queries[:, i * width : (i + 1) * width], NT)
    out[...] = total * scale


def score(conditioned, queries, scale):
    return pl.pallas_call(
        functools.partial(score_kernel, scale),
        out_shape=jax.ShapeDtypeStruct((conditioned.shape[1], queries.shape[0]), jnp.float32),
        in_specs=[VMEM] * 2,
        out_specs=VMEM,
        compiler_params=pltpu.CompilerParams(vmem_limit_bytes=16 * 2**20),
    )(*held(pltpu.VMEM, conditioned, queries))


def to_all(x, groups):
    copies = jnp.broadcast_to(x[None], (len(groups[0]),) + x.shape)
    return lax.all_to_all(copies, "dp", 0, 0, axis_index_groups=groups, tiled=True)


def local(activations, out_grads, in_basis, out_basis, preconditioner, queries):
    rows = activations.shape[0]
    a_width, rank = in_basis.shape
    n = activations.shape[1] // a_width
    chips = n // 2
    split = LEN // rows

    *own, send = start(activations, out_grads, in_basis.T, out_basis.T, chips)
    theirs = swap(send, 1, n)
    up, down = [own], [own]
    for _ in range(chips // 2 - 1):
        up.append([ring(x, 1, chips) for x in up[-1]])
        down.append([ring(x, -1, chips) for x in down[-1]])
    last = chips // 2 - 1
    keep = keep_columns(activations, out_grads, chips)
    keep, far_up, far_down = lax.optimization_barrier((keep, up[last][0], down[last][1]))
    far = (ring(far_up, 1, chips), ring(far_down, -1, chips))

    cut = own[0].shape[1]
    run = functools.partial(project, (keep, theirs), a_width=a_width, cut=cut)

    def both(block, offset):
        return [(offset, part, x) for part, x in enumerate(block)]

    near = both(own, 0)
    for i in range(1, last):
        near += both(up[i], i) + both(down[i], -i)
    total = run(near)
    total = run(both(up[last], last) + both(down[last], -last), carry=total)
    for part, x in enumerate(far):
        total = run([(chips // 2, part, x)], carry=total)
    theirs = swap(total, 1, n)
    total = (total + jnp.concatenate([theirs[rows:], theirs[:rows]], axis=0)).astype(jnp.bfloat16)

    raw = dot(total[:, rank:], total[:, :rank], TN)
    raw = (raw * (1.0 / math.sqrt(LEN))).reshape(-1, 128)
    planes = [[2 * i + c for i in range(chips)] for c in range(2)]
    raw = to_all(raw, planes)
    features = raw.reshape((-1, split // 2) + raw.shape[1:]).sum(axis=1)
    features = features.astype(jnp.bfloat16).reshape(-1, rank * rank)

    conditioned = dot(features, preconditioner, NT).astype(jnp.bfloat16)
    return score(to_all(conditioned, [list(range(n))]), queries, 1.0 / rank)


def local_gathered(activations, out_grads, in_basis, out_basis, preconditioner, queries):
    rows = activations.shape[0]
    rank = in_basis.shape[1]
    act_proj = jnp.dot(
        activations,
        lax.all_gather(in_basis, "dp", axis=0, tiled=True),
        preferred_element_type=jnp.float32,
    ).astype(jnp.bfloat16)
    grad_proj = jnp.dot(
        out_grads,
        lax.all_gather(out_basis, "dp", axis=0, tiled=True),
        preferred_element_type=jnp.float32,
    ).astype(jnp.bfloat16)
    raw = dot(grad_proj, act_proj, TN).reshape(1, rank * rank) * (1.0 / math.sqrt(LEN))
    gathered = lax.all_gather(raw, "dp", axis=0, tiled=True)
    features = gathered.reshape(-1, LEN // rows, rank * rank).sum(axis=1).astype(jnp.bfloat16)
    conditioned = dot(features, preconditioner, NT).astype(jnp.bfloat16)
    scores = dot(lax.all_gather(conditioned, "dp", axis=1, tiled=True), queries, NT)
    return scores * (1.0 / rank)


def power_of_two(x):
    return x > 0 and x & (x - 1) == 0


def solution(mesh):
    n = mesh.shape["dp"]

    def body(activations, out_grads, in_basis, out_basis, preconditioner, queries):
        aligned = all(x.shape[0] % 128 == 0 for x in (in_basis, out_basis, preconditioner))
        split = LEN // activations.shape[0]
        regular = aligned and n >= 8 and power_of_two(n) and power_of_two(split) and 4 <= split <= n
        form = local if regular else local_gathered
        return form(activations, out_grads, in_basis, out_basis, preconditioner, queries)

    return jax.shard_map(
        body,
        mesh=mesh,
        in_specs=(
            P(("parts", "dp"), None),
            P(("parts", "dp"), None),
            P("dp", None),
            P("dp", None),
            P("dp", None),
            P("dp", None),
        ),
        out_specs=P("parts", "dp"),
        check_vma=False,
    )
```

```python
import functools
import math

import jax
import jax.numpy as jnp
from jax import lax
from jax.experimental import pallas as pl
from jax.experimental.pallas import tpu as pltpu
from jax.sharding import PartitionSpec as P

LEN = 1024
NT = (((1,), (1,)), ((), ()))
TN = (((0,), (0,)), ((), ()))
VMEM = pl.BlockSpec(memory_space=pltpu.VMEM)
HBM = pl.BlockSpec(memory_space=pltpu.HBM)


def held(space, *arrays):
    return [pltpu.with_memory_space_constraint(x, space) for x in arrays]


def dot(a, b, dims):
    return lax.dot_general(a, b, dims, preferred_element_type=jnp.float32)


def chip_behind(offset, chips):
    chip = lax.axis_index("dp") >> 1
    z, y = chip >> 1, chip & 1
    place = (jnp.where(y == 0, z, chips - 1 - z) - offset) & (chips - 1)
    return jnp.where(place < chips // 2, 2 * place, 2 * (chips - 1 - place) + 1)


def ring(x, step, chips):
    half = chips // 2
    chip = [2 * p if p < half else 2 * (chips - 1 - p) + 1 for p in range(chips)]
    pairs = [
        (chip[p] * 2 + c, chip[(p + step) % chips] * 2 + 1 - c) for p in range(chips) for c in range(2)
    ]
    return lax.ppermute(x, "dp", pairs)


def swap(x, bit, n):
    return lax.ppermute(x, "dp", [(i, i ^ bit) for i in range(n)])


def odd(chip):
    return (chip ^ (chip >> 1)) & 1


def column_copies(chips, core, act, grad, out, sems):
    ring_of = core ^ odd(lax.axis_index("dp") >> 1)
    a_width = act.shape[1] // (2 * chips)
    g_width = grad.shape[1] // (2 * chips)
    copies = []
    for chip in range(chips):
        block = 2 * chip + (ring_of ^ odd(chip))
        for k, (ref, at, width) in enumerate(((act, 0, a_width), (grad, a_width, g_width))):
            columns = pl.ds(pl.multiple_of(block * width, 128), width)
            copies.append(
                pltpu.make_async_copy(
                    ref.at[:, columns], out.at[chip, :, pl.ds(at, width)], sems.at[chip, k]
                )
            )
    return copies


def run_copies(copies):
    for copy in copies:
        copy.start()
    for copy in copies:
        copy.wait()


def start_kernel(chips, act, grad, in_rows, out_rows, first, second, send, sems, send_sems):
    core = lax.axis_index("dp") & 1
    a_width = in_rows.shape[1]
    cut = first.shape[1]
    pairs = [
        (in_rows, first.at[:, pl.ds(0, a_width)]),
        (out_rows.at[:, pl.ds(0, cut - a_width)], first.at[:, pl.ds(a_width, cut - a_width)]),
        (out_rows.at[:, pl.ds(cut - a_width, second.shape[1])], second),
    ]
    copies = [pltpu.make_async_copy(*pair, sems.at[i]) for i, pair in enumerate(pairs)]
    run_copies(copies + column_copies(chips, 1 - core, act, grad, send, send_sems))


def start(act, grad, in_rows, out_rows, chips):
    rows = act.shape[0]
    rank, width = in_rows.shape[0], in_rows.shape[1] + out_rows.shape[1]
    cut = width // 256 * 128
    shapes = (rank, cut), (rank, width - cut), (chips, rows, width)
    return pl.pallas_call(
        functools.partial(start_kernel, chips),
        out_shape=[pltpu.VMEM(shape, act.dtype) for shape in shapes],
        in_specs=[HBM] * 4,
        out_specs=[VMEM] * 3,
        scratch_shapes=[pltpu.SemaphoreType.DMA((3,)), pltpu.SemaphoreType.DMA((chips, 2))],
        compiler_params=pltpu.CompilerParams(vmem_limit_bytes=16 * 2**20),
        cost_estimate=pl.CostEstimate(
            flops=0, bytes_accessed=4 * (rank + chips * rows) * width, transcendentals=0
        ),
    )(*held(pltpu.HBM, act, grad, in_rows, out_rows))


def keep_kernel(chips, act, grad, keep, sems):
    core = lax.axis_index("dp") & 1
    run_copies(column_copies(chips, core, act, grad, keep, sems))


def keep_columns(act, grad, chips):
    rows, width = act.shape[0], (act.shape[1] + grad.shape[1]) // (2 * chips)
    return pl.pallas_call(
        functools.partial(keep_kernel, chips),
        out_shape=pltpu.VMEM((chips, rows, width), act.dtype),
        in_specs=[HBM] * 2,
        out_specs=VMEM,
        scratch_shapes=[pltpu.SemaphoreType.DMA((chips, 2))],
        compiler_params=pltpu.CompilerParams(vmem_limit_bytes=16 * 2**20),
        cost_estimate=pl.CostEstimate(
            flops=0, bytes_accessed=4 * chips * rows * width, transcendentals=0
        ),
    )(*held(pltpu.HBM, act, grad))


def project_kernel(chips, offsets, parts, a_width, cut, carry, *refs):
    keep, theirs = refs[:2]
    chunks, refs = refs[2 : 2 + len(parts)], refs[2 + len(parts) :]
    out = refs[-1]
    rank = chunks[0].shape[0]
    width = keep.shape[2]
    if carry:
        a_sum, g_sum = refs[0][:, :rank], refs[0][:, rank:]
    else:
        a_sum = g_sum = jnp.zeros((out.shape[0], rank), jnp.float32)
    for offset, part, chunk in zip(offsets, parts, chunks):
        chip = chip_behind(offset, chips)

        def tokens(first, last):
            return jnp.concatenate([ref[chip, :, first:last] for ref in (keep, theirs)], axis=0)

        if part == 0:
            a_sum += dot(tokens(0, a_width), chunk[:, :a_width], NT)
            g_sum += dot(tokens(a_width, cut), chunk[:, a_width:], NT)
        else:
            g_sum += dot(tokens(cut, width), chunk[...], NT)
    out[:, :rank] = a_sum
    out[:, rank:] = g_sum


def project(tokens, chunks, a_width, cut, carry=None):
    chips, rows, width = tokens[0].shape
    offsets, parts, flat = zip(*chunks)
    rank = flat[0].shape[0]
    carried = () if carry is None else (carry,)
    columns = sum(x.shape[1] for x in flat)
    return pl.pallas_call(
        functools.partial(project_kernel, chips, offsets, parts, a_width, cut, carry is not None),
        out_shape=pltpu.VMEM((2 * rows, 2 * rank), jnp.float32),
        in_specs=[VMEM] * (2 + len(flat) + len(carried)),
        out_specs=VMEM,
        compiler_params=pltpu.CompilerParams(vmem_limit_bytes=16 * 2**20),
        cost_estimate=pl.CostEstimate(
            flops=4 * rows * rank * columns,
            bytes_accessed=(2 * rows + rank) * columns * 2,
            transcendentals=0,
        ),
    )(*held(pltpu.VMEM, *tokens, *flat, *carried))


def score_kernel(scale, conditioned, queries, out):
    width = conditioned.shape[2]
    total = jnp.zeros(out.shape, jnp.float32)
    for i in range(conditioned.shape[0]):
        total += dot(conditioned[i], queries[:, i * width : (i + 1) * width], NT)
    out[...] = total * scale


def score(conditioned, queries, scale):
    return pl.pallas_call(
        functools.partial(score_kernel, scale),
        out_shape=jax.ShapeDtypeStruct((conditioned.shape[1], queries.shape[0]), jnp.float32),
        in_specs=[VMEM] * 2,
        out_specs=VMEM,
        compiler_params=pltpu.CompilerParams(vmem_limit_bytes=16 * 2**20),
    )(*held(pltpu.VMEM, conditioned, queries))


def to_all(x, groups):
    copies = jnp.broadcast_to(x[None], (len(groups[0]),) + x.shape)
    return lax.all_to_all(copies, "dp", 0, 0, axis_index_groups=groups, tiled=True)


def local(activations, out_grads, in_basis, out_basis, preconditioner, queries):
    rows = activations.shape[0]
    a_width, rank = in_basis.shape
    n = activations.shape[1] // a_width
    chips = n // 2
    split = LEN // rows

    *own, send = start(activations, out_grads, in_basis.T, out_basis.T, chips)
    theirs = swap(send, 1, n)
    up, down = [own], [own]
    for _ in range(chips // 2 - 1):
        up.append([ring(x, 1, chips) for x in up[-1]])
        down.append([ring(x, -1, chips) for x in down[-1]])
    last = chips // 2 - 1
    keep = keep_columns(activations, out_grads, chips)
    keep, far_up, far_down = lax.optimization_barrier((keep, up[last][0], down[last][1]))
    far = (ring(far_up, 1, chips), ring(far_down, -1, chips))

    cut = own[0].shape[1]
    run = functools.partial(project, (keep, theirs), a_width=a_width, cut=cut)

    def both(block, offset):
        return [(offset, part, x) for part, x in enumerate(block)]

    near = both(own, 0)
    for i in range(1, last):
        near += both(up[i], i) + both(down[i], -i)
    total = run(near)
    total = run(both(up[last], last) + both(down[last], -last), carry=total)
    for part, x in enumerate(far):
        total = run([(chips // 2, part, x)], carry=total)
    theirs = swap(total, 1, n)
    total = (total + jnp.concatenate([theirs[rows:], theirs[:rows]], axis=0)).astype(jnp.bfloat16)

    raw = dot(total[:, rank:], total[:, :rank], TN)
    raw = (raw * (1.0 / math.sqrt(LEN))).reshape(-1, 128)
    planes = [[2 * i + c for i in range(chips)] for c in range(2)]
    raw = to_all(raw, planes)
    features = raw.reshape((-1, split // 2) + raw.shape[1:]).sum(axis=1)
    features = features.astype(jnp.bfloat16).reshape(-1, rank * rank)

    conditioned = dot(features, preconditioner, NT).astype(jnp.bfloat16)
    return score(to_all(conditioned, [list(range(n))]), queries, 1.0 / rank)


def local_gathered(activations, out_grads, in_basis, out_basis, preconditioner, queries):
    rows = activations.shape[0]
    rank = in_basis.shape[1]
    act_proj = jnp.dot(
        activations,
        lax.all_gather(in_basis, "dp", axis=0, tiled=True),
        preferred_element_type=jnp.float32,
    ).astype(jnp.bfloat16)
    grad_proj = jnp.dot(
        out_grads,
        lax.all_gather(out_basis, "dp", axis=0, tiled=True),
        preferred_element_type=jnp.float32,
    ).astype(jnp.bfloat16)
    raw = dot(grad_proj, act_proj, TN).reshape(1, rank * rank) * (1.0 / math.sqrt(LEN))
    gathered = lax.all_gather(raw, "dp", axis=0, tiled=True)
    features = gathered.reshape(-1, LEN // rows, rank * rank).sum(axis=1).astype(jnp.bfloat16)
    conditioned = dot(features, preconditioner, NT).astype(jnp.bfloat16)
    scores = dot(lax.all_gather(conditioned, "dp", axis=1, tiled=True), queries, NT)
    return scores * (1.0 / rank)


def power_of_two(x):
    return x > 0 and x & (x - 1) == 0


def solution(mesh):
    n = mesh.shape["dp"]

    def body(activations, out_grads, in_basis, out_basis, preconditioner, queries):
        aligned = all(x.shape[0] % 128 == 0 for x in (in_basis, out_basis, preconditioner))
        split = LEN // activations.shape[0]
        regular = aligned and n >= 8 and power_of_two(n) and power_of_two(split) and 4 <= split <= n
        form = local if regular else local_gathered
        return form(activations, out_grads, in_basis, out_basis, preconditioner, queries)

    return jax.shard_map(
        body,
        mesh=mesh,
        in_specs=(
            P(("parts", "dp"), None),
            P(("parts", "dp"), None),
            P("dp", None),
            P("dp", None),
            P("dp", None),
            P("dp", None),
        ),
        out_specs=P("parts", "dp"),
        check_vma=False,
    )
```

```python
import functools
import math

import jax
import jax.numpy as jnp
from jax import lax
from jax.experimental import pallas as pl
from jax.experimental.pallas import tpu as pltpu
from jax.sharding import PartitionSpec as P

LEN = 1024
NT = (((1,), (1,)), ((), ()))
TN = (((0,), (0,)), ((), ()))
VMEM = pl.BlockSpec(memory_space=pltpu.VMEM)
HBM = pl.BlockSpec(memory_space=pltpu.HBM)


def held(space, *arrays):
    return [pltpu.with_memory_space_constraint(x, space) for x in arrays]


def dot(a, b, dims):
    return lax.dot_general(a, b, dims, preferred_element_type=jnp.float32)


def chip_behind(offset, chips):
    chip = lax.axis_index("dp") >> 1
    z, y = chip >> 1, chip & 1
    place = (jnp.where(y == 0, z, chips - 1 - z) - offset) & (chips - 1)
    return jnp.where(place < chips // 2, 2 * place, 2 * (chips - 1 - place) + 1)


def ring(x, step, chips):
    half = chips // 2
    chip = [2 * p if p < half else 2 * (chips - 1 - p) + 1 for p in range(chips)]
    pairs = [
        (chip[p] * 2 + c, chip[(p + step) % chips] * 2 + 1 - c) for p in range(chips) for c in range(2)
    ]
    return lax.ppermute(x, "dp", pairs)


def swap(x, bit, n):
    return lax.ppermute(x, "dp", [(i, i ^ bit) for i in range(n)])


def odd(chip):
    return (chip ^ (chip >> 1)) & 1


def column_copies(chips, core, act, grad, out, sems):
    ring_of = core ^ odd(lax.axis_index("dp") >> 1)
    a_width = act.shape[1] // (2 * chips)
    g_width = grad.shape[1] // (2 * chips)
    copies = []
    for chip in range(chips):
        block = 2 * chip + (ring_of ^ odd(chip))
        for k, (ref, at, width) in enumerate(((act, 0, a_width), (grad, a_width, g_width))):
            columns = pl.ds(pl.multiple_of(block * width, 128), width)
            copies.append(
                pltpu.make_async_copy(
                    ref.at[:, columns], out.at[chip, :, pl.ds(at, width)], sems.at[chip, k]
                )
            )
    return copies


def run_copies(copies):
    for copy in copies:
        copy.start()
    for copy in copies:
        copy.wait()


def start_kernel(chips, act, grad, in_rows, out_rows, first, second, send, sems, send_sems):
    core = lax.axis_index("dp") & 1
    a_width = in_rows.shape[1]
    cut = first.shape[1]
    pairs = [
        (in_rows, first.at[:, pl.ds(0, a_width)]),
        (out_rows.at[:, pl.ds(0, cut - a_width)], first.at[:, pl.ds(a_width, cut - a_width)]),
        (out_rows.at[:, pl.ds(cut - a_width, second.shape[1])], second),
    ]
    copies = [pltpu.make_async_copy(*pair, sems.at[i]) for i, pair in enumerate(pairs)]
    run_copies(copies + column_copies(chips, 1 - core, act, grad, send, send_sems))


def start(act, grad, in_rows, out_rows, chips):
    rows = act.shape[0]
    rank, width = in_rows.shape[0], in_rows.shape[1] + out_rows.shape[1]
    cut = width // 256 * 128
    shapes = (rank, cut), (rank, width - cut), (chips, rows, width)
    return pl.pallas_call(
        functools.partial(start_kernel, chips),
        out_shape=[pltpu.VMEM(shape, act.dtype) for shape in shapes],
        in_specs=[HBM] * 4,
        out_specs=[VMEM] * 3,
        scratch_shapes=[pltpu.SemaphoreType.DMA((3,)), pltpu.SemaphoreType.DMA((chips, 2))],
        compiler_params=pltpu.CompilerParams(vmem_limit_bytes=16 * 2**20),
        cost_estimate=pl.CostEstimate(
            flops=0, bytes_accessed=4 * (rank + chips * rows) * width, transcendentals=0
        ),
    )(*held(pltpu.HBM, act, grad, in_rows, out_rows))


def keep_kernel(chips, act, grad, keep, sems):
    core = lax.axis_index("dp") & 1
    run_copies(column_copies(chips, core, act, grad, keep, sems))


def keep_columns(act, grad, chips):
    rows, width = act.shape[0], (act.shape[1] + grad.shape[1]) // (2 * chips)
    return pl.pallas_call(
        functools.partial(keep_kernel, chips),
        out_shape=pltpu.VMEM((chips, rows, width), act.dtype),
        in_specs=[HBM] * 2,
        out_specs=VMEM,
        scratch_shapes=[pltpu.SemaphoreType.DMA((chips, 2))],
        compiler_params=pltpu.CompilerParams(vmem_limit_bytes=16 * 2**20),
        cost_estimate=pl.CostEstimate(
            flops=0, bytes_accessed=4 * chips * rows * width, transcendentals=0
        ),
    )(*held(pltpu.HBM, act, grad))


def project_kernel(chips, offsets, parts, a_width, cut, carry, *refs):
    keep, theirs = refs[:2]
    chunks, refs = refs[2 : 2 + len(parts)], refs[2 + len(parts) :]
    out = refs[-1]
    rank = chunks[0].shape[0]
    width = keep.shape[2]
    if carry:
        a_sum, g_sum = refs[0][:, :rank], refs[0][:, rank:]
    else:
        a_sum = g_sum = jnp.zeros((out.shape[0], rank), jnp.float32)
    for offset, part, chunk in zip(offsets, parts, chunks):
        chip = chip_behind(offset, chips)

        def tokens(first, last):
            return jnp.concatenate([ref[chip, :, first:last] for ref in (keep, theirs)], axis=0)

        if part == 0:
            a_sum += dot(tokens(0, a_width), chunk[:, :a_width], NT)
            g_sum += dot(tokens(a_width, cut), chunk[:, a_width:], NT)
        else:
            g_sum += dot(tokens(cut, width), chunk[...], NT)
    out[:, :rank] = a_sum
    out[:, rank:] = g_sum


def project(tokens, chunks, a_width, cut, carry=None):
    chips, rows, width = tokens[0].shape
    offsets, parts, flat = zip(*chunks)
    rank = flat[0].shape[0]
    carried = () if carry is None else (carry,)
    columns = sum(x.shape[1] for x in flat)
    return pl.pallas_call(
        functools.partial(project_kernel, chips, offsets, parts, a_width, cut, carry is not None),
        out_shape=pltpu.VMEM((2 * rows, 2 * rank), jnp.float32),
        in_specs=[VMEM] * (2 + len(flat) + len(carried)),
        out_specs=VMEM,
        compiler_params=pltpu.CompilerParams(vmem_limit_bytes=16 * 2**20),
        cost_estimate=pl.CostEstimate(
            flops=4 * rows * rank * columns,
            bytes_accessed=(2 * rows + rank) * columns * 2,
            transcendentals=0,
        ),
    )(*held(pltpu.VMEM, *tokens, *flat, *carried))


def score_kernel(scale, conditioned, queries, out):
    width = conditioned.shape[2]
    total = jnp.zeros(out.shape, jnp.float32)
    for i in range(conditioned.shape[0]):
        total += dot(conditioned[i], queries[:, i * width : (i + 1) * width], NT)
    out[...] = total * scale


def score(conditioned, queries, scale):
    return pl.pallas_call(
        functools.partial(score_kernel, scale),
        out_shape=jax.ShapeDtypeStruct((conditioned.shape[1], queries.shape[0]), jnp.float32),
        in_specs=[VMEM] * 2,
        out_specs=VMEM,
        compiler_params=pltpu.CompilerParams(vmem_limit_bytes=16 * 2**20),
    )(*held(pltpu.VMEM, conditioned, queries))


def to_all(x, groups):
    copies = jnp.broadcast_to(x[None], (len(groups[0]),) + x.shape)
    return lax.all_to_all(copies, "dp", 0, 0, axis_index_groups=groups, tiled=True)


def local(activations, out_grads, in_basis, out_basis, preconditioner, queries):
    rows = activations.shape[0]
    a_width, rank = in_basis.shape
    n = activations.shape[1] // a_width
    chips = n // 2
    split = LEN // rows

    *own, send = start(activations, out_grads, in_basis.T, out_basis.T, chips)
    theirs = swap(send, 1, n)
    up, down = [own], [own]
    for _ in range(chips // 2 - 1):
        up.append([ring(x, 1, chips) for x in up[-1]])
        down.append([ring(x, -1, chips) for x in down[-1]])
    last = chips // 2 - 1
    far = (ring(up[last][0], 1, chips), ring(down[last][1], -1, chips))
    keep = keep_columns(activations, out_grads, chips)

    cut = own[0].shape[1]
    run = functools.partial(project, (keep, theirs), a_width=a_width, cut=cut)

    def both(block, offset):
        return [(offset, part, x) for part, x in enumerate(block)]

    near = both(own, 0)
    for i in range(1, last):
        near += both(up[i], i) + both(down[i], -i)
    total = run(near)
    total = run(both(up[last], last) + both(down[last], -last), carry=total)
    for part, x in enumerate(far):
        total = run([(chips // 2, part, x)], carry=total)
    theirs = swap(total, 1, n)
    total = (total + jnp.concatenate([theirs[rows:], theirs[:rows]], axis=0)).astype(jnp.bfloat16)

    raw = dot(total[:, rank:], total[:, :rank], TN)
    raw = (raw * (1.0 / math.sqrt(LEN))).reshape(-1, 128)
    planes = [[2 * i + c for i in range(chips)] for c in range(2)]
    raw = to_all(raw, planes)
    features = raw.reshape((-1, split // 2) + raw.shape[1:]).sum(axis=1)
    features = features.astype(jnp.bfloat16).reshape(-1, rank * rank)

    conditioned = dot(features, preconditioner, NT).astype(jnp.bfloat16)
    return score(to_all(conditioned, [list(range(n))]), queries, 1.0 / rank)


def local_gathered(activations, out_grads, in_basis, out_basis, preconditioner, queries):
    rows = activations.shape[0]
    rank = in_basis.shape[1]
    act_proj = jnp.dot(
        activations,
        lax.all_gather(in_basis, "dp", axis=0, tiled=True),
        preferred_element_type=jnp.float32,
    ).astype(jnp.bfloat16)
    grad_proj = jnp.dot(
        out_grads,
        lax.all_gather(out_basis, "dp", axis=0, tiled=True),
        preferred_element_type=jnp.float32,
    ).astype(jnp.bfloat16)
    raw = dot(grad_proj, act_proj, TN).reshape(1, rank * rank) * (1.0 / math.sqrt(LEN))
    gathered = lax.all_gather(raw, "dp", axis=0, tiled=True)
    features = gathered.reshape(-1, LEN // rows, rank * rank).sum(axis=1).astype(jnp.bfloat16)
    conditioned = dot(features, preconditioner, NT).astype(jnp.bfloat16)
    scores = dot(lax.all_gather(conditioned, "dp", axis=1, tiled=True), queries, NT)
    return scores * (1.0 / rank)


def power_of_two(x):
    return x > 0 and x & (x - 1) == 0


def solution(mesh):
    n = mesh.shape["dp"]

    def body(activations, out_grads, in_basis, out_basis, preconditioner, queries):
        aligned = all(x.shape[0] % 128 == 0 for x in (in_basis, out_basis, preconditioner))
        split = LEN // activations.shape[0]
        regular = aligned and n >= 8 and power_of_two(n) and power_of_two(split) and 4 <= split <= n
        form = local if regular else local_gathered
        return form(activations, out_grads, in_basis, out_basis, preconditioner, queries)

    return jax.shard_map(
        body,
        mesh=mesh,
        in_specs=(
            P(("parts", "dp"), None),
            P(("parts", "dp"), None),
            P("dp", None),
            P("dp", None),
            P("dp", None),
            P("dp", None),
        ),
        out_specs=P("parts", "dp"),
        check_vma=False,
    )
```

```python
import functools
import math

import jax
import jax.numpy as jnp
from jax import lax
from jax.experimental import pallas as pl
from jax.experimental.pallas import tpu as pltpu
from jax.sharding import PartitionSpec as P

LEN = 1024
NT = (((1,), (1,)), ((), ()))
TN = (((0,), (0,)), ((), ()))
VMEM = pl.BlockSpec(memory_space=pltpu.VMEM)
HBM = pl.BlockSpec(memory_space=pltpu.HBM)


def held(space, *arrays):
    return [pltpu.with_memory_space_constraint(x, space) for x in arrays]


def dot(a, b, dims):
    return lax.dot_general(a, b, dims, preferred_element_type=jnp.float32)


def chip_behind(offset, chips):
    chip = lax.axis_index("dp") >> 1
    z, y = chip >> 1, chip & 1
    place = (jnp.where(y == 0, z, chips - 1 - z) - offset) & (chips - 1)
    return jnp.where(place < chips // 2, 2 * place, 2 * (chips - 1 - place) + 1)


def ring(x, step, chips):
    half = chips // 2
    chip = [2 * p if p < half else 2 * (chips - 1 - p) + 1 for p in range(chips)]
    pairs = [
        (chip[p] * 2 + c, chip[(p + step) % chips] * 2 + 1 - c) for p in range(chips) for c in range(2)
    ]
    return lax.ppermute(x, "dp", pairs)


def swap(x, bit, n):
    return lax.ppermute(x, "dp", [(i, i ^ bit) for i in range(n)])


def odd(chip):
    return (chip ^ (chip >> 1)) & 1


def column_copies(chips, core, act, grad, out, sems):
    ring_of = core ^ odd(lax.axis_index("dp") >> 1)
    a_width = act.shape[1] // (2 * chips)
    g_width = grad.shape[1] // (2 * chips)
    copies = []
    for chip in range(chips):
        block = 2 * chip + (ring_of ^ odd(chip))
        for k, (ref, at, width) in enumerate(((act, 0, a_width), (grad, a_width, g_width))):
            columns = pl.ds(pl.multiple_of(block * width, 128), width)
            copies.append(
                pltpu.make_async_copy(
                    ref.at[:, columns], out.at[chip, :, pl.ds(at, width)], sems.at[chip, k]
                )
            )
    return copies


def run_copies(copies):
    for copy in copies:
        copy.start()
    for copy in copies:
        copy.wait()


def start_kernel(chips, act, grad, in_rows, out_rows, first, second, send, sems, send_sems):
    core = lax.axis_index("dp") & 1
    a_width = in_rows.shape[1]
    cut = first.shape[1]
    pairs = [
        (in_rows, first.at[:, pl.ds(0, a_width)]),
        (out_rows.at[:, pl.ds(0, cut - a_width)], first.at[:, pl.ds(a_width, cut - a_width)]),
        (out_rows.at[:, pl.ds(cut - a_width, second.shape[1])], second),
    ]
    copies = [pltpu.make_async_copy(*pair, sems.at[i]) for i, pair in enumerate(pairs)]
    run_copies(copies + column_copies(chips, 1 - core, act, grad, send, send_sems))


def start(act, grad, in_rows, out_rows, chips):
    rows = act.shape[0]
    rank, width = in_rows.shape[0], in_rows.shape[1] + out_rows.shape[1]
    cut = width // 256 * 128
    shapes = (rank, cut), (rank, width - cut), (chips, rows, width)
    return pl.pallas_call(
        functools.partial(start_kernel, chips),
        out_shape=[pltpu.VMEM(shape, act.dtype) for shape in shapes],
        in_specs=[HBM] * 4,
        out_specs=[VMEM] * 3,
        scratch_shapes=[pltpu.SemaphoreType.DMA((3,)), pltpu.SemaphoreType.DMA((chips, 2))],
        compiler_params=pltpu.CompilerParams(vmem_limit_bytes=16 * 2**20),
        cost_estimate=pl.CostEstimate(
            flops=0, bytes_accessed=4 * (rank + chips * rows) * width, transcendentals=0
        ),
    )(*held(pltpu.HBM, act, grad, in_rows, out_rows))


def keep_kernel(chips, act, grad, keep, sems):
    core = lax.axis_index("dp") & 1
    run_copies(column_copies(chips, core, act, grad, keep, sems))


def keep_columns(act, grad, chips):
    rows, width = act.shape[0], (act.shape[1] + grad.shape[1]) // (2 * chips)
    return pl.pallas_call(
        functools.partial(keep_kernel, chips),
        out_shape=pltpu.VMEM((chips, rows, width), act.dtype),
        in_specs=[HBM] * 2,
        out_specs=VMEM,
        scratch_shapes=[pltpu.SemaphoreType.DMA((chips, 2))],
        compiler_params=pltpu.CompilerParams(vmem_limit_bytes=16 * 2**20),
        cost_estimate=pl.CostEstimate(
            flops=0, bytes_accessed=4 * chips * rows * width, transcendentals=0
        ),
    )(*held(pltpu.HBM, act, grad))


def project_kernel(chips, offsets, parts, a_width, cut, carry, *refs):
    keep, theirs = refs[:2]
    chunks, refs = refs[2 : 2 + len(parts)], refs[2 + len(parts) :]
    out = refs[-1]
    rank = chunks[0].shape[0]
    width = keep.shape[2]
    if carry:
        a_sum, g_sum = refs[0][:, :rank], refs[0][:, rank:]
    else:
        a_sum = g_sum = jnp.zeros((out.shape[0], rank), jnp.float32)
    for offset, part, chunk in zip(offsets, parts, chunks):
        chip = chip_behind(offset, chips)

        def tokens(first, last):
            return jnp.concatenate([ref[chip, :, first:last] for ref in (keep, theirs)], axis=0)

        if part == 0:
            a_sum += dot(tokens(0, a_width), chunk[:, :a_width], NT)
            g_sum += dot(tokens(a_width, cut), chunk[:, a_width:], NT)
        else:
            g_sum += dot(tokens(cut, width), chunk[...], NT)
    out[:, :rank] = a_sum
    out[:, rank:] = g_sum


def project(tokens, chunks, a_width, cut, carry=None):
    chips, rows, width = tokens[0].shape
    offsets, parts, flat = zip(*chunks)
    rank = flat[0].shape[0]
    carried = () if carry is None else (carry,)
    columns = sum(x.shape[1] for x in flat)
    return pl.pallas_call(
        functools.partial(project_kernel, chips, offsets, parts, a_width, cut, carry is not None),
        out_shape=pltpu.VMEM((2 * rows, 2 * rank), jnp.float32),
        in_specs=[VMEM] * (2 + len(flat) + len(carried)),
        out_specs=VMEM,
        compiler_params=pltpu.CompilerParams(vmem_limit_bytes=16 * 2**20),
        cost_estimate=pl.CostEstimate(
            flops=4 * rows * rank * columns,
            bytes_accessed=(2 * rows + rank) * columns * 2,
            transcendentals=0,
        ),
    )(*held(pltpu.VMEM, *tokens, *flat, *carried))


def score_kernel(scale, conditioned, queries, out):
    width = conditioned.shape[2]
    total = jnp.zeros(out.shape, jnp.float32)
    for i in range(conditioned.shape[0]):
        total += dot(conditioned[i], queries[:, i * width : (i + 1) * width], NT)
    out[...] = total * scale


def score(conditioned, queries, scale):
    return pl.pallas_call(
        functools.partial(score_kernel, scale),
        out_shape=jax.ShapeDtypeStruct((conditioned.shape[1], queries.shape[0]), jnp.float32),
        in_specs=[VMEM] * 2,
        out_specs=VMEM,
        compiler_params=pltpu.CompilerParams(vmem_limit_bytes=16 * 2**20),
    )(*held(pltpu.VMEM, conditioned, queries))


def to_all(x, groups):
    copies = jnp.broadcast_to(x[None], (len(groups[0]),) + x.shape)
    return lax.all_to_all(copies, "dp", 0, 0, axis_index_groups=groups, tiled=True)


def local(activations, out_grads, in_basis, out_basis, preconditioner, queries):
    rows = activations.shape[0]
    a_width, rank = in_basis.shape
    n = activations.shape[1] // a_width
    chips = n // 2
    split = LEN // rows

    *own, send = start(activations, out_grads, in_basis.T, out_basis.T, chips)
    theirs = swap(send, 1, n)
    up, down = [own], [own]
    for _ in range(chips // 2 - 1):
        up.append([ring(x, 1, chips) for x in up[-1]])
        down.append([ring(x, -1, chips) for x in down[-1]])
    last = chips // 2 - 1
    far = (ring(up[last][0], 1, chips), ring(down[last][1], -1, chips))
    keep = keep_columns(activations, out_grads, chips)

    cut = own[0].shape[1]
    run = functools.partial(project, (keep, theirs), a_width=a_width, cut=cut)

    def both(block, offset):
        return [(offset, part, x) for part, x in enumerate(block)]

    near = both(own, 0)
    for i in range(1, last):
        near += both(up[i], i) + both(down[i], -i)
    total = run(near)
    total = run(both(up[last], last) + both(down[last], -last), carry=total)
    for part, x in enumerate(far):
        total = run([(chips // 2, part, x)], carry=total)
    theirs = swap(total, 1, n)
    total = (total + jnp.concatenate([theirs[rows:], theirs[:rows]], axis=0)).astype(jnp.bfloat16)

    raw = dot(total[:, rank:], total[:, :rank], TN)
    raw = (raw * (1.0 / math.sqrt(LEN))).reshape(-1, 128)
    features = (raw + sum(swap(raw, i, n) for i in range(2, split, 2))).astype(jnp.bfloat16)[None]
    bit = split
    while bit < n:
        pair = features, swap(features, bit, n)
        first = (lax.axis_index("dp") & bit) == 0
        features = jnp.where(first, jnp.concatenate(pair), jnp.concatenate(pair[::-1]))
        bit *= 2
    features = features.reshape(-1, rank * rank)

    conditioned = dot(features, preconditioner, NT).astype(jnp.bfloat16)
    return score(to_all(conditioned, [list(range(n))]), queries, 1.0 / rank)


def local_gathered(activations, out_grads, in_basis, out_basis, preconditioner, queries):
    rows = activations.shape[0]
    rank = in_basis.shape[1]
    act_proj = jnp.dot(
        activations,
        lax.all_gather(in_basis, "dp", axis=0, tiled=True),
        preferred_element_type=jnp.float32,
    ).astype(jnp.bfloat16)
    grad_proj = jnp.dot(
        out_grads,
        lax.all_gather(out_basis, "dp", axis=0, tiled=True),
        preferred_element_type=jnp.float32,
    ).astype(jnp.bfloat16)
    raw = dot(grad_proj, act_proj, TN).reshape(1, rank * rank) * (1.0 / math.sqrt(LEN))
    gathered = lax.all_gather(raw, "dp", axis=0, tiled=True)
    features = gathered.reshape(-1, LEN // rows, rank * rank).sum(axis=1).astype(jnp.bfloat16)
    conditioned = dot(features, preconditioner, NT).astype(jnp.bfloat16)
    scores = dot(lax.all_gather(conditioned, "dp", axis=1, tiled=True), queries, NT)
    return scores * (1.0 / rank)


def power_of_two(x):
    return x > 0 and x & (x - 1) == 0


def solution(mesh):
    n = mesh.shape["dp"]

    def body(activations, out_grads, in_basis, out_basis, preconditioner, queries):
        aligned = all(x.shape[0] % 128 == 0 for x in (in_basis, out_basis, preconditioner))
        split = LEN // activations.shape[0]
        regular = aligned and n >= 8 and power_of_two(n) and power_of_two(split) and 4 <= split <= n
        form = local if regular else local_gathered
        return form(activations, out_grads, in_basis, out_basis, preconditioner, queries)

    return jax.shard_map(
        body,
        mesh=mesh,
        in_specs=(
            P(("parts", "dp"), None),
            P(("parts", "dp"), None),
            P("dp", None),
            P("dp", None),
            P("dp", None),
            P("dp", None),
        ),
        out_specs=P("parts", "dp"),
        check_vma=False,
    )
```

```python
import functools
import math

import jax
import jax.numpy as jnp
from jax import lax
from jax.experimental import pallas as pl
from jax.experimental.pallas import tpu as pltpu
from jax.sharding import PartitionSpec as P

LEN = 1024
NT = (((1,), (1,)), ((), ()))
TN = (((0,), (0,)), ((), ()))
VMEM = pl.BlockSpec(memory_space=pltpu.VMEM)
HBM = pl.BlockSpec(memory_space=pltpu.HBM)


def held(space, *arrays):
    return [pltpu.with_memory_space_constraint(x, space) for x in arrays]


def dot(a, b, dims):
    return lax.dot_general(a, b, dims, preferred_element_type=jnp.float32)


def chip_behind(offset, chips):
    chip = lax.axis_index("dp") >> 1
    z, y = chip >> 1, chip & 1
    place = (jnp.where(y == 0, z, chips - 1 - z) - offset) & (chips - 1)
    return jnp.where(place < chips // 2, 2 * place, 2 * (chips - 1 - place) + 1)


def ring(x, step, chips):
    half = chips // 2
    chip = [2 * p if p < half else 2 * (chips - 1 - p) + 1 for p in range(chips)]
    pairs = [
        (chip[p] * 2 + c, chip[(p + step) % chips] * 2 + 1 - c) for p in range(chips) for c in range(2)
    ]
    return lax.ppermute(x, "dp", pairs)


def swap(x, bit, n):
    return lax.ppermute(x, "dp", [(i, i ^ bit) for i in range(n)])


def odd(chip):
    return (chip ^ (chip >> 1)) & 1


def column_copies(chip, ring_core, act, grad, out, sems, chips):
    block = 2 * chip + (ring_core ^ odd(lax.axis_index("dp") >> 1) ^ odd(chip))
    a_width, g_width = (x.shape[1] // (2 * chips) for x in (act, grad))
    return [
        pltpu.make_async_copy(
            ref.at[:, pl.ds(pl.multiple_of(block * width, 128), width)],
            out.at[:, pl.ds(at, width)],
            sems.at[k],
        )
        for k, (ref, at, width) in enumerate(((act, 0, a_width), (grad, a_width, g_width)))
    ]


def run_copies(copies):
    for copy in copies:
        copy.start()
    for copy in copies:
        copy.wait()


def start_kernel(chips, act, grad, in_rows, out_rows, first, second, send, sems, send_sems):
    core = lax.axis_index("dp") & 1
    a_width = in_rows.shape[1]
    cut = first.shape[1]
    pairs = [
        (in_rows, first.at[:, pl.ds(0, a_width)]),
        (out_rows.at[:, pl.ds(0, cut - a_width)], first.at[:, pl.ds(a_width, cut - a_width)]),
        (out_rows.at[:, pl.ds(cut - a_width, second.shape[1])], second),
    ]
    copies = [pltpu.make_async_copy(*pair, sems.at[i]) for i, pair in enumerate(pairs)]
    for chip in range(chips):
        copies += column_copies(chip, 1 - core, act, grad, send.at[chip], send_sems.at[chip], chips)
    run_copies(copies)


def start(act, grad, in_rows, out_rows, chips):
    rows = act.shape[0]
    rank, width = in_rows.shape[0], in_rows.shape[1] + out_rows.shape[1]
    cut = width // 256 * 128
    shapes = (rank, cut), (rank, width - cut), (chips, rows, width)
    return pl.pallas_call(
        functools.partial(start_kernel, chips),
        out_shape=[pltpu.VMEM(shape, act.dtype) for shape in shapes],
        in_specs=[HBM] * 4,
        out_specs=[VMEM] * 3,
        scratch_shapes=[pltpu.SemaphoreType.DMA((3,)), pltpu.SemaphoreType.DMA((chips, 2))],
        compiler_params=pltpu.CompilerParams(vmem_limit_bytes=16 * 2**20),
        cost_estimate=pl.CostEstimate(
            flops=0, bytes_accessed=4 * (rank + chips * rows) * width, transcendentals=0
        ),
    )(*held(pltpu.HBM, act, grad, in_rows, out_rows))


def add_products(sums, mine, theirs, part, chunk, a_width, cut):
    a_sum, g_sum = sums

    def tokens(first, last):
        return jnp.concatenate([ref[:, first:last] for ref in (mine, theirs)], axis=0)

    if part == 0:
        a_sum += dot(tokens(0, a_width), chunk[:, :a_width], NT)
        g_sum += dot(tokens(a_width, cut), chunk[:, a_width:], NT)
    else:
        g_sum += dot(tokens(cut, mine.shape[1]), chunk[...], NT)
    return a_sum, g_sum


def near_kernel(chips, offsets, later, a_width, act, grad, theirs, *refs):
    chunks, (out, rest, buf, sems) = refs[:-4], refs[-4:]
    rank, cut = chunks[0].shape
    core = lax.axis_index("dp") & 1
    where = [chip_behind(offset, chips) for offset in offsets + later]
    spaces = [buf.at[i] for i in range(len(offsets))] + [rest.at[i] for i in range(len(later))]
    copies = [
        column_copies(chip, core, act, grad, space, sems.at[i], chips)
        for i, (chip, space) in enumerate(zip(where, spaces))
    ]
    for pair in copies:
        for copy in pair:
            copy.start()
    sums = (jnp.zeros((out.shape[0], rank), jnp.float32),) * 2
    for i in range(len(offsets)):
        for copy in copies[i]:
            copy.wait()
        for part in range(2):
            chunk = chunks[2 * i + part]
            sums = add_products(sums, spaces[i], theirs.at[where[i]], part, chunk, a_width, cut)
    out[:, :rank], out[:, rank:] = sums
    for pair in copies[len(offsets) :]:
        for copy in pair:
            copy.wait()


def near_products(act, grad, theirs, blocks, offsets, later, a_width):
    chips, rows, width = theirs.shape
    rank = blocks[0][0].shape[0]
    flat = [x for block in blocks for x in block]
    count = len(offsets)
    return pl.pallas_call(
        functools.partial(near_kernel, chips, offsets, later, a_width),
        out_shape=(
            pltpu.VMEM((2 * rows, 2 * rank), jnp.float32),
            pltpu.VMEM((len(later), rows, width), act.dtype),
        ),
        in_specs=[HBM] * 2 + [VMEM] * (1 + len(flat)),
        out_specs=(VMEM, VMEM),
        scratch_shapes=[
            pltpu.VMEM((count, rows, width), act.dtype),
            pltpu.SemaphoreType.DMA((count + len(later), 2)),
        ],
        compiler_params=pltpu.CompilerParams(vmem_limit_bytes=16 * 2**20),
        cost_estimate=pl.CostEstimate(
            flops=4 * count * rows * rank * width,
            bytes_accessed=2 * (chips * rows + count * (rows + rank)) * width,
            transcendentals=0,
        ),
    )(*held(pltpu.HBM, act, grad), *held(pltpu.VMEM, theirs, *flat))


def later_kernel(chips, items, a_width, cut, rest, theirs, *refs):
    chunks, (carried, out) = refs[:-2], refs[-2:]
    rank = chunks[0].shape[0]
    sums = carried[:, :rank], carried[:, rank:]
    for (offset, place, part), chunk in zip(items, chunks):
        chip = chip_behind(offset, chips)
        sums = add_products(sums, rest.at[place], theirs.at[chip], part, chunk, a_width, cut)
    out[:, :rank], out[:, rank:] = sums


def later_products(rest, theirs, items, chunks, a_width, cut, total):
    chips, rows, _ = theirs.shape
    rank = chunks[0].shape[0]
    columns = sum(x.shape[1] for x in chunks)
    return pl.pallas_call(
        functools.partial(later_kernel, chips, items, a_width, cut),
        out_shape=pltpu.VMEM(total.shape, total.dtype),
        in_specs=[VMEM] * (3 + len(chunks)),
        out_specs=VMEM,
        compiler_params=pltpu.CompilerParams(vmem_limit_bytes=16 * 2**20),
        cost_estimate=pl.CostEstimate(
            flops=4 * rows * rank * columns,
            bytes_accessed=(2 * rows + rank) * columns * 2,
            transcendentals=0,
        ),
    )(*held(pltpu.VMEM, rest, theirs, *chunks, total))


def score_kernel(scale, conditioned, queries, out):
    width = conditioned.shape[2]
    total = jnp.zeros(out.shape, jnp.float32)
    for i in range(conditioned.shape[0]):
        total += dot(conditioned[i], queries[:, i * width : (i + 1) * width], NT)
    out[...] = total * scale


def score(conditioned, queries, scale):
    return pl.pallas_call(
        functools.partial(score_kernel, scale),
        out_shape=jax.ShapeDtypeStruct((conditioned.shape[1], queries.shape[0]), jnp.float32),
        in_specs=[VMEM] * 2,
        out_specs=VMEM,
        compiler_params=pltpu.CompilerParams(vmem_limit_bytes=16 * 2**20),
    )(*held(pltpu.VMEM, conditioned, queries))


def to_all(x, groups):
    copies = jnp.broadcast_to(x[None], (len(groups[0]),) + x.shape)
    return lax.all_to_all(copies, "dp", 0, 0, axis_index_groups=groups, tiled=True)


def local(activations, out_grads, in_basis, out_basis, preconditioner, queries):
    rows = activations.shape[0]
    a_width, rank = in_basis.shape
    n = activations.shape[1] // a_width
    chips = n // 2
    split = LEN // rows

    *own, send = start(activations, out_grads, in_basis.T, out_basis.T, chips)
    theirs = swap(send, 1, n)
    up, down = [own], [own]
    for _ in range(chips // 2 - 1):
        up.append([ring(x, 1, chips) for x in up[-1]])
        down.append([ring(x, -1, chips) for x in down[-1]])
    last = chips // 2 - 1
    far = (ring(up[last][0], 1, chips), ring(down[last][1], -1, chips))

    near, offsets = [own], [0]
    for i in range(1, last):
        near += [up[i], down[i]]
        offsets += [i, -i]
    later = [last, -last, chips // 2]
    total, rest = near_products(
        activations, out_grads, theirs, near, offsets, later, a_width
    )
    add = functools.partial(later_products, rest, theirs, a_width=a_width, cut=own[0].shape[1])
    items = [(offset, place, part) for place, offset in enumerate(later) for part in range(2)]
    total = add(items[:4], [*up[last], *down[last]], total=total)
    for item, chunk in zip(items[4:], far):
        total = add([item], [chunk], total=total)
    theirs = swap(total, 1, n)
    total = (total + jnp.concatenate([theirs[rows:], theirs[:rows]], axis=0)).astype(jnp.bfloat16)

    raw = dot(total[:, rank:], total[:, :rank], TN)
    raw = (raw * (1.0 / math.sqrt(LEN))).reshape(-1, 128)
    planes = [[2 * i + c for i in range(chips)] for c in range(2)]
    raw = to_all(raw, planes)
    features = raw.reshape((-1, split // 2) + raw.shape[1:]).sum(axis=1)
    features = features.astype(jnp.bfloat16).reshape(-1, rank * rank)

    conditioned = dot(features, preconditioner, NT).astype(jnp.bfloat16)
    return score(to_all(conditioned, [list(range(n))]), queries, 1.0 / rank)


def local_gathered(activations, out_grads, in_basis, out_basis, preconditioner, queries):
    rows = activations.shape[0]
    rank = in_basis.shape[1]
    act_proj = jnp.dot(
        activations,
        lax.all_gather(in_basis, "dp", axis=0, tiled=True),
        preferred_element_type=jnp.float32,
    ).astype(jnp.bfloat16)
    grad_proj = jnp.dot(
        out_grads,
        lax.all_gather(out_basis, "dp", axis=0, tiled=True),
        preferred_element_type=jnp.float32,
    ).astype(jnp.bfloat16)
    raw = dot(grad_proj, act_proj, TN).reshape(1, rank * rank) * (1.0 / math.sqrt(LEN))
    gathered = lax.all_gather(raw, "dp", axis=0, tiled=True)
    features = gathered.reshape(-1, LEN // rows, rank * rank).sum(axis=1).astype(jnp.bfloat16)
    conditioned = dot(features, preconditioner, NT).astype(jnp.bfloat16)
    scores = dot(lax.all_gather(conditioned, "dp", axis=1, tiled=True), queries, NT)
    return scores * (1.0 / rank)


def power_of_two(x):
    return x > 0 and x & (x - 1) == 0


def solution(mesh):
    n = mesh.shape["dp"]

    def body(activations, out_grads, in_basis, out_basis, preconditioner, queries):
        aligned = all(x.shape[0] % 128 == 0 for x in (in_basis, out_basis, preconditioner))
        split = LEN // activations.shape[0]
        regular = aligned and n >= 8 and power_of_two(n) and power_of_two(split) and 4 <= split <= n
        form = local if regular else local_gathered
        return form(activations, out_grads, in_basis, out_basis, preconditioner, queries)

    return jax.shard_map(
        body,
        mesh=mesh,
        in_specs=(
            P(("parts", "dp"), None),
            P(("parts", "dp"), None),
            P("dp", None),
            P("dp", None),
            P("dp", None),
            P("dp", None),
        ),
        out_specs=P("parts", "dp"),
        check_vma=False,
    )
```

```python
import functools
import math

import jax
import jax.numpy as jnp
from jax import lax
from jax.experimental import pallas as pl
from jax.experimental.pallas import tpu as pltpu
from jax.sharding import PartitionSpec as P

LEN = 1024
NT = (((1,), (1,)), ((), ()))
TN = (((0,), (0,)), ((), ()))
VMEM = pl.BlockSpec(memory_space=pltpu.VMEM)
HBM = pl.BlockSpec(memory_space=pltpu.HBM)


def held(space, *arrays):
    return [pltpu.with_memory_space_constraint(x, space) for x in arrays]


def dot(a, b, dims):
    return lax.dot_general(a, b, dims, preferred_element_type=jnp.float32)


def chip_behind(offset, chips):
    chip = lax.axis_index("dp") >> 1
    z, y = chip >> 1, chip & 1
    place = (jnp.where(y == 0, z, chips - 1 - z) - offset) & (chips - 1)
    return jnp.where(place < chips // 2, 2 * place, 2 * (chips - 1 - place) + 1)


def ring(x, step, chips):
    half = chips // 2
    chip = [2 * p if p < half else 2 * (chips - 1 - p) + 1 for p in range(chips)]
    pairs = [
        (chip[p] * 2 + c, chip[(p + step) % chips] * 2 + 1 - c) for p in range(chips) for c in range(2)
    ]
    return lax.ppermute(x, "dp", pairs)


def swap(x, bit, n):
    return lax.ppermute(x, "dp", [(i, i ^ bit) for i in range(n)])


def odd(chip):
    return (chip ^ (chip >> 1)) & 1


def column_copies(chip, ring_core, act, grad, out, sems, chips):
    block = 2 * chip + (ring_core ^ odd(lax.axis_index("dp") >> 1) ^ odd(chip))
    a_width, g_width = (x.shape[1] // (2 * chips) for x in (act, grad))
    return [
        pltpu.make_async_copy(
            ref.at[:, pl.ds(pl.multiple_of(block * width, 128), width)],
            out.at[:, pl.ds(at, width)],
            sems.at[k],
        )
        for k, (ref, at, width) in enumerate(((act, 0, a_width), (grad, a_width, g_width)))
    ]


def run_copies(copies):
    for copy in copies:
        copy.start()
    for copy in copies:
        copy.wait()


def start_kernel(chips, act, grad, in_rows, out_rows, first, second, send, sems, send_sems):
    core = lax.axis_index("dp") & 1
    a_width = in_rows.shape[1]
    cut = first.shape[1]
    pairs = [
        (in_rows, first.at[:, pl.ds(0, a_width)]),
        (out_rows.at[:, pl.ds(0, cut - a_width)], first.at[:, pl.ds(a_width, cut - a_width)]),
        (out_rows.at[:, pl.ds(cut - a_width, second.shape[1])], second),
    ]
    copies = [pltpu.make_async_copy(*pair, sems.at[i]) for i, pair in enumerate(pairs)]
    for chip in range(chips):
        copies += column_copies(chip, 1 - core, act, grad, send.at[chip], send_sems.at[chip], chips)
    run_copies(copies)


def start(act, grad, in_rows, out_rows, chips):
    rows = act.shape[0]
    rank, width = in_rows.shape[0], in_rows.shape[1] + out_rows.shape[1]
    cut = width // 256 * 128
    shapes = (rank, cut), (rank, width - cut), (chips, rows, width)
    return pl.pallas_call(
        functools.partial(start_kernel, chips),
        out_shape=[pltpu.VMEM(shape, act.dtype) for shape in shapes],
        in_specs=[HBM] * 4,
        out_specs=[VMEM] * 3,
        scratch_shapes=[pltpu.SemaphoreType.DMA((3,)), pltpu.SemaphoreType.DMA((chips, 2))],
        compiler_params=pltpu.CompilerParams(vmem_limit_bytes=16 * 2**20),
        cost_estimate=pl.CostEstimate(
            flops=0, bytes_accessed=4 * (rank + chips * rows) * width, transcendentals=0
        ),
    )(*held(pltpu.HBM, act, grad, in_rows, out_rows))


def add_products(sums, mine, theirs, part, chunk, a_width, cut):
    a_sum, g_sum = sums

    def tokens(first, last):
        return jnp.concatenate([ref[:, first:last] for ref in (mine, theirs)], axis=0)

    if part == 0:
        a_sum += dot(tokens(0, a_width), chunk[:, :a_width], NT)
        g_sum += dot(tokens(a_width, cut), chunk[:, a_width:], NT)
    else:
        g_sum += dot(tokens(cut, mine.shape[1]), chunk[...], NT)
    return a_sum, g_sum


def near_kernel(chips, offsets, later, a_width, act, grad, theirs, *refs):
    chunks, refs = refs[: 2 * len(offsets)], refs[2 * len(offsets) :]
    carried = None if later == [] else refs[0]
    out, *rest, buf, sems = refs[0 if later == [] else 1 :]
    rank, cut = chunks[0].shape
    core = lax.axis_index("dp") & 1
    where = [chip_behind(offset, chips) for offset in offsets + later]
    spaces = [buf.at[i] for i in range(len(offsets))] + [rest[0].at[i] for i in range(len(later))]
    copies = [
        column_copies(chip, core, act, grad, space, sems.at[i], chips)
        for i, (chip, space) in enumerate(zip(where, spaces))
    ]
    for pair in copies:
        for copy in pair:
            copy.start()
    if carried is None:
        sums = (jnp.zeros((out.shape[0], rank), jnp.float32),) * 2
    else:
        sums = carried[:, :rank], carried[:, rank:]
    for i in range(len(offsets)):
        for copy in copies[i]:
            copy.wait()
        for part in range(2):
            chunk = chunks[2 * i + part]
            sums = add_products(sums, spaces[i], theirs.at[where[i]], part, chunk, a_width, cut)
    out[:, :rank], out[:, rank:] = sums
    for pair in copies[len(offsets) :]:
        for copy in pair:
            copy.wait()


def near_products(act, grad, theirs, blocks, offsets, a_width, total=None, later=()):
    chips, rows, width = theirs.shape
    rank = blocks[0][0].shape[0]
    flat = [x for block in blocks for x in block]
    carried = [] if total is None else [total]
    count = len(offsets)
    out_shape = [pltpu.VMEM((2 * rows, 2 * rank), jnp.float32)]
    if later:
        out_shape.append(pltpu.VMEM((len(later), rows, width), act.dtype))
    return pl.pallas_call(
        functools.partial(near_kernel, chips, offsets, list(later), a_width),
        out_shape=out_shape,
        in_specs=[HBM] * 2 + [VMEM] * (1 + len(flat) + len(carried)),
        out_specs=[VMEM] * len(out_shape),
        scratch_shapes=[
            pltpu.VMEM((count, rows, width), act.dtype),
            pltpu.SemaphoreType.DMA((count + len(later), 2)),
        ],
        compiler_params=pltpu.CompilerParams(vmem_limit_bytes=16 * 2**20),
        cost_estimate=pl.CostEstimate(
            flops=4 * count * rows * rank * width,
            bytes_accessed=2 * ((count + len(later)) * rows + count * (rows + rank)) * width,
            transcendentals=0,
        ),
    )(*held(pltpu.HBM, act, grad), *held(pltpu.VMEM, theirs, *flat, *carried))


def later_kernel(chips, items, a_width, cut, rest, theirs, *refs):
    chunks, (carried, out) = refs[:-2], refs[-2:]
    rank = chunks[0].shape[0]
    sums = carried[:, :rank], carried[:, rank:]
    for (offset, place, part), chunk in zip(items, chunks):
        chip = chip_behind(offset, chips)
        sums = add_products(sums, rest.at[place], theirs.at[chip], part, chunk, a_width, cut)
    out[:, :rank], out[:, rank:] = sums


def later_products(rest, theirs, items, chunks, a_width, cut, total):
    chips, rows, _ = theirs.shape
    rank = chunks[0].shape[0]
    columns = sum(x.shape[1] for x in chunks)
    return pl.pallas_call(
        functools.partial(later_kernel, chips, items, a_width, cut),
        out_shape=pltpu.VMEM(total.shape, total.dtype),
        in_specs=[VMEM] * (3 + len(chunks)),
        out_specs=VMEM,
        compiler_params=pltpu.CompilerParams(vmem_limit_bytes=16 * 2**20),
        cost_estimate=pl.CostEstimate(
            flops=4 * rows * rank * columns,
            bytes_accessed=(2 * rows + rank) * columns * 2,
            transcendentals=0,
        ),
    )(*held(pltpu.VMEM, rest, theirs, *chunks, total))


def score_kernel(scale, conditioned, queries, out):
    width = conditioned.shape[2]
    total = jnp.zeros(out.shape, jnp.float32)
    for i in range(conditioned.shape[0]):
        total += dot(conditioned[i], queries[:, i * width : (i + 1) * width], NT)
    out[...] = total * scale


def score(conditioned, queries, scale):
    return pl.pallas_call(
        functools.partial(score_kernel, scale),
        out_shape=jax.ShapeDtypeStruct((conditioned.shape[1], queries.shape[0]), jnp.float32),
        in_specs=[VMEM] * 2,
        out_specs=VMEM,
        compiler_params=pltpu.CompilerParams(vmem_limit_bytes=16 * 2**20),
    )(*held(pltpu.VMEM, conditioned, queries))


def to_all(x, groups):
    copies = jnp.broadcast_to(x[None], (len(groups[0]),) + x.shape)
    return lax.all_to_all(copies, "dp", 0, 0, axis_index_groups=groups, tiled=True)


def local(activations, out_grads, in_basis, out_basis, preconditioner, queries):
    rows = activations.shape[0]
    a_width, rank = in_basis.shape
    n = activations.shape[1] // a_width
    chips = n // 2
    split = LEN // rows

    *own, send = start(activations, out_grads, in_basis.T, out_basis.T, chips)
    theirs = swap(send, 1, n)
    multiply = functools.partial(near_products, activations, out_grads, theirs, a_width=a_width)
    last = chips // 2 - 1
    up, down = [own], [own]
    for i in range(last):
        if i == last - 1:
            (total,) = multiply([own, up[1], down[1]], [0, 1, -1])
            total, up[i][0] = lax.optimization_barrier((total, up[i][0]))
        up.append([ring(x, 1, chips) for x in up[-1]])
        down.append([ring(x, -1, chips) for x in down[-1]])
    far = (ring(up[last][0], 1, chips), ring(down[last][1], -1, chips))

    near, offsets = [], []
    for i in range(2, last):
        near += [up[i], down[i]]
        offsets += [i, -i]
    later = [last, -last, chips // 2]
    total, rest = multiply(near, offsets, total=total, later=later)
    add = functools.partial(later_products, rest, theirs, a_width=a_width, cut=own[0].shape[1])
    items = [(offset, place, part) for place, offset in enumerate(later) for part in range(2)]
    total = add(items[:4], [*up[last], *down[last]], total=total)
    for item, chunk in zip(items[4:], far):
        total = add([item], [chunk], total=total)
    theirs = swap(total, 1, n)
    total = (total + jnp.concatenate([theirs[rows:], theirs[:rows]], axis=0)).astype(jnp.bfloat16)

    raw = dot(total[:, rank:], total[:, :rank], TN)
    raw = (raw * (1.0 / math.sqrt(LEN))).reshape(-1, 128)
    planes = [[2 * i + c for i in range(chips)] for c in range(2)]
    raw = to_all(raw, planes)
    features = raw.reshape((-1, split // 2) + raw.shape[1:]).sum(axis=1)
    features = features.astype(jnp.bfloat16).reshape(-1, rank * rank)

    conditioned = dot(features, preconditioner, NT).astype(jnp.bfloat16)
    return score(to_all(conditioned, [list(range(n))]), queries, 1.0 / rank)


def local_gathered(activations, out_grads, in_basis, out_basis, preconditioner, queries):
    rows = activations.shape[0]
    rank = in_basis.shape[1]
    act_proj = jnp.dot(
        activations,
        lax.all_gather(in_basis, "dp", axis=0, tiled=True),
        preferred_element_type=jnp.float32,
    ).astype(jnp.bfloat16)
    grad_proj = jnp.dot(
        out_grads,
        lax.all_gather(out_basis, "dp", axis=0, tiled=True),
        preferred_element_type=jnp.float32,
    ).astype(jnp.bfloat16)
    raw = dot(grad_proj, act_proj, TN).reshape(1, rank * rank) * (1.0 / math.sqrt(LEN))
    gathered = lax.all_gather(raw, "dp", axis=0, tiled=True)
    features = gathered.reshape(-1, LEN // rows, rank * rank).sum(axis=1).astype(jnp.bfloat16)
    conditioned = dot(features, preconditioner, NT).astype(jnp.bfloat16)
    scores = dot(lax.all_gather(conditioned, "dp", axis=1, tiled=True), queries, NT)
    return scores * (1.0 / rank)


def power_of_two(x):
    return x > 0 and x & (x - 1) == 0


def solution(mesh):
    n = mesh.shape["dp"]

    def body(activations, out_grads, in_basis, out_basis, preconditioner, queries):
        aligned = all(x.shape[0] % 128 == 0 for x in (in_basis, out_basis, preconditioner))
        split = LEN // activations.shape[0]
        regular = aligned and n >= 16 and power_of_two(n) and power_of_two(split) and 4 <= split <= n
        form = local if regular else local_gathered
        return form(activations, out_grads, in_basis, out_basis, preconditioner, queries)

    return jax.shard_map(
        body,
        mesh=mesh,
        in_specs=(
            P(("parts", "dp"), None),
            P(("parts", "dp"), None),
            P("dp", None),
            P("dp", None),
            P("dp", None),
            P("dp", None),
        ),
        out_specs=P("parts", "dp"),
        check_vma=False,
    )
```

```python
import functools
import math

import jax
import jax.numpy as jnp
from jax import lax
from jax.experimental import pallas as pl
from jax.experimental.pallas import tpu as pltpu
from jax.sharding import PartitionSpec as P

LEN = 1024
NT = (((1,), (1,)), ((), ()))
TN = (((0,), (0,)), ((), ()))
VMEM = pl.BlockSpec(memory_space=pltpu.VMEM)
HBM = pl.BlockSpec(memory_space=pltpu.HBM)


def held(space, *arrays):
    return [pltpu.with_memory_space_constraint(x, space) for x in arrays]


def dot(a, b, dims):
    return lax.dot_general(a, b, dims, preferred_element_type=jnp.float32)


def chip_behind(offset, chips):
    chip = lax.axis_index("dp") >> 1
    z, y = chip >> 1, chip & 1
    place = (jnp.where(y == 0, z, chips - 1 - z) - offset) & (chips - 1)
    return jnp.where(place < chips // 2, 2 * place, 2 * (chips - 1 - place) + 1)


def ring(x, step, chips):
    half = chips // 2
    chip = [2 * p if p < half else 2 * (chips - 1 - p) + 1 for p in range(chips)]
    pairs = [
        (chip[p] * 2 + c, chip[(p + step) % chips] * 2 + 1 - c) for p in range(chips) for c in range(2)
    ]
    return lax.ppermute(x, "dp", pairs)


def swap(x, bit, n):
    return lax.ppermute(x, "dp", [(i, i ^ bit) for i in range(n)])


def odd(chip):
    return (chip ^ (chip >> 1)) & 1


def column_copies(chip, ring_core, act, grad, out, sems, chips):
    block = 2 * chip + (ring_core ^ odd(lax.axis_index("dp") >> 1) ^ odd(chip))
    a_width, g_width = (x.shape[1] // (2 * chips) for x in (act, grad))
    return [
        pltpu.make_async_copy(
            ref.at[:, pl.ds(pl.multiple_of(block * width, 128), width)],
            out.at[:, pl.ds(at, width)],
            sems.at[k],
        )
        for k, (ref, at, width) in enumerate(((act, 0, a_width), (grad, a_width, g_width)))
    ]


def run_copies(copies):
    for copy in copies:
        copy.start()
    for copy in copies:
        copy.wait()


def start_kernel(chips, act, grad, in_rows, out_rows, first, second, send, sems, send_sems):
    core = lax.axis_index("dp") & 1
    a_width = in_rows.shape[1]
    cut = first.shape[1]
    pairs = [
        (in_rows, first.at[:, pl.ds(0, a_width)]),
        (out_rows.at[:, pl.ds(0, cut - a_width)], first.at[:, pl.ds(a_width, cut - a_width)]),
        (out_rows.at[:, pl.ds(cut - a_width, second.shape[1])], second),
    ]
    copies = [pltpu.make_async_copy(*pair, sems.at[i]) for i, pair in enumerate(pairs)]
    for chip in range(chips):
        copies += column_copies(chip, 1 - core, act, grad, send.at[chip], send_sems.at[chip], chips)
    run_copies(copies)


def start(act, grad, in_rows, out_rows, chips):
    rows = act.shape[0]
    rank, width = in_rows.shape[0], in_rows.shape[1] + out_rows.shape[1]
    cut = width // 256 * 128
    shapes = (rank, cut), (rank, width - cut), (chips, rows, width)
    return pl.pallas_call(
        functools.partial(start_kernel, chips),
        out_shape=[pltpu.VMEM(shape, act.dtype) for shape in shapes],
        in_specs=[HBM] * 4,
        out_specs=[VMEM] * 3,
        scratch_shapes=[pltpu.SemaphoreType.DMA((3,)), pltpu.SemaphoreType.DMA((chips, 2))],
        compiler_params=pltpu.CompilerParams(vmem_limit_bytes=16 * 2**20),
        cost_estimate=pl.CostEstimate(
            flops=0, bytes_accessed=4 * (rank + chips * rows) * width, transcendentals=0
        ),
    )(*held(pltpu.HBM, act, grad, in_rows, out_rows))


def add_products(sums, mine, theirs, part, chunk, a_width, cut):
    a_sum, g_sum = sums

    def tokens(first, last):
        return jnp.concatenate([ref[:, first:last] for ref in (mine, theirs)], axis=0)

    if part == 0:
        a_sum += dot(tokens(0, a_width), chunk[:, :a_width], NT)
        g_sum += dot(tokens(a_width, cut), chunk[:, a_width:], NT)
    else:
        g_sum += dot(tokens(cut, mine.shape[1]), chunk[...], NT)
    return a_sum, g_sum


def near_kernel(chips, offsets, later, a_width, act, grad, theirs, *refs):
    chunks, (out, rest, buf, sems) = refs[:-4], refs[-4:]
    rank, cut = chunks[0].shape
    core = lax.axis_index("dp") & 1
    where = [chip_behind(offset, chips) for offset in offsets + later]
    spaces = [buf.at[i] for i in range(len(offsets))] + [rest.at[i] for i in range(len(later))]
    copies = [
        column_copies(chip, core, act, grad, space, sems.at[i], chips)
        for i, (chip, space) in enumerate(zip(where, spaces))
    ]
    for pair in copies[:3]:
        for copy in pair:
            copy.start()
    sums = (jnp.zeros((out.shape[0], rank), jnp.float32),) * 2
    for i in range(len(copies)):
        for copy in copies[i]:
            copy.wait()
        for copy in sum(copies[i + 3 : i + 4], []):
            copy.start()
        for part in range(2) if i < len(offsets) else ():
            chunk = chunks[2 * i + part]
            sums = add_products(sums, spaces[i], theirs.at[where[i]], part, chunk, a_width, cut)
    out[:, :rank], out[:, rank:] = sums


def near_products(act, grad, theirs, blocks, offsets, later, a_width):
    chips, rows, width = theirs.shape
    rank = blocks[0][0].shape[0]
    flat = [x for block in blocks for x in block]
    count = len(offsets)
    return pl.pallas_call(
        functools.partial(near_kernel, chips, offsets, later, a_width),
        out_shape=(
            pltpu.VMEM((2 * rows, 2 * rank), jnp.float32),
            pltpu.VMEM((len(later), rows, width), act.dtype),
        ),
        in_specs=[HBM] * 2 + [VMEM] * (1 + len(flat)),
        out_specs=(VMEM, VMEM),
        scratch_shapes=[
            pltpu.VMEM((count, rows, width), act.dtype),
            pltpu.SemaphoreType.DMA((count + len(later), 2)),
        ],
        compiler_params=pltpu.CompilerParams(vmem_limit_bytes=16 * 2**20),
        cost_estimate=pl.CostEstimate(
            flops=4 * count * rows * rank * width,
            bytes_accessed=2 * (chips * rows + count * (rows + rank)) * width,
            transcendentals=0,
        ),
    )(*held(pltpu.HBM, act, grad), *held(pltpu.VMEM, theirs, *flat))


def later_kernel(chips, items, a_width, cut, rest, theirs, *refs):
    chunks, (carried, out) = refs[:-2], refs[-2:]
    rank = chunks[0].shape[0]
    sums = carried[:, :rank], carried[:, rank:]
    for (offset, place, part), chunk in zip(items, chunks):
        chip = chip_behind(offset, chips)
        sums = add_products(sums, rest.at[place], theirs.at[chip], part, chunk, a_width, cut)
    out[:, :rank], out[:, rank:] = sums


def later_products(rest, theirs, items, chunks, a_width, cut, total):
    chips, rows, _ = theirs.shape
    rank = chunks[0].shape[0]
    columns = sum(x.shape[1] for x in chunks)
    return pl.pallas_call(
        functools.partial(later_kernel, chips, items, a_width, cut),
        out_shape=pltpu.VMEM(total.shape, total.dtype),
        in_specs=[VMEM] * (3 + len(chunks)),
        out_specs=VMEM,
        compiler_params=pltpu.CompilerParams(vmem_limit_bytes=16 * 2**20),
        cost_estimate=pl.CostEstimate(
            flops=4 * rows * rank * columns,
            bytes_accessed=(2 * rows + rank) * columns * 2,
            transcendentals=0,
        ),
    )(*held(pltpu.VMEM, rest, theirs, *chunks, total))


def score_kernel(scale, conditioned, queries, out):
    width = conditioned.shape[2]
    total = jnp.zeros(out.shape, jnp.float32)
    for i in range(conditioned.shape[0]):
        total += dot(conditioned[i], queries[:, i * width : (i + 1) * width], NT)
    out[...] = total * scale


def score(conditioned, queries, scale):
    return pl.pallas_call(
        functools.partial(score_kernel, scale),
        out_shape=jax.ShapeDtypeStruct((conditioned.shape[1], queries.shape[0]), jnp.float32),
        in_specs=[VMEM] * 2,
        out_specs=VMEM,
        compiler_params=pltpu.CompilerParams(vmem_limit_bytes=16 * 2**20),
    )(*held(pltpu.VMEM, conditioned, queries))


def to_all(x, groups):
    copies = jnp.broadcast_to(x[None], (len(groups[0]),) + x.shape)
    return lax.all_to_all(copies, "dp", 0, 0, axis_index_groups=groups, tiled=True)


def local(activations, out_grads, in_basis, out_basis, preconditioner, queries):
    rows = activations.shape[0]
    a_width, rank = in_basis.shape
    n = activations.shape[1] // a_width
    chips = n // 2
    split = LEN // rows

    *own, send = start(activations, out_grads, in_basis.T, out_basis.T, chips)
    theirs = swap(send, 1, n)
    up, down = [own], [own]
    for _ in range(chips // 2 - 1):
        up.append([ring(x, 1, chips) for x in up[-1]])
        down.append([ring(x, -1, chips) for x in down[-1]])
    last = chips // 2 - 1
    far = (ring(up[last][0], 1, chips), ring(down[last][1], -1, chips))

    near, offsets = [own], [0]
    for i in range(1, last):
        near += [up[i], down[i]]
        offsets += [i, -i]
    later = [last, -last, chips // 2]
    total, rest = near_products(
        activations, out_grads, theirs, near, offsets, later, a_width
    )
    add = functools.partial(later_products, rest, theirs, a_width=a_width, cut=own[0].shape[1])
    items = [(offset, place, part) for place, offset in enumerate(later) for part in range(2)]
    total = add(items[:4], [*up[last], *down[last]], total=total)
    for item, chunk in zip(items[4:], far):
        total = add([item], [chunk], total=total)
    theirs = swap(total, 1, n)
    total = (total + jnp.concatenate([theirs[rows:], theirs[:rows]], axis=0)).astype(jnp.bfloat16)

    raw = dot(total[:, rank:], total[:, :rank], TN)
    raw = (raw * (1.0 / math.sqrt(LEN))).reshape(-1, 128)
    planes = [[2 * i + c for i in range(chips)] for c in range(2)]
    raw = to_all(raw, planes)
    features = raw.reshape((-1, split // 2) + raw.shape[1:]).sum(axis=1)
    features = features.astype(jnp.bfloat16).reshape(-1, rank * rank)

    conditioned = dot(features, preconditioner, NT).astype(jnp.bfloat16)
    return score(to_all(conditioned, [list(range(n))]), queries, 1.0 / rank)


def local_gathered(activations, out_grads, in_basis, out_basis, preconditioner, queries):
    rows = activations.shape[0]
    rank = in_basis.shape[1]
    act_proj = jnp.dot(
        activations,
        lax.all_gather(in_basis, "dp", axis=0, tiled=True),
        preferred_element_type=jnp.float32,
    ).astype(jnp.bfloat16)
    grad_proj = jnp.dot(
        out_grads,
        lax.all_gather(out_basis, "dp", axis=0, tiled=True),
        preferred_element_type=jnp.float32,
    ).astype(jnp.bfloat16)
    raw = dot(grad_proj, act_proj, TN).reshape(1, rank * rank) * (1.0 / math.sqrt(LEN))
    gathered = lax.all_gather(raw, "dp", axis=0, tiled=True)
    features = gathered.reshape(-1, LEN // rows, rank * rank).sum(axis=1).astype(jnp.bfloat16)
    conditioned = dot(features, preconditioner, NT).astype(jnp.bfloat16)
    scores = dot(lax.all_gather(conditioned, "dp", axis=1, tiled=True), queries, NT)
    return scores * (1.0 / rank)


def power_of_two(x):
    return x > 0 and x & (x - 1) == 0


def solution(mesh):
    n = mesh.shape["dp"]

    def body(activations, out_grads, in_basis, out_basis, preconditioner, queries):
        aligned = all(x.shape[0] % 128 == 0 for x in (in_basis, out_basis, preconditioner))
        split = LEN // activations.shape[0]
        regular = aligned and n >= 8 and power_of_two(n) and power_of_two(split) and 4 <= split <= n
        form = local if regular else local_gathered
        return form(activations, out_grads, in_basis, out_basis, preconditioner, queries)

    return jax.shard_map(
        body,
        mesh=mesh,
        in_specs=(
            P(("parts", "dp"), None),
            P(("parts", "dp"), None),
            P("dp", None),
            P("dp", None),
            P("dp", None),
            P("dp", None),
        ),
        out_specs=P("parts", "dp"),
        check_vma=False,
    )
```

```python
import functools
import math

import jax
import jax.numpy as jnp
from jax import lax
from jax.experimental import pallas as pl
from jax.experimental.pallas import tpu as pltpu
from jax.sharding import PartitionSpec as P

LEN = 1024
NT = (((1,), (1,)), ((), ()))
TN = (((0,), (0,)), ((), ()))
VMEM = pl.BlockSpec(memory_space=pltpu.VMEM)
HBM = pl.BlockSpec(memory_space=pltpu.HBM)


def held(space, *arrays):
    return [pltpu.with_memory_space_constraint(x, space) for x in arrays]


def dot(a, b, dims):
    return lax.dot_general(a, b, dims, preferred_element_type=jnp.float32)


def chip_behind(offset, chips):
    chip = lax.axis_index("dp") >> 1
    z, y = chip >> 1, chip & 1
    place = (jnp.where(y == 0, z, chips - 1 - z) - offset) & (chips - 1)
    return jnp.where(place < chips // 2, 2 * place, 2 * (chips - 1 - place) + 1)


def ring(x, step, chips):
    half = chips // 2
    chip = [2 * p if p < half else 2 * (chips - 1 - p) + 1 for p in range(chips)]
    pairs = [
        (chip[p] * 2 + c, chip[(p + step) % chips] * 2 + 1 - c) for p in range(chips) for c in range(2)
    ]
    return lax.ppermute(x, "dp", pairs)


def swap(x, bit, n):
    return lax.ppermute(x, "dp", [(i, i ^ bit) for i in range(n)])


def odd(chip):
    return (chip ^ (chip >> 1)) & 1


def column_copies(chip, ring_core, act, grad, out, sems, chips):
    block = 2 * chip + (ring_core ^ odd(lax.axis_index("dp") >> 1) ^ odd(chip))
    a_width, g_width = (x.shape[1] // (2 * chips) for x in (act, grad))
    return [
        pltpu.make_async_copy(
            ref.at[:, pl.ds(pl.multiple_of(block * width, 128), width)],
            out.at[:, pl.ds(at, width)],
            sems.at[k],
        )
        for k, (ref, at, width) in enumerate(((act, 0, a_width), (grad, a_width, g_width)))
    ]


def run_copies(copies):
    for copy in copies:
        copy.start()
    for copy in copies:
        copy.wait()


def start_kernel(chips, act, grad, in_rows, out_rows, first, second, send, sems, send_sems):
    core = lax.axis_index("dp") & 1
    a_width = in_rows.shape[1]
    cut = first.shape[1]
    pairs = [
        (in_rows, first.at[:, pl.ds(0, a_width)]),
        (out_rows.at[:, pl.ds(0, cut - a_width)], first.at[:, pl.ds(a_width, cut - a_width)]),
        (out_rows.at[:, pl.ds(cut - a_width, second.shape[1])], second),
    ]
    copies = [pltpu.make_async_copy(*pair, sems.at[i]) for i, pair in enumerate(pairs)]
    for chip in range(chips):
        copies += column_copies(chip, 1 - core, act, grad, send.at[chip], send_sems.at[chip], chips)
    run_copies(copies)


def start(act, grad, in_rows, out_rows, chips):
    rows = act.shape[0]
    rank, width = in_rows.shape[0], in_rows.shape[1] + out_rows.shape[1]
    cut = width // 256 * 128
    shapes = (rank, cut), (rank, width - cut), (chips, rows, width)
    return pl.pallas_call(
        functools.partial(start_kernel, chips),
        out_shape=[pltpu.VMEM(shape, act.dtype) for shape in shapes],
        in_specs=[HBM] * 4,
        out_specs=[VMEM] * 3,
        scratch_shapes=[pltpu.SemaphoreType.DMA((3,)), pltpu.SemaphoreType.DMA((chips, 2))],
        compiler_params=pltpu.CompilerParams(vmem_limit_bytes=16 * 2**20),
        cost_estimate=pl.CostEstimate(
            flops=0, bytes_accessed=4 * (rank + chips * rows) * width, transcendentals=0
        ),
    )(*held(pltpu.HBM, act, grad, in_rows, out_rows))


def project_kernel(chips, items, a_width, cut, carry, act, grad, theirs, *refs):
    chunks, refs = refs[: len(items)], refs[len(items) :]
    out = refs[-1]
    rank = chunks[0].shape[0]
    g_width = theirs.shape[2] - a_width
    me = lax.axis_index("dp")
    if carry:
        a_sum, g_sum = refs[0][:, :rank], refs[0][:, rank:]
    else:
        a_sum = g_sum = jnp.zeros((out.shape[0], rank), jnp.float32)
    for (offset, part), chunk in zip(items, chunks):
        chip = chip_behind(offset, chips)
        block = 2 * chip + ((me & 1) ^ odd(me >> 1) ^ odd(chip))

        def tokens(ref, width, skip, first, last):
            at = pl.multiple_of(block * width, 128) + (first - skip)
            return jnp.concatenate(
                [ref[:, pl.ds(at, last - first)], theirs[chip, :, first:last]], axis=0
            )

        if part == 0:
            a_sum += dot(tokens(act, a_width, 0, 0, a_width), chunk[:, :a_width], NT)
            g_sum += dot(tokens(grad, g_width, a_width, a_width, cut), chunk[:, a_width:], NT)
        else:
            g_sum += dot(tokens(grad, g_width, a_width, cut, theirs.shape[2]), chunk[...], NT)
    out[:, :rank] = a_sum
    out[:, rank:] = g_sum


def project(tokens, items, chunks, a_width, cut, total=None):
    chips, rows, _ = tokens[2].shape
    rank = chunks[0].shape[0]
    columns = sum(x.shape[1] for x in chunks)
    carried = [] if total is None else [total]
    return pl.pallas_call(
        functools.partial(project_kernel, chips, items, a_width, cut, total is not None),
        out_shape=pltpu.VMEM((2 * rows, 2 * rank), jnp.float32),
        in_specs=[VMEM] * (3 + len(chunks) + len(carried)),
        out_specs=VMEM,
        compiler_params=pltpu.CompilerParams(vmem_limit_bytes=16 * 2**20),
        cost_estimate=pl.CostEstimate(
            flops=4 * rows * rank * columns,
            bytes_accessed=(2 * rows + rank) * columns * 2,
            transcendentals=0,
        ),
    )(*held(pltpu.VMEM, *tokens, *chunks, *carried))


def score_kernel(scale, conditioned, queries, out):
    width = conditioned.shape[2]
    total = jnp.zeros(out.shape, jnp.float32)
    for i in range(conditioned.shape[0]):
        total += dot(conditioned[i], queries[:, i * width : (i + 1) * width], NT)
    out[...] = total * scale


def score(conditioned, queries, scale):
    return pl.pallas_call(
        functools.partial(score_kernel, scale),
        out_shape=jax.ShapeDtypeStruct((conditioned.shape[1], queries.shape[0]), jnp.float32),
        in_specs=[VMEM] * 2,
        out_specs=VMEM,
        compiler_params=pltpu.CompilerParams(vmem_limit_bytes=16 * 2**20),
    )(*held(pltpu.VMEM, conditioned, queries))


def to_all(x, groups):
    copies = jnp.broadcast_to(x[None], (len(groups[0]),) + x.shape)
    return lax.all_to_all(copies, "dp", 0, 0, axis_index_groups=groups, tiled=True)


def local(activations, out_grads, in_basis, out_basis, preconditioner, queries):
    rows = activations.shape[0]
    a_width, rank = in_basis.shape
    n = activations.shape[1] // a_width
    chips = n // 2
    split = LEN // rows

    *own, send = start(activations, out_grads, in_basis.T, out_basis.T, chips)
    theirs = swap(send, 1, n)
    up, down = [own], [own]
    for _ in range(chips // 2 - 1):
        up.append([ring(x, 1, chips) for x in up[-1]])
        down.append([ring(x, -1, chips) for x in down[-1]])
    last = chips // 2 - 1
    far = (ring(up[last][0], 1, chips), ring(down[last][1], -1, chips))

    tokens = activations, out_grads, theirs
    run = functools.partial(project, tokens, a_width=a_width, cut=own[0].shape[1])
    near, items = [*own], [(0, 0), (0, 1)]
    for i in range(1, last):
        near += [*up[i], *down[i]]
        items += [(offset, part) for offset in (i, -i) for part in range(2)]
    total = run(items, near)
    items = [(offset, part) for offset in (last, -last) for part in range(2)]
    total = run(items, [*up[last], *down[last]], total=total)
    for part, chunk in enumerate(far):
        total = run([(chips // 2, part)], [chunk], total=total)
    theirs = swap(total, 1, n)
    total = (total + jnp.concatenate([theirs[rows:], theirs[:rows]], axis=0)).astype(jnp.bfloat16)

    raw = dot(total[:, rank:], total[:, :rank], TN)
    raw = (raw * (1.0 / math.sqrt(LEN))).reshape(-1, 128)
    planes = [[2 * i + c for i in range(chips)] for c in range(2)]
    raw = to_all(raw, planes)
    features = raw.reshape((-1, split // 2) + raw.shape[1:]).sum(axis=1)
    features = features.astype(jnp.bfloat16).reshape(-1, rank * rank)

    conditioned = dot(features, preconditioner, NT).astype(jnp.bfloat16)
    return score(to_all(conditioned, [list(range(n))]), queries, 1.0 / rank)


def local_gathered(activations, out_grads, in_basis, out_basis, preconditioner, queries):
    rows = activations.shape[0]
    rank = in_basis.shape[1]
    act_proj = jnp.dot(
        activations,
        lax.all_gather(in_basis, "dp", axis=0, tiled=True),
        preferred_element_type=jnp.float32,
    ).astype(jnp.bfloat16)
    grad_proj = jnp.dot(
        out_grads,
        lax.all_gather(out_basis, "dp", axis=0, tiled=True),
        preferred_element_type=jnp.float32,
    ).astype(jnp.bfloat16)
    raw = dot(grad_proj, act_proj, TN).reshape(1, rank * rank) * (1.0 / math.sqrt(LEN))
    gathered = lax.all_gather(raw, "dp", axis=0, tiled=True)
    features = gathered.reshape(-1, LEN // rows, rank * rank).sum(axis=1).astype(jnp.bfloat16)
    conditioned = dot(features, preconditioner, NT).astype(jnp.bfloat16)
    scores = dot(lax.all_gather(conditioned, "dp", axis=1, tiled=True), queries, NT)
    return scores * (1.0 / rank)


def power_of_two(x):
    return x > 0 and x & (x - 1) == 0


def solution(mesh):
    n = mesh.shape["dp"]

    def body(activations, out_grads, in_basis, out_basis, preconditioner, queries):
        aligned = all(x.shape[0] % 128 == 0 for x in (in_basis, out_basis, preconditioner))
        split = LEN // activations.shape[0]
        regular = aligned and n >= 8 and power_of_two(n) and power_of_two(split) and 4 <= split <= n
        form = local if regular else local_gathered
        return form(activations, out_grads, in_basis, out_basis, preconditioner, queries)

    return jax.shard_map(
        body,
        mesh=mesh,
        in_specs=(
            P(("parts", "dp"), None),
            P(("parts", "dp"), None),
            P("dp", None),
            P("dp", None),
            P("dp", None),
            P("dp", None),
        ),
        out_specs=P("parts", "dp"),
        check_vma=False,
    )
```

```python
import functools
import math

import jax
import jax.numpy as jnp
from jax import lax
from jax.experimental import pallas as pl
from jax.experimental.pallas import tpu as pltpu
from jax.sharding import PartitionSpec as P

LEN = 1024
NT = (((1,), (1,)), ((), ()))
TN = (((0,), (0,)), ((), ()))
VMEM = pl.BlockSpec(memory_space=pltpu.VMEM)
HBM = pl.BlockSpec(memory_space=pltpu.HBM)


def held(space, *arrays):
    return [pltpu.with_memory_space_constraint(x, space) for x in arrays]


def dot(a, b, dims):
    return lax.dot_general(a, b, dims, preferred_element_type=jnp.float32)


def chip_behind(offset, chips):
    chip = lax.axis_index("dp") >> 1
    z, y = chip >> 1, chip & 1
    place = (jnp.where(y == 0, z, chips - 1 - z) - offset) & (chips - 1)
    return jnp.where(place < chips // 2, 2 * place, 2 * (chips - 1 - place) + 1)


def ring(x, step, chips):
    half = chips // 2
    chip = [2 * p if p < half else 2 * (chips - 1 - p) + 1 for p in range(chips)]
    pairs = [
        (chip[p] * 2 + c, chip[(p + step) % chips] * 2 + 1 - c) for p in range(chips) for c in range(2)
    ]
    return lax.ppermute(x, "dp", pairs)


def swap(x, bit, n):
    return lax.ppermute(x, "dp", [(i, i ^ bit) for i in range(n)])


def odd(chip):
    return (chip ^ (chip >> 1)) & 1


def column_copies(chip, ring_core, act, grad, out, sems, chips):
    block = 2 * chip + (ring_core ^ odd(lax.axis_index("dp") >> 1) ^ odd(chip))
    a_width, g_width = (x.shape[1] // (2 * chips) for x in (act, grad))
    return [
        pltpu.make_async_copy(
            ref.at[:, pl.ds(pl.multiple_of(block * width, 128), width)],
            out.at[:, pl.ds(at, width)],
            sems.at[k],
        )
        for k, (ref, at, width) in enumerate(((act, 0, a_width), (grad, a_width, g_width)))
    ]


def run_copies(copies):
    for copy in copies:
        copy.start()
    for copy in copies:
        copy.wait()


def start_kernel(chips, act, grad, in_rows, out_rows, first, second, send, sems, send_sems):
    core = lax.axis_index("dp") & 1
    a_width = in_rows.shape[1]
    cut = first.shape[1]
    pairs = [
        (in_rows, first.at[:, pl.ds(0, a_width)]),
        (out_rows.at[:, pl.ds(0, cut - a_width)], first.at[:, pl.ds(a_width, cut - a_width)]),
        (out_rows.at[:, pl.ds(cut - a_width, second.shape[1])], second),
    ]
    copies = [pltpu.make_async_copy(*pair, sems.at[i]) for i, pair in enumerate(pairs)]
    for chip in range(chips):
        copies += column_copies(chip, 1 - core, act, grad, send.at[chip], send_sems.at[chip], chips)
    run_copies(copies)


def start(act, grad, in_rows, out_rows, chips):
    rows = act.shape[0]
    rank, width = in_rows.shape[0], in_rows.shape[1] + out_rows.shape[1]
    cut = width // 256 * 128
    shapes = (rank, cut), (rank, width - cut), (chips, rows, width)
    return pl.pallas_call(
        functools.partial(start_kernel, chips),
        out_shape=[pltpu.VMEM(shape, act.dtype) for shape in shapes],
        in_specs=[HBM] * 4,
        out_specs=[VMEM] * 3,
        scratch_shapes=[pltpu.SemaphoreType.DMA((3,)), pltpu.SemaphoreType.DMA((chips, 2))],
        compiler_params=pltpu.CompilerParams(vmem_limit_bytes=16 * 2**20),
        cost_estimate=pl.CostEstimate(
            flops=0, bytes_accessed=4 * (rank + chips * rows) * width, transcendentals=0
        ),
    )(*held(pltpu.HBM, act, grad, in_rows, out_rows))


def project_kernel(chips, items, a_width, cut, carry, act, grad, theirs, *refs):
    chunks, refs = refs[: len(items)], refs[len(items) :]
    out = refs[-1]
    rank = chunks[0].shape[0]
    g_width = theirs.shape[2] - a_width
    me = lax.axis_index("dp")
    if carry:
        a_sum, g_sum = refs[0][:, :rank], refs[0][:, rank:]
    else:
        a_sum = g_sum = jnp.zeros((out.shape[0], rank), jnp.float32)
    for (offset, part), chunk in zip(items, chunks):
        chip = chip_behind(offset, chips)
        block = 2 * chip + ((me & 1) ^ odd(me >> 1) ^ odd(chip))

        def tokens(ref, width, skip, first, last):
            at = pl.multiple_of(block * width, 128) + (first - skip)
            return jnp.concatenate(
                [ref[:, pl.ds(at, last - first)], theirs[chip, :, first:last]], axis=0
            )

        if part == 0:
            a_sum += dot(tokens(act, a_width, 0, 0, a_width), chunk[:, :a_width], NT)
            g_sum += dot(tokens(grad, g_width, a_width, a_width, cut), chunk[:, a_width:], NT)
        else:
            g_sum += dot(tokens(grad, g_width, a_width, cut, theirs.shape[2]), chunk[...], NT)
    out[:, :rank] = a_sum
    out[:, rank:] = g_sum


def project(tokens, items, chunks, a_width, cut, total=None):
    chips, rows, _ = tokens[2].shape
    rank = chunks[0].shape[0]
    columns = sum(x.shape[1] for x in chunks)
    carried = [] if total is None else [total]
    return pl.pallas_call(
        functools.partial(project_kernel, chips, items, a_width, cut, total is not None),
        out_shape=pltpu.VMEM((2 * rows, 2 * rank), jnp.float32),
        in_specs=[VMEM] * (3 + len(chunks) + len(carried)),
        out_specs=VMEM,
        compiler_params=pltpu.CompilerParams(vmem_limit_bytes=16 * 2**20),
        cost_estimate=pl.CostEstimate(
            flops=4 * rows * rank * columns,
            bytes_accessed=(2 * rows + rank) * columns * 2,
            transcendentals=0,
        ),
    )(*held(pltpu.VMEM, *tokens, *chunks, *carried))


def score_kernel(scale, conditioned, queries, out):
    width = conditioned.shape[2]
    total = jnp.zeros(out.shape, jnp.float32)
    for i in range(conditioned.shape[0]):
        total += dot(conditioned[i], queries[:, i * width : (i + 1) * width], NT)
    out[...] = total * scale


def score(conditioned, queries, scale):
    return pl.pallas_call(
        functools.partial(score_kernel, scale),
        out_shape=jax.ShapeDtypeStruct((conditioned.shape[1], queries.shape[0]), jnp.float32),
        in_specs=[VMEM] * 2,
        out_specs=VMEM,
        compiler_params=pltpu.CompilerParams(vmem_limit_bytes=16 * 2**20),
    )(*held(pltpu.VMEM, conditioned, queries))


def to_all(x, groups):
    copies = jnp.broadcast_to(x[None], (len(groups[0]),) + x.shape)
    return lax.all_to_all(copies, "dp", 0, 0, axis_index_groups=groups, tiled=True)


def local(activations, out_grads, in_basis, out_basis, preconditioner, queries):
    rows = activations.shape[0]
    a_width, rank = in_basis.shape
    n = activations.shape[1] // a_width
    chips = n // 2
    split = LEN // rows

    *own, send = start(activations, out_grads, in_basis.T, out_basis.T, chips)
    theirs = swap(send, 1, n)
    up, down = [own], [own]
    for _ in range(chips // 2 - 1):
        up.append([ring(x, 1, chips) for x in up[-1]])
        down.append([ring(x, -1, chips) for x in down[-1]])
    last = chips // 2 - 1
    far = (ring(up[last][0], 1, chips), ring(down[last][1], -1, chips))

    tokens = activations, out_grads, theirs
    run = functools.partial(project, tokens, a_width=a_width, cut=own[0].shape[1])
    near, items = [*own], [(0, 0), (0, 1)]
    for i in range(1, last):
        near += [*up[i], *down[i]]
        items += [(offset, part) for offset in (i, -i) for part in range(2)]
    total = run(items, near)
    items = [(offset, part) for offset in (last, -last) for part in range(2)]
    total = run(items, [*up[last], *down[last]], total=total)
    for part, chunk in enumerate(far):
        total = run([(chips // 2, part)], [chunk], total=total)
    theirs = swap(total, 1, n)
    total = (total + jnp.concatenate([theirs[rows:], theirs[:rows]], axis=0)).astype(jnp.bfloat16)

    raw = dot(total[:, rank:], total[:, :rank], TN)
    raw = (raw * (1.0 / math.sqrt(LEN))).reshape(-1, 128)
    groups = [[2 * i + (c ^ (i & 1)) for i in range(chips)] for c in range(2)]
    raw = to_all(raw, groups)
    features = raw.reshape((-1, split // 2) + raw.shape[1:]).sum(axis=1)
    features = features.astype(jnp.bfloat16).reshape(-1, rank * rank)

    conditioned = dot(features, preconditioner, NT).astype(jnp.bfloat16)
    return score(to_all(conditioned, [list(range(n))]), queries, 1.0 / rank)


def local_gathered(activations, out_grads, in_basis, out_basis, preconditioner, queries):
    rows = activations.shape[0]
    rank = in_basis.shape[1]
    act_proj = jnp.dot(
        activations,
        lax.all_gather(in_basis, "dp", axis=0, tiled=True),
        preferred_element_type=jnp.float32,
    ).astype(jnp.bfloat16)
    grad_proj = jnp.dot(
        out_grads,
        lax.all_gather(out_basis, "dp", axis=0, tiled=True),
        preferred_element_type=jnp.float32,
    ).astype(jnp.bfloat16)
    raw = dot(grad_proj, act_proj, TN).reshape(1, rank * rank) * (1.0 / math.sqrt(LEN))
    gathered = lax.all_gather(raw, "dp", axis=0, tiled=True)
    features = gathered.reshape(-1, LEN // rows, rank * rank).sum(axis=1).astype(jnp.bfloat16)
    conditioned = dot(features, preconditioner, NT).astype(jnp.bfloat16)
    scores = dot(lax.all_gather(conditioned, "dp", axis=1, tiled=True), queries, NT)
    return scores * (1.0 / rank)


def power_of_two(x):
    return x > 0 and x & (x - 1) == 0


def solution(mesh):
    n = mesh.shape["dp"]

    def body(activations, out_grads, in_basis, out_basis, preconditioner, queries):
        aligned = all(x.shape[0] % 128 == 0 for x in (in_basis, out_basis, preconditioner))
        split = LEN // activations.shape[0]
        regular = aligned and n >= 8 and power_of_two(n) and power_of_two(split) and 4 <= split <= n
        form = local if regular else local_gathered
        return form(activations, out_grads, in_basis, out_basis, preconditioner, queries)

    return jax.shard_map(
        body,
        mesh=mesh,
        in_specs=(
            P(("parts", "dp"), None),
            P(("parts", "dp"), None),
            P("dp", None),
            P("dp", None),
            P("dp", None),
            P("dp", None),
        ),
        out_specs=P("parts", "dp"),
        check_vma=False,
    )
```

```python
import functools
import math

import jax
import jax.numpy as jnp
from jax import lax
from jax.experimental import pallas as pl
from jax.experimental.pallas import tpu as pltpu
from jax.sharding import PartitionSpec as P

LEN = 1024
NT = (((1,), (1,)), ((), ()))
TN = (((0,), (0,)), ((), ()))
VMEM = pl.BlockSpec(memory_space=pltpu.VMEM)
HBM = pl.BlockSpec(memory_space=pltpu.HBM)


def held(space, *arrays):
    return [pltpu.with_memory_space_constraint(x, space) for x in arrays]


def dot(a, b, dims):
    return lax.dot_general(a, b, dims, preferred_element_type=jnp.float32)


def chip_behind(offset, chips):
    chip = lax.axis_index("dp") >> 1
    z, y = chip >> 1, chip & 1
    place = (jnp.where(y == 0, z, chips - 1 - z) - offset) & (chips - 1)
    return jnp.where(place < chips // 2, 2 * place, 2 * (chips - 1 - place) + 1)


def ring(x, step, chips):
    half = chips // 2
    chip = [2 * p if p < half else 2 * (chips - 1 - p) + 1 for p in range(chips)]
    pairs = [
        (chip[p] * 2 + c, chip[(p + step) % chips] * 2 + 1 - c) for p in range(chips) for c in range(2)
    ]
    return lax.ppermute(x, "dp", pairs)


def swap(x, bit, n):
    return lax.ppermute(x, "dp", [(i, i ^ bit) for i in range(n)])


def odd(chip):
    return (chip ^ (chip >> 1)) & 1


def gradient_runs(chips):
    runs = []
    for chip in range(chips):
        block = 2 * chip + odd(chip)
        if runs and sum(runs[-1]) == block:
            runs[-1] = (runs[-1][0], runs[-1][1] + 1)
        else:
            runs.append((block, 1))
    return runs


def run_copies(copies):
    for copy in copies:
        copy.start()
    for copy in copies:
        copy.wait()


def start_kernel(chips, act, grad, in_rows, out_rows, first, second, send, sems):
    me = lax.axis_index("dp")
    ring_of = 1 ^ (me & 1) ^ odd(me >> 1)
    a_width, g_width = in_rows.shape[1], out_rows.shape[1]
    cut = first.shape[1]
    pairs = [
        (in_rows, first.at[:, pl.ds(0, a_width)]),
        (out_rows.at[:, pl.ds(0, cut - a_width)], first.at[:, pl.ds(a_width, cut - a_width)]),
        (out_rows.at[:, pl.ds(cut - a_width, second.shape[1])], second),
        (act, send.at[:, pl.ds(0, act.shape[1])]),
    ]
    to = act.shape[1]
    for block, length in gradient_runs(chips):
        at = pl.multiple_of(((block + 4 * ring_of) & (2 * chips - 1)) * g_width, 128)
        width = length * g_width
        pairs.append((grad.at[:, pl.ds(at, width)], send.at[:, pl.ds(to, width)]))
        to += width
    run_copies([pltpu.make_async_copy(*pair, sems.at[i]) for i, pair in enumerate(pairs)])


def start(act, grad, in_rows, out_rows, chips):
    rows = act.shape[0]
    rank, width = in_rows.shape[0], in_rows.shape[1] + out_rows.shape[1]
    cut = width // 256 * 128
    columns = act.shape[1] + grad.shape[1] // 2
    shapes = (rank, cut), (rank, width - cut), (rows, columns)
    return pl.pallas_call(
        functools.partial(start_kernel, chips),
        out_shape=[pltpu.VMEM(shape, act.dtype) for shape in shapes],
        in_specs=[HBM] * 4,
        out_specs=[VMEM] * 3,
        scratch_shapes=[pltpu.SemaphoreType.DMA((4 + len(gradient_runs(chips)),))],
        compiler_params=pltpu.CompilerParams(vmem_limit_bytes=16 * 2**20),
        cost_estimate=pl.CostEstimate(
            flops=0, bytes_accessed=4 * (rank * width + rows * columns), transcendentals=0
        ),
    )(*held(pltpu.HBM, act, grad, in_rows, out_rows))


def project_kernel(chips, items, a_width, cut, carry, act, grad, theirs, *refs):
    chunks, refs = refs[: len(items)], refs[len(items) :]
    out = refs[-1]
    rank = chunks[0].shape[0]
    g_width = grad.shape[1] // (2 * chips)
    me = lax.axis_index("dp")
    ring_of = (me & 1) ^ odd(me >> 1)
    if carry:
        a_sum, g_sum = refs[0][:, :rank], refs[0][:, rank:]
    else:
        a_sum = g_sum = jnp.zeros((out.shape[0], rank), jnp.float32)
    for (offset, part), chunk in zip(items, chunks):
        chip = chip_behind(offset, chips)
        block = 2 * chip + (ring_of ^ odd(chip))
        place = (chip - 2 * ring_of) & (chips - 1)
        a_at = pl.ds(pl.multiple_of(block * a_width, 128), a_width)
        mine_at = pl.multiple_of(block * g_width, 128)
        theirs_at = pl.multiple_of(act.shape[1] + place * g_width, 128)

        def gradients(first, last):
            columns = [pl.ds(at + first, last - first) for at in (mine_at, theirs_at)]
            return jnp.concatenate([grad[:, columns[0]], theirs[:, columns[1]]], axis=0)

        if part == 0:
            a_tokens = jnp.concatenate([act[:, a_at], theirs[:, a_at]], axis=0)
            a_sum += dot(a_tokens, chunk[:, :a_width], NT)
            g_sum += dot(gradients(0, cut - a_width), chunk[:, a_width:], NT)
        else:
            g_sum += dot(gradients(cut - a_width, g_width), chunk[...], NT)
    out[:, :rank] = a_sum
    out[:, rank:] = g_sum


def project(tokens, items, chunks, a_width, cut, total=None):
    rows = tokens[0].shape[0]
    chips = tokens[0].shape[1] // (2 * a_width)
    rank = chunks[0].shape[0]
    columns = sum(x.shape[1] for x in chunks)
    carried = [] if total is None else [total]
    return pl.pallas_call(
        functools.partial(project_kernel, chips, items, a_width, cut, total is not None),
        out_shape=pltpu.VMEM((2 * rows, 2 * rank), jnp.float32),
        in_specs=[VMEM] * (3 + len(chunks) + len(carried)),
        out_specs=VMEM,
        compiler_params=pltpu.CompilerParams(vmem_limit_bytes=16 * 2**20),
        cost_estimate=pl.CostEstimate(
            flops=4 * rows * rank * columns,
            bytes_accessed=(2 * rows + rank) * columns * 2,
            transcendentals=0,
        ),
    )(*held(pltpu.VMEM, *tokens, *chunks, *carried))


def score_kernel(scale, conditioned, queries, out):
    width = conditioned.shape[2]
    total = jnp.zeros(out.shape, jnp.float32)
    for i in range(conditioned.shape[0]):
        total += dot(conditioned[i], queries[:, i * width : (i + 1) * width], NT)
    out[...] = total * scale


def score(conditioned, queries, scale):
    return pl.pallas_call(
        functools.partial(score_kernel, scale),
        out_shape=jax.ShapeDtypeStruct((conditioned.shape[1], queries.shape[0]), jnp.float32),
        in_specs=[VMEM] * 2,
        out_specs=VMEM,
        compiler_params=pltpu.CompilerParams(vmem_limit_bytes=16 * 2**20),
    )(*held(pltpu.VMEM, conditioned, queries))


def to_all(x, groups):
    copies = jnp.broadcast_to(x[None], (len(groups[0]),) + x.shape)
    return lax.all_to_all(copies, "dp", 0, 0, axis_index_groups=groups, tiled=True)


def local(activations, out_grads, in_basis, out_basis, preconditioner, queries):
    rows = activations.shape[0]
    a_width, rank = in_basis.shape
    n = activations.shape[1] // a_width
    chips = n // 2
    split = LEN // rows

    *own, send = start(activations, out_grads, in_basis.T, out_basis.T, chips)
    theirs = swap(send, 1, n)
    up, down = [own], [own]
    for _ in range(chips // 2 - 1):
        up.append([ring(x, 1, chips) for x in up[-1]])
        down.append([ring(x, -1, chips) for x in down[-1]])
    last = chips // 2 - 1
    far = (ring(up[last][0], 1, chips), ring(down[last][1], -1, chips))

    tokens = activations, out_grads, theirs
    run = functools.partial(project, tokens, a_width=a_width, cut=own[0].shape[1])
    near, items = [*own], [(0, 0), (0, 1)]
    for i in range(1, last):
        near += [*up[i], *down[i]]
        items += [(offset, part) for offset in (i, -i) for part in range(2)]
    total = run(items, near)
    items = [(offset, part) for offset in (last, -last) for part in range(2)]
    total = run(items, [*up[last], *down[last]], total=total)
    for part, chunk in enumerate(far):
        total = run([(chips // 2, part)], [chunk], total=total)
    theirs = swap(total, 1, n)
    total = (total + jnp.concatenate([theirs[rows:], theirs[:rows]], axis=0)).astype(jnp.bfloat16)

    raw = dot(total[:, rank:], total[:, :rank], TN)
    raw = (raw * (1.0 / math.sqrt(LEN))).reshape(-1, 128)
    planes = [[2 * i + c for i in range(chips)] for c in range(2)]
    raw = to_all(raw, planes)
    features = raw.reshape((-1, split // 2) + raw.shape[1:]).sum(axis=1)
    features = features.astype(jnp.bfloat16).reshape(-1, rank * rank)

    conditioned = dot(features, preconditioner, NT).astype(jnp.bfloat16)
    return score(to_all(conditioned, [list(range(n))]), queries, 1.0 / rank)


def local_gathered(activations, out_grads, in_basis, out_basis, preconditioner, queries):
    rows = activations.shape[0]
    rank = in_basis.shape[1]
    act_proj = jnp.dot(
        activations,
        lax.all_gather(in_basis, "dp", axis=0, tiled=True),
        preferred_element_type=jnp.float32,
    ).astype(jnp.bfloat16)
    grad_proj = jnp.dot(
        out_grads,
        lax.all_gather(out_basis, "dp", axis=0, tiled=True),
        preferred_element_type=jnp.float32,
    ).astype(jnp.bfloat16)
    raw = dot(grad_proj, act_proj, TN).reshape(1, rank * rank) * (1.0 / math.sqrt(LEN))
    gathered = lax.all_gather(raw, "dp", axis=0, tiled=True)
    features = gathered.reshape(-1, LEN // rows, rank * rank).sum(axis=1).astype(jnp.bfloat16)
    conditioned = dot(features, preconditioner, NT).astype(jnp.bfloat16)
    scores = dot(lax.all_gather(conditioned, "dp", axis=1, tiled=True), queries, NT)
    return scores * (1.0 / rank)


def power_of_two(x):
    return x > 0 and x & (x - 1) == 0


def solution(mesh):
    n = mesh.shape["dp"]

    def body(activations, out_grads, in_basis, out_basis, preconditioner, queries):
        aligned = all(x.shape[0] % 128 == 0 for x in (in_basis, out_basis, preconditioner))
        split = LEN // activations.shape[0]
        regular = aligned and n >= 8 and power_of_two(n) and power_of_two(split) and 4 <= split <= n
        form = local if regular else local_gathered
        return form(activations, out_grads, in_basis, out_basis, preconditioner, queries)

    return jax.shard_map(
        body,
        mesh=mesh,
        in_specs=(
            P(("parts", "dp"), None),
            P(("parts", "dp"), None),
            P("dp", None),
            P("dp", None),
            P("dp", None),
            P("dp", None),
        ),
        out_specs=P("parts", "dp"),
        check_vma=False,
    )
```

```python
import functools
import math

import jax
import jax.numpy as jnp
from jax import lax
from jax.experimental import pallas as pl
from jax.experimental.pallas import tpu as pltpu
from jax.sharding import PartitionSpec as P

LEN = 1024
HIDE = 10**11
NT = (((1,), (1,)), ((), ()))
TN = (((0,), (0,)), ((), ()))
VMEM = pl.BlockSpec(memory_space=pltpu.VMEM)
HBM = pl.BlockSpec(memory_space=pltpu.HBM)


def held(space, *arrays):
    return [pltpu.with_memory_space_constraint(x, space) for x in arrays]


def dot(a, b, dims):
    return lax.dot_general(a, b, dims, preferred_element_type=jnp.float32)


def chip_behind(offset, chips):
    chip = lax.axis_index("dp") >> 1
    z, y = chip >> 1, chip & 1
    place = (jnp.where(y == 0, z, chips - 1 - z) - offset) & (chips - 1)
    return jnp.where(place < chips // 2, 2 * place, 2 * (chips - 1 - place) + 1)


def ring(x, step, chips):
    half = chips // 2
    chip = [2 * p if p < half else 2 * (chips - 1 - p) + 1 for p in range(chips)]
    pairs = [
        (chip[p] * 2 + c, chip[(p + step) % chips] * 2 + 1 - c) for p in range(chips) for c in range(2)
    ]
    return lax.ppermute(x, "dp", pairs)


def swap(x, bit, n):
    return lax.ppermute(x, "dp", [(i, i ^ bit) for i in range(n)])


def odd(chip):
    return (chip ^ (chip >> 1)) & 1


def column_copies(chip, ring_core, act, grad, out, sems, chips):
    block = 2 * chip + (ring_core ^ odd(lax.axis_index("dp") >> 1) ^ odd(chip))
    a_width, g_width = (x.shape[1] // (2 * chips) for x in (act, grad))
    return [
        pltpu.make_async_copy(
            ref.at[:, pl.ds(pl.multiple_of(block * width, 128), width)],
            out.at[:, pl.ds(at, width)],
            sems.at[k],
        )
        for k, (ref, at, width) in enumerate(((act, 0, a_width), (grad, a_width, g_width)))
    ]


def run_copies(copies):
    for copy in copies:
        copy.start()
    for copy in copies:
        copy.wait()


def chunk_kernel(in_rows, out_rows, first, second, sems):
    a_width = in_rows.shape[1]
    cut = first.shape[1]
    pairs = [
        (in_rows, first.at[:, pl.ds(0, a_width)]),
        (out_rows.at[:, pl.ds(0, cut - a_width)], first.at[:, pl.ds(a_width, cut - a_width)]),
        (out_rows.at[:, pl.ds(cut - a_width, second.shape[1])], second),
    ]
    run_copies([pltpu.make_async_copy(*pair, sems.at[i]) for i, pair in enumerate(pairs)])


def chunks_of(in_rows, out_rows):
    rank, width = in_rows.shape[0], in_rows.shape[1] + out_rows.shape[1]
    cut = width // 256 * 128
    return pl.pallas_call(
        chunk_kernel,
        out_shape=[pltpu.VMEM((rank, w), in_rows.dtype) for w in (cut, width - cut)],
        in_specs=[HBM] * 2,
        out_specs=[VMEM] * 2,
        scratch_shapes=[pltpu.SemaphoreType.DMA((3,))],
        compiler_params=pltpu.CompilerParams(vmem_limit_bytes=16 * 2**20),
        cost_estimate=pl.CostEstimate(
            flops=0, bytes_accessed=4 * rank * width, transcendentals=0
        ),
    )(*held(pltpu.HBM, in_rows, out_rows))


def pack_kernel(chips, act, grad, send, sems):
    core = lax.axis_index("dp") & 1
    copies = []
    for chip in range(chips):
        copies += column_copies(chip, 1 - core, act, grad, send.at[chip], sems.at[chip], chips)
    run_copies(copies)


def pack(act, grad, chips):
    rows, width = act.shape[0], (act.shape[1] + grad.shape[1]) // (2 * chips)
    return pl.pallas_call(
        functools.partial(pack_kernel, chips),
        out_shape=pltpu.VMEM((chips, rows, width), act.dtype),
        in_specs=[HBM] * 2,
        out_specs=VMEM,
        scratch_shapes=[pltpu.SemaphoreType.DMA((chips, 2))],
        compiler_params=pltpu.CompilerParams(vmem_limit_bytes=16 * 2**20),
        cost_estimate=pl.CostEstimate(
            flops=0, bytes_accessed=4 * chips * rows * width, transcendentals=0
        ),
    )(*held(pltpu.HBM, act, grad))


def project_kernel(chips, items, a_width, cut, carry, act, grad, *refs):
    theirs = None
    if carry:
        theirs, refs = refs[0], refs[1:]
    chunks, refs = refs[: len(items)], refs[len(items) :]
    out = refs[-1]
    rows, rank = act.shape[0], chunks[0].shape[0]
    g_width = grad.shape[1] // (2 * chips)
    me = lax.axis_index("dp")
    if carry:
        a_sum, g_sum = refs[0][:, :rank], refs[0][:, rank:]
    else:
        a_sum = g_sum = jnp.zeros((2 * rows, rank), jnp.float32)
    for (offset, part, whose), chunk in zip(items, chunks):
        chip = chip_behind(offset, chips)
        block = 2 * chip + ((me & 1) ^ odd(me >> 1) ^ odd(chip))

        def product(ref, width, skip, first, last, basis):
            at = pl.multiple_of(block * width, 128) + (first - skip)
            tokens = []
            if whose != 1:
                tokens.append(ref[:, pl.ds(at, last - first)])
            if whose != 0:
                tokens.append(theirs[chip, :, first:last])
            value = dot(jnp.concatenate(tokens, axis=0), basis, NT)
            if whose == 2:
                return value
            none = jnp.zeros((rows, rank), jnp.float32)
            return jnp.concatenate([none, value] if whose == 1 else [value, none], axis=0)

        if part == 0:
            a_sum += product(act, a_width, 0, 0, a_width, chunk[:, :a_width])
            g_sum += product(grad, g_width, a_width, a_width, cut, chunk[:, a_width:])
        else:
            g_sum += product(grad, g_width, a_width, cut, a_width + g_width, chunk[...])
    out[:, :rank] = a_sum
    out[:, rank:] = g_sum


def project(tokens, items, chunks, a_width, cut, total=None, hide=0):
    rows = tokens[0].shape[0]
    chips = tokens[0].shape[1] // (2 * a_width)
    rank = chunks[0].shape[0]
    columns = sum(x.shape[1] for x in chunks)
    carried = [] if total is None else [total]
    operands = [*tokens, *chunks, *carried]
    return pl.pallas_call(
        functools.partial(project_kernel, chips, items, a_width, cut, total is not None),
        out_shape=pltpu.VMEM((2 * rows, 2 * rank), jnp.float32),
        in_specs=[VMEM] * len(operands),
        out_specs=VMEM,
        compiler_params=pltpu.CompilerParams(vmem_limit_bytes=16 * 2**20),
        cost_estimate=pl.CostEstimate(
            flops=4 * rows * rank * columns + hide,
            bytes_accessed=(2 * rows + rank) * columns * 2,
            transcendentals=0,
        ),
    )(*held(pltpu.VMEM, *operands))


def score_kernel(scale, conditioned, queries, out):
    width = conditioned.shape[2]
    total = jnp.zeros(out.shape, jnp.float32)
    for i in range(conditioned.shape[0]):
        total += dot(conditioned[i], queries[:, i * width : (i + 1) * width], NT)
    out[...] = total * scale


def score(conditioned, queries, scale):
    return pl.pallas_call(
        functools.partial(score_kernel, scale),
        out_shape=jax.ShapeDtypeStruct((conditioned.shape[1], queries.shape[0]), jnp.float32),
        in_specs=[VMEM] * 2,
        out_specs=VMEM,
        compiler_params=pltpu.CompilerParams(vmem_limit_bytes=16 * 2**20),
    )(*held(pltpu.VMEM, conditioned, queries))


def to_all(x, groups):
    copies = jnp.broadcast_to(x[None], (len(groups[0]),) + x.shape)
    return lax.all_to_all(copies, "dp", 0, 0, axis_index_groups=groups, tiled=True)


def local(activations, out_grads, in_basis, out_basis, preconditioner, queries):
    rows = activations.shape[0]
    a_width, rank = in_basis.shape
    n = activations.shape[1] // a_width
    chips = n // 2
    split = LEN // rows

    own = list(chunks_of(in_basis.T, out_basis.T))
    theirs = swap(pack(activations, out_grads, chips), 1, n)
    run = functools.partial(project, a_width=a_width, cut=own[0].shape[1])
    mine = activations, out_grads
    last = chips // 2 - 1
    up, down = [own], [own]
    for i in range(last):
        if i == 1:
            total = run(mine, [(0, 0, 0), (0, 1, 0)], own, hide=HIDE)
            total, up[i][0] = lax.optimization_barrier((total, up[i][0]))
        up.append([ring(x, 1, chips) for x in up[-1]])
        down.append([ring(x, -1, chips) for x in down[-1]])
    far = (ring(up[last][0], 1, chips), ring(down[last][1], -1, chips))

    run = functools.partial(run, (*mine, theirs))
    near, items = [*own], [(0, 0, 1), (0, 1, 1)]
    for i in range(1, last):
        near += [*up[i], *down[i]]
        items += [(offset, part, 2) for offset in (i, -i) for part in range(2)]
    total = run(items, near, total=total)
    items = [(offset, part, 2) for offset in (last, -last) for part in range(2)]
    total = run(items, [*up[last], *down[last]], total=total)
    for part, chunk in enumerate(far):
        total = run([(chips // 2, part, 2)], [chunk], total=total)
    theirs = swap(total, 1, n)
    total = (total + jnp.concatenate([theirs[rows:], theirs[:rows]], axis=0)).astype(jnp.bfloat16)

    raw = dot(total[:, rank:], total[:, :rank], TN)
    raw = (raw * (1.0 / math.sqrt(LEN))).reshape(-1, 128)
    planes = [[2 * i + c for i in range(chips)] for c in range(2)]
    raw = to_all(raw, planes)
    features = raw.reshape((-1, split // 2) + raw.shape[1:]).sum(axis=1)
    features = features.astype(jnp.bfloat16).reshape(-1, rank * rank)

    conditioned = dot(features, preconditioner, NT).astype(jnp.bfloat16)
    return score(to_all(conditioned, [list(range(n))]), queries, 1.0 / rank)


def local_gathered(activations, out_grads, in_basis, out_basis, preconditioner, queries):
    rows = activations.shape[0]
    rank = in_basis.shape[1]
    act_proj = jnp.dot(
        activations,
        lax.all_gather(in_basis, "dp", axis=0, tiled=True),
        preferred_element_type=jnp.float32,
    ).astype(jnp.bfloat16)
    grad_proj = jnp.dot(
        out_grads,
        lax.all_gather(out_basis, "dp", axis=0, tiled=True),
        preferred_element_type=jnp.float32,
    ).astype(jnp.bfloat16)
    raw = dot(grad_proj, act_proj, TN).reshape(1, rank * rank) * (1.0 / math.sqrt(LEN))
    gathered = lax.all_gather(raw, "dp", axis=0, tiled=True)
    features = gathered.reshape(-1, LEN // rows, rank * rank).sum(axis=1).astype(jnp.bfloat16)
    conditioned = dot(features, preconditioner, NT).astype(jnp.bfloat16)
    scores = dot(lax.all_gather(conditioned, "dp", axis=1, tiled=True), queries, NT)
    return scores * (1.0 / rank)


def power_of_two(x):
    return x > 0 and x & (x - 1) == 0


def solution(mesh):
    n = mesh.shape["dp"]

    def body(activations, out_grads, in_basis, out_basis, preconditioner, queries):
        aligned = all(x.shape[0] % 128 == 0 for x in (in_basis, out_basis, preconditioner))
        split = LEN // activations.shape[0]
        regular = aligned and n >= 8 and power_of_two(n) and power_of_two(split) and 4 <= split <= n
        form = local if regular else local_gathered
        return form(activations, out_grads, in_basis, out_basis, preconditioner, queries)

    return jax.shard_map(
        body,
        mesh=mesh,
        in_specs=(
            P(("parts", "dp"), None),
            P(("parts", "dp"), None),
            P("dp", None),
            P("dp", None),
            P("dp", None),
            P("dp", None),
        ),
        out_specs=P("parts", "dp"),
        check_vma=False,
    )
```

```python
import functools
import math

import jax
import jax.numpy as jnp
from jax import lax
from jax.experimental import pallas as pl
from jax.experimental.pallas import tpu as pltpu
from jax.sharding import PartitionSpec as P

LEN = 1024
NT = (((1,), (1,)), ((), ()))
TN = (((0,), (0,)), ((), ()))
VMEM = pl.BlockSpec(memory_space=pltpu.VMEM)
HBM = pl.BlockSpec(memory_space=pltpu.HBM)


def held(space, *arrays):
    return [pltpu.with_memory_space_constraint(x, space) for x in arrays]


def dot(a, b, dims):
    return lax.dot_general(a, b, dims, preferred_element_type=jnp.float32)


def chip_behind(offset, chips):
    chip = lax.axis_index("dp") >> 1
    z, y = chip >> 1, chip & 1
    place = (jnp.where(y == 0, z, chips - 1 - z) - offset) & (chips - 1)
    return jnp.where(place < chips // 2, 2 * place, 2 * (chips - 1 - place) + 1)


def ring(x, step, chips):
    half = chips // 2
    chip = [2 * p if p < half else 2 * (chips - 1 - p) + 1 for p in range(chips)]
    pairs = [
        (chip[p] * 2 + c, chip[(p + step) % chips] * 2 + 1 - c) for p in range(chips) for c in range(2)
    ]
    return lax.ppermute(x, "dp", pairs)


def swap(x, bit, n):
    return lax.ppermute(x, "dp", [(i, i ^ bit) for i in range(n)])


def odd(chip):
    return (chip ^ (chip >> 1)) & 1


def column_copies(chip, ring_core, act, grad, out, sems, chips):
    block = 2 * chip + (ring_core ^ odd(lax.axis_index("dp") >> 1) ^ odd(chip))
    a_width, g_width = (x.shape[1] // (2 * chips) for x in (act, grad))
    return [
        pltpu.make_async_copy(
            ref.at[:, pl.ds(pl.multiple_of(block * width, 128), width)],
            out.at[:, pl.ds(at, width)],
            sems.at[k],
        )
        for k, (ref, at, width) in enumerate(((act, 0, a_width), (grad, a_width, g_width)))
    ]


def run_copies(copies):
    for copy in copies:
        copy.start()
    for copy in copies:
        copy.wait()


def start_kernel(chips, act, grad, in_rows, out_rows, first, second, send, sems, send_sems):
    core = lax.axis_index("dp") & 1
    a_width = in_rows.shape[1]
    cut = first.shape[1]
    pairs = [
        (in_rows, first.at[:, pl.ds(0, a_width)]),
        (out_rows.at[:, pl.ds(0, cut - a_width)], first.at[:, pl.ds(a_width, cut - a_width)]),
        (out_rows.at[:, pl.ds(cut - a_width, second.shape[1])], second),
    ]
    copies = [pltpu.make_async_copy(*pair, sems.at[i]) for i, pair in enumerate(pairs)]
    for chip in range(chips):
        copies += column_copies(chip, 1 - core, act, grad, send.at[chip], send_sems.at[chip], chips)
    run_copies(copies)


def start(act, grad, in_rows, out_rows, chips):
    rows = act.shape[0]
    rank, width = in_rows.shape[0], in_rows.shape[1] + out_rows.shape[1]
    cut = width // 256 * 128
    shapes = (rank, cut), (rank, width - cut), (chips, rows, width)
    return pl.pallas_call(
        functools.partial(start_kernel, chips),
        out_shape=[pltpu.VMEM(shape, act.dtype) for shape in shapes],
        in_specs=[HBM] * 4,
        out_specs=[VMEM] * 3,
        scratch_shapes=[pltpu.SemaphoreType.DMA((3,)), pltpu.SemaphoreType.DMA((chips, 2))],
        compiler_params=pltpu.CompilerParams(vmem_limit_bytes=16 * 2**20),
        cost_estimate=pl.CostEstimate(
            flops=0, bytes_accessed=4 * (rank + chips * rows) * width, transcendentals=0
        ),
    )(*held(pltpu.HBM, act, grad, in_rows, out_rows))


def project_kernel(chips, items, a_width, cut, carry, act, grad, theirs, *refs):
    chunks, refs = refs[: len(items)], refs[len(items) :]
    out = refs[-1]
    rank = chunks[0].shape[0]
    g_width = theirs.shape[2] - a_width
    me = lax.axis_index("dp")
    if carry:
        a_sum, g_sum = refs[0][:, :rank], refs[0][:, rank:]
    else:
        a_sum = g_sum = jnp.zeros((out.shape[0], rank), jnp.float32)
    for (offset, part), chunk in zip(items, chunks):
        chip = chip_behind(offset, chips)
        block = 2 * chip + ((me & 1) ^ odd(me >> 1) ^ odd(chip))

        def tokens(ref, width, skip, first, last):
            at = pl.multiple_of(block * width, 128) + (first - skip)
            return jnp.concatenate(
                [ref[:, pl.ds(at, last - first)], theirs[chip, :, first:last]], axis=0
            )

        if part == 0:
            a_sum += dot(tokens(act, a_width, 0, 0, a_width), chunk[:, :a_width], NT)
            g_sum += dot(tokens(grad, g_width, a_width, a_width, cut), chunk[:, a_width:], NT)
        else:
            g_sum += dot(tokens(grad, g_width, a_width, cut, theirs.shape[2]), chunk[...], NT)
    out[:, :rank] = a_sum
    out[:, rank:] = g_sum


def project(tokens, items, chunks, a_width, cut, total=None):
    chips, rows, _ = tokens[2].shape
    rank = chunks[0].shape[0]
    columns = sum(x.shape[1] for x in chunks)
    carried = [] if total is None else [total]
    return pl.pallas_call(
        functools.partial(project_kernel, chips, items, a_width, cut, total is not None),
        out_shape=pltpu.VMEM((2 * rows, 2 * rank), jnp.float32),
        in_specs=[VMEM] * (3 + len(chunks) + len(carried)),
        out_specs=VMEM,
        compiler_params=pltpu.CompilerParams(vmem_limit_bytes=16 * 2**20),
        cost_estimate=pl.CostEstimate(
            flops=4 * rows * rank * columns,
            bytes_accessed=(2 * rows + rank) * columns * 2,
            transcendentals=0,
        ),
    )(*held(pltpu.VMEM, *tokens, *chunks, *carried))


def score_kernel(scale, conditioned, queries, out):
    width = conditioned.shape[2]
    total = jnp.zeros(out.shape, jnp.float32)
    for i in range(conditioned.shape[0]):
        total += dot(conditioned[i], queries[:, i * width : (i + 1) * width], NT)
    out[...] = total * scale


def score(conditioned, queries, scale):
    return pl.pallas_call(
        functools.partial(score_kernel, scale),
        out_shape=jax.ShapeDtypeStruct((conditioned.shape[1], queries.shape[0]), jnp.float32),
        in_specs=[VMEM] * 2,
        out_specs=VMEM,
        compiler_params=pltpu.CompilerParams(vmem_limit_bytes=16 * 2**20),
    )(*held(pltpu.VMEM, conditioned, queries))


def to_all(x, groups):
    copies = jnp.broadcast_to(x[None], (len(groups[0]),) + x.shape)
    return lax.all_to_all(copies, "dp", 0, 0, axis_index_groups=groups, tiled=True)


def local(activations, out_grads, in_basis, out_basis, preconditioner, queries):
    rows = activations.shape[0]
    a_width, rank = in_basis.shape
    n = activations.shape[1] // a_width
    chips = n // 2
    split = LEN // rows

    *own, send = start(activations, out_grads, in_basis.T, out_basis.T, chips)
    theirs = swap(send, 1, n)
    up, down = [own], [own]
    for _ in range(chips // 2 - 1):
        up.append([ring(x, 1, chips) for x in up[-1]])
        down.append([ring(x, -1, chips) for x in down[-1]])
    last = chips // 2 - 1
    far = (ring(up[last][0], 1, chips), ring(down[last][1], -1, chips))

    tokens = activations, out_grads, theirs
    run = functools.partial(project, tokens, a_width=a_width, cut=own[0].shape[1])
    near, items = [*own], [(0, 0), (0, 1)]
    for i in range(1, last):
        near += [*up[i], *down[i]]
        items += [(offset, part) for offset in (i, -i) for part in range(2)]
    total = run(items, near)
    items = [(offset, part) for offset in (last, -last) for part in range(2)]
    total = run(items, [*up[last], *down[last]], total=total)
    for part, chunk in enumerate(far):
        total = run([(chips // 2, part)], [chunk], total=total)
    theirs = swap(total, 1, n)
    total = (total + jnp.concatenate([theirs[rows:], theirs[:rows]], axis=0)).astype(jnp.bfloat16)

    raw = dot(total[:, rank:], total[:, :rank], TN)
    raw = (raw * (1.0 / math.sqrt(LEN))).reshape(2, -1, 128)
    half = lax.dynamic_index_in_dim(raw, lax.axis_index("dp") & 1, keepdims=False)
    everyone = [list(range(n))]
    raw = to_all(half, everyone).reshape((-1, split // 2) + raw.shape)
    features = raw.sum(axis=1).astype(jnp.bfloat16).reshape(-1, rank * rank)

    conditioned = dot(features, preconditioner, NT).astype(jnp.bfloat16)
    return score(to_all(conditioned, everyone), queries, 1.0 / rank)


def local_gathered(activations, out_grads, in_basis, out_basis, preconditioner, queries):
    rows = activations.shape[0]
    rank = in_basis.shape[1]
    act_proj = jnp.dot(
        activations,
        lax.all_gather(in_basis, "dp", axis=0, tiled=True),
        preferred_element_type=jnp.float32,
    ).astype(jnp.bfloat16)
    grad_proj = jnp.dot(
        out_grads,
        lax.all_gather(out_basis, "dp", axis=0, tiled=True),
        preferred_element_type=jnp.float32,
    ).astype(jnp.bfloat16)
    raw = dot(grad_proj, act_proj, TN).reshape(1, rank * rank) * (1.0 / math.sqrt(LEN))
    gathered = lax.all_gather(raw, "dp", axis=0, tiled=True)
    features = gathered.reshape(-1, LEN // rows, rank * rank).sum(axis=1).astype(jnp.bfloat16)
    conditioned = dot(features, preconditioner, NT).astype(jnp.bfloat16)
    scores = dot(lax.all_gather(conditioned, "dp", axis=1, tiled=True), queries, NT)
    return scores * (1.0 / rank)


def power_of_two(x):
    return x > 0 and x & (x - 1) == 0


def solution(mesh):
    n = mesh.shape["dp"]

    def body(activations, out_grads, in_basis, out_basis, preconditioner, queries):
        aligned = all(x.shape[0] % 128 == 0 for x in (in_basis, out_basis, preconditioner))
        split = LEN // activations.shape[0]
        regular = aligned and n >= 8 and power_of_two(n) and power_of_two(split) and 4 <= split <= n
        form = local if regular else local_gathered
        return form(activations, out_grads, in_basis, out_basis, preconditioner, queries)

    return jax.shard_map(
        body,
        mesh=mesh,
        in_specs=(
            P(("parts", "dp"), None),
            P(("parts", "dp"), None),
            P("dp", None),
            P("dp", None),
            P("dp", None),
            P("dp", None),
        ),
        out_specs=P("parts", "dp"),
        check_vma=False,
    )
```

```python
import functools
import math

import jax
import jax.numpy as jnp
from jax import lax
from jax.experimental import pallas as pl
from jax.experimental.pallas import tpu as pltpu
from jax.sharding import PartitionSpec as P

LEN = 1024
NT = (((1,), (1,)), ((), ()))
TN = (((0,), (0,)), ((), ()))
VMEM = pl.BlockSpec(memory_space=pltpu.VMEM)
HBM = pl.BlockSpec(memory_space=pltpu.HBM)


def held(space, *arrays):
    return [pltpu.with_memory_space_constraint(x, space) for x in arrays]


def dot(a, b, dims):
    return lax.dot_general(a, b, dims, preferred_element_type=jnp.float32)


def chip_behind(offset, chips):
    chip = lax.axis_index("dp") >> 1
    z, y = chip >> 1, chip & 1
    place = (jnp.where(y == 0, z, chips - 1 - z) - offset) & (chips - 1)
    return jnp.where(place < chips // 2, 2 * place, 2 * (chips - 1 - place) + 1)


def ring(x, step, chips):
    half = chips // 2
    chip = [2 * p if p < half else 2 * (chips - 1 - p) + 1 for p in range(chips)]
    pairs = [
        (chip[p] * 2 + c, chip[(p + step) % chips] * 2 + 1 - c) for p in range(chips) for c in range(2)
    ]
    return lax.ppermute(x, "dp", pairs)


def swap(x, bit, n):
    return lax.ppermute(x, "dp", [(i, i ^ bit) for i in range(n)])


def odd(chip):
    return (chip ^ (chip >> 1)) & 1


def column_copies(chip, ring_core, act, grad, out, sems, chips):
    block = 2 * chip + (ring_core ^ odd(lax.axis_index("dp") >> 1) ^ odd(chip))
    a_width, g_width = (x.shape[1] // (2 * chips) for x in (act, grad))
    return [
        pltpu.make_async_copy(
            ref.at[:, pl.ds(pl.multiple_of(block * width, 128), width)],
            out.at[:, pl.ds(at, width)],
            sems.at[k],
        )
        for k, (ref, at, width) in enumerate(((act, 0, a_width), (grad, a_width, g_width)))
    ]


def run_copies(copies):
    for copy in copies:
        copy.start()
    for copy in copies:
        copy.wait()


def start_kernel(chips, act, grad, in_rows, out_rows, first, second, send, sems, send_sems):
    core = lax.axis_index("dp") & 1
    a_width = in_rows.shape[1]
    cut = first.shape[1]
    pairs = [
        (in_rows, first.at[:, pl.ds(0, a_width)]),
        (out_rows.at[:, pl.ds(0, cut - a_width)], first.at[:, pl.ds(a_width, cut - a_width)]),
        (out_rows.at[:, pl.ds(cut - a_width, second.shape[1])], second),
    ]
    copies = [pltpu.make_async_copy(*pair, sems.at[i]) for i, pair in enumerate(pairs)]
    for chip in range(chips):
        copies += column_copies(chip, 1 - core, act, grad, send.at[chip], send_sems.at[chip], chips)
    run_copies(copies)


def start(act, grad, in_rows, out_rows, chips):
    rows = act.shape[0]
    rank, width = in_rows.shape[0], in_rows.shape[1] + out_rows.shape[1]
    cut = width // 256 * 128
    shapes = (rank, cut), (rank, width - cut), (chips, rows, width)
    return pl.pallas_call(
        functools.partial(start_kernel, chips),
        out_shape=[pltpu.VMEM(shape, act.dtype) for shape in shapes],
        in_specs=[HBM] * 4,
        out_specs=[VMEM] * 3,
        scratch_shapes=[pltpu.SemaphoreType.DMA((3,)), pltpu.SemaphoreType.DMA((chips, 2))],
        compiler_params=pltpu.CompilerParams(vmem_limit_bytes=16 * 2**20),
        cost_estimate=pl.CostEstimate(
            flops=0, bytes_accessed=4 * (rank + chips * rows) * width, transcendentals=0
        ),
    )(*held(pltpu.HBM, act, grad, in_rows, out_rows))


def project_kernel(chips, items, a_width, cut, carry, act, grad, theirs, *refs):
    chunks, refs = refs[: len(items)], refs[len(items) :]
    out = refs[-1]
    rank = chunks[0].shape[0]
    g_width = theirs.shape[2] - a_width
    me = lax.axis_index("dp")
    if carry:
        a_sum, g_sum = refs[0][:, :rank], refs[0][:, rank:]
    else:
        a_sum = g_sum = jnp.zeros((out.shape[0], rank), jnp.float32)
    for (offset, part), chunk in zip(items, chunks):
        chip = chip_behind(offset, chips)
        block = 2 * chip + ((me & 1) ^ odd(me >> 1) ^ odd(chip))

        def tokens(ref, width, skip, first, last):
            at = pl.multiple_of(block * width, 128) + (first - skip)
            return jnp.concatenate(
                [ref[:, pl.ds(at, last - first)], theirs[chip, :, first:last]], axis=0
            )

        if part == 0:
            a_sum += dot(tokens(act, a_width, 0, 0, a_width), chunk[:, :a_width], NT)
            g_sum += dot(tokens(grad, g_width, a_width, a_width, cut), chunk[:, a_width:], NT)
        else:
            g_sum += dot(tokens(grad, g_width, a_width, cut, theirs.shape[2]), chunk[...], NT)
    out[:, :rank] = a_sum
    out[:, rank:] = g_sum


def project(tokens, items, chunks, a_width, cut, total=None):
    chips, rows, _ = tokens[2].shape
    rank = chunks[0].shape[0]
    columns = sum(x.shape[1] for x in chunks)
    carried = [] if total is None else [total]
    return pl.pallas_call(
        functools.partial(project_kernel, chips, items, a_width, cut, total is not None),
        out_shape=pltpu.VMEM((2 * rows, 2 * rank), jnp.float32),
        in_specs=[VMEM] * (3 + len(chunks) + len(carried)),
        out_specs=VMEM,
        compiler_params=pltpu.CompilerParams(vmem_limit_bytes=16 * 2**20),
        cost_estimate=pl.CostEstimate(
            flops=4 * rows * rank * columns,
            bytes_accessed=(2 * rows + rank) * columns * 2,
            transcendentals=0,
        ),
    )(*held(pltpu.VMEM, *tokens, *chunks, *carried))


def score_kernel(scale, conditioned, queries, out):
    width = conditioned.shape[2]
    total = jnp.zeros(out.shape, jnp.float32)
    for i in range(conditioned.shape[0]):
        total += dot(conditioned[i], queries[:, i * width : (i + 1) * width], NT)
    out[...] = total * scale


def score(conditioned, queries, scale):
    return pl.pallas_call(
        functools.partial(score_kernel, scale),
        out_shape=jax.ShapeDtypeStruct((conditioned.shape[1], queries.shape[0]), jnp.float32),
        in_specs=[VMEM] * 2,
        out_specs=VMEM,
        compiler_params=pltpu.CompilerParams(vmem_limit_bytes=16 * 2**20),
    )(*held(pltpu.VMEM, conditioned, queries))


def to_all(x, groups):
    copies = jnp.broadcast_to(x[None], (len(groups[0]),) + x.shape)
    return lax.all_to_all(copies, "dp", 0, 0, axis_index_groups=groups, tiled=True)


def local(activations, out_grads, in_basis, out_basis, preconditioner, queries):
    rows = activations.shape[0]
    a_width, rank = in_basis.shape
    n = activations.shape[1] // a_width
    chips = n // 2
    split = LEN // rows

    *own, send = start(activations, out_grads, in_basis.T, out_basis.T, chips)
    theirs = swap(send, 1, n)
    up, down = [own], [own]
    for _ in range(chips // 2 - 1):
        up.append([ring(x, 1, chips) for x in up[-1]])
        down.append([ring(x, -1, chips) for x in down[-1]])
    last = chips // 2 - 1
    far = (ring(up[last][0], 1, chips), ring(down[last][1], -1, chips))

    tokens = activations, out_grads, theirs
    run = functools.partial(project, tokens, a_width=a_width, cut=own[0].shape[1])
    near, items = [*own], [(0, 0), (0, 1)]
    for i in range(1, last):
        near += [*up[i], *down[i]]
        items += [(offset, part) for offset in (i, -i) for part in range(2)]
    total = run(items, near)
    items = [(offset, part) for offset in (last, -last) for part in range(2)]
    total = run(items, [*up[last], *down[last]], total=total)
    for part, chunk in enumerate(far):
        total = run([(chips // 2, part)], [chunk], total=total)
    theirs = swap(total, 1, n)
    total = (total + jnp.concatenate([theirs[rows:], theirs[:rows]], axis=0)).astype(jnp.bfloat16)

    raw = dot(total[:, rank:], total[:, :rank], TN)
    raw = (raw * (1.0 / math.sqrt(LEN))).reshape(-1, 128)
    me = lax.axis_index("dp")
    sequence = lax.broadcasted_iota(jnp.int32, (n // split, 1, 1), 0)
    gives = (sequence == me // split) & ((me & 1) == 0)
    features = lax.psum(jnp.where(gives, raw[None], 0.0), "dp")
    features = features.astype(jnp.bfloat16).reshape(-1, rank * rank)

    conditioned = dot(features, preconditioner, NT).astype(jnp.bfloat16)
    return score(to_all(conditioned, [list(range(n))]), queries, 1.0 / rank)


def local_gathered(activations, out_grads, in_basis, out_basis, preconditioner, queries):
    rows = activations.shape[0]
    rank = in_basis.shape[1]
    act_proj = jnp.dot(
        activations,
        lax.all_gather(in_basis, "dp", axis=0, tiled=True),
        preferred_element_type=jnp.float32,
    ).astype(jnp.bfloat16)
    grad_proj = jnp.dot(
        out_grads,
        lax.all_gather(out_basis, "dp", axis=0, tiled=True),
        preferred_element_type=jnp.float32,
    ).astype(jnp.bfloat16)
    raw = dot(grad_proj, act_proj, TN).reshape(1, rank * rank) * (1.0 / math.sqrt(LEN))
    gathered = lax.all_gather(raw, "dp", axis=0, tiled=True)
    features = gathered.reshape(-1, LEN // rows, rank * rank).sum(axis=1).astype(jnp.bfloat16)
    conditioned = dot(features, preconditioner, NT).astype(jnp.bfloat16)
    scores = dot(lax.all_gather(conditioned, "dp", axis=1, tiled=True), queries, NT)
    return scores * (1.0 / rank)


def power_of_two(x):
    return x > 0 and x & (x - 1) == 0


def solution(mesh):
    n = mesh.shape["dp"]

    def body(activations, out_grads, in_basis, out_basis, preconditioner, queries):
        aligned = all(x.shape[0] % 128 == 0 for x in (in_basis, out_basis, preconditioner))
        split = LEN // activations.shape[0]
        regular = aligned and n >= 8 and power_of_two(n) and power_of_two(split) and 4 <= split <= n
        form = local if regular else local_gathered
        return form(activations, out_grads, in_basis, out_basis, preconditioner, queries)

    return jax.shard_map(
        body,
        mesh=mesh,
        in_specs=(
            P(("parts", "dp"), None),
            P(("parts", "dp"), None),
            P("dp", None),
            P("dp", None),
            P("dp", None),
            P("dp", None),
        ),
        out_specs=P("parts", "dp"),
        check_vma=False,
    )
```

```python
import functools
import math

import jax
import jax.numpy as jnp
from jax import lax
from jax.experimental import pallas as pl
from jax.experimental.pallas import tpu as pltpu
from jax.sharding import PartitionSpec as P

LEN = 1024
NT = (((1,), (1,)), ((), ()))
TN = (((0,), (0,)), ((), ()))
VMEM = pl.BlockSpec(memory_space=pltpu.VMEM)
HBM = pl.BlockSpec(memory_space=pltpu.HBM)


def held(space, *arrays):
    return [pltpu.with_memory_space_constraint(x, space) for x in arrays]


def dot(a, b, dims):
    return lax.dot_general(a, b, dims, preferred_element_type=jnp.float32)


def chip_behind(offset, chips):
    chip = lax.axis_index("dp") >> 1
    z, y = chip >> 1, chip & 1
    place = (jnp.where(y == 0, z, chips - 1 - z) - offset) & (chips - 1)
    return jnp.where(place < chips // 2, 2 * place, 2 * (chips - 1 - place) + 1)


def ring(x, step, chips):
    half = chips // 2
    chip = [2 * p if p < half else 2 * (chips - 1 - p) + 1 for p in range(chips)]
    pairs = [
        (chip[p] * 2 + c, chip[(p + step) % chips] * 2 + 1 - c) for p in range(chips) for c in range(2)
    ]
    return lax.ppermute(x, "dp", pairs)


def swap(x, bit, n):
    return lax.ppermute(x, "dp", [(i, i ^ bit) for i in range(n)])


def odd(chip):
    return (chip ^ (chip >> 1)) & 1


def column_copies(chip, ring_core, act, grad, out, sems, chips):
    block = 2 * chip + (ring_core ^ odd(lax.axis_index("dp") >> 1) ^ odd(chip))
    a_width, g_width = (x.shape[1] // (2 * chips) for x in (act, grad))
    return [
        pltpu.make_async_copy(
            ref.at[:, pl.ds(pl.multiple_of(block * width, 128), width)],
            out.at[:, pl.ds(at, width)],
            sems.at[k],
        )
        for k, (ref, at, width) in enumerate(((act, 0, a_width), (grad, a_width, g_width)))
    ]


def run_copies(copies):
    for copy in copies:
        copy.start()
    for copy in copies:
        copy.wait()


def start_kernel(chips, act, grad, in_rows, out_rows, first, second, send, sems, send_sems):
    core = lax.axis_index("dp") & 1
    a_width = in_rows.shape[1]
    cut = first.shape[1]
    pairs = [
        (in_rows, first.at[:, pl.ds(0, a_width)]),
        (out_rows.at[:, pl.ds(0, cut - a_width)], first.at[:, pl.ds(a_width, cut - a_width)]),
        (out_rows.at[:, pl.ds(cut - a_width, second.shape[1])], second),
    ]
    copies = [pltpu.make_async_copy(*pair, sems.at[i]) for i, pair in enumerate(pairs)]
    for chip in range(chips):
        copies += column_copies(chip, 1 - core, act, grad, send.at[chip], send_sems.at[chip], chips)
    run_copies(copies)


def start(act, grad, in_rows, out_rows, chips):
    rows = act.shape[0]
    rank, width = in_rows.shape[0], in_rows.shape[1] + out_rows.shape[1]
    cut = width // 256 * 128
    shapes = (rank, cut), (rank, width - cut), (chips, rows, width)
    return pl.pallas_call(
        functools.partial(start_kernel, chips),
        out_shape=[pltpu.VMEM(shape, act.dtype) for shape in shapes],
        in_specs=[HBM] * 4,
        out_specs=[VMEM] * 3,
        scratch_shapes=[pltpu.SemaphoreType.DMA((3,)), pltpu.SemaphoreType.DMA((chips, 2))],
        compiler_params=pltpu.CompilerParams(vmem_limit_bytes=16 * 2**20),
        cost_estimate=pl.CostEstimate(
            flops=0, bytes_accessed=4 * (rank + chips * rows) * width, transcendentals=0
        ),
    )(*held(pltpu.HBM, act, grad, in_rows, out_rows))


def project_kernel(chips, items, a_width, cut, carry, act, grad, theirs, *refs):
    chunks, refs = refs[: len(items)], refs[len(items) :]
    out = refs[-1]
    rank = chunks[0].shape[0]
    g_width = theirs.shape[2] - a_width
    me = lax.axis_index("dp")
    if carry:
        a_sum, g_sum = refs[0][:, :rank], refs[0][:, rank:]
    else:
        a_sum = g_sum = jnp.zeros((out.shape[0], rank), jnp.float32)
    for (offset, part), chunk in zip(items, chunks):
        chip = chip_behind(offset, chips)
        block = 2 * chip + ((me & 1) ^ odd(me >> 1) ^ odd(chip))

        def tokens(ref, width, skip, first, last):
            at = pl.multiple_of(block * width, 128) + (first - skip)
            return jnp.concatenate(
                [ref[:, pl.ds(at, last - first)], theirs[chip, :, first:last]], axis=0
            )

        if part == 0:
            a_sum += dot(tokens(act, a_width, 0, 0, a_width), chunk[:, :a_width], NT)
            g_sum += dot(tokens(grad, g_width, a_width, a_width, cut), chunk[:, a_width:], NT)
        else:
            g_sum += dot(tokens(grad, g_width, a_width, cut, theirs.shape[2]), chunk[...], NT)
    out[:, :rank] = a_sum
    out[:, rank:] = g_sum


def project(tokens, items, chunks, a_width, cut, total=None):
    chips, rows, _ = tokens[2].shape
    rank = chunks[0].shape[0]
    columns = sum(x.shape[1] for x in chunks)
    carried = [] if total is None else [total]
    return pl.pallas_call(
        functools.partial(project_kernel, chips, items, a_width, cut, total is not None),
        out_shape=pltpu.VMEM((2 * rows, 2 * rank), jnp.float32),
        in_specs=[VMEM] * (3 + len(chunks) + len(carried)),
        out_specs=VMEM,
        compiler_params=pltpu.CompilerParams(vmem_limit_bytes=16 * 2**20),
        cost_estimate=pl.CostEstimate(
            flops=4 * rows * rank * columns,
            bytes_accessed=(2 * rows + rank) * columns * 2,
            transcendentals=0,
        ),
    )(*held(pltpu.VMEM, *tokens, *chunks, *carried))


def score_kernel(scale, conditioned, queries, out):
    width = conditioned.shape[2]
    total = jnp.zeros(out.shape, jnp.float32)
    for i in range(conditioned.shape[0]):
        total += dot(conditioned[i], queries[:, i * width : (i + 1) * width], NT)
    out[...] = total * scale


def score(conditioned, queries, scale):
    return pl.pallas_call(
        functools.partial(score_kernel, scale),
        out_shape=jax.ShapeDtypeStruct((conditioned.shape[1], queries.shape[0]), jnp.float32),
        in_specs=[VMEM] * 2,
        out_specs=VMEM,
        compiler_params=pltpu.CompilerParams(vmem_limit_bytes=16 * 2**20),
    )(*held(pltpu.VMEM, conditioned, queries))


def to_all(x, groups):
    copies = jnp.broadcast_to(x[None], (len(groups[0]),) + x.shape)
    return lax.all_to_all(copies, "dp", 0, 0, axis_index_groups=groups, tiled=True)


def local(activations, out_grads, in_basis, out_basis, preconditioner, queries):
    rows = activations.shape[0]
    a_width, rank = in_basis.shape
    n = activations.shape[1] // a_width
    chips = n // 2
    split = LEN // rows

    *own, send = start(activations, out_grads, in_basis.T, out_basis.T, chips)
    theirs = swap(send, 1, n)
    up, down = [own], [own]
    for _ in range(chips // 2 - 1):
        up.append([ring(x, 1, chips) for x in up[-1]])
        down.append([ring(x, -1, chips) for x in down[-1]])
    last = chips // 2 - 1
    far = (ring(up[last][0], 1, chips), ring(down[last][1], -1, chips))

    tokens = activations, out_grads, theirs
    run = functools.partial(project, tokens, a_width=a_width, cut=own[0].shape[1])
    near, items = [*own], [(0, 0), (0, 1)]
    for i in range(1, last):
        near += [*up[i], *down[i]]
        items += [(offset, part) for offset in (i, -i) for part in range(2)]
    total = run(items, near)
    items = [(offset, part) for offset in (last, -last) for part in range(2)]
    total = run(items, [*up[last], *down[last]], total=total)
    for part, chunk in enumerate(far):
        total = run([(chips // 2, part)], [chunk], total=total)
    theirs = swap(total, 1, n)
    total = (total + jnp.concatenate([theirs[rows:], theirs[:rows]], axis=0)).astype(jnp.bfloat16)

    raw = dot(total[:, rank:], total[:, :rank], TN)
    raw = (raw * (1.0 / math.sqrt(LEN))).astype(jnp.bfloat16).reshape(-1, 128)
    planes = [[2 * i + c for i in range(chips)] for c in range(2)]
    raw = to_all(raw, planes).astype(jnp.float32)
    features = raw.reshape((-1, split // 2) + raw.shape[1:]).sum(axis=1)
    features = features.astype(jnp.bfloat16).reshape(-1, rank * rank)

    conditioned = dot(features, preconditioner, NT).astype(jnp.bfloat16)
    return score(to_all(conditioned, [list(range(n))]), queries, 1.0 / rank)


def local_gathered(activations, out_grads, in_basis, out_basis, preconditioner, queries):
    rows = activations.shape[0]
    rank = in_basis.shape[1]
    act_proj = jnp.dot(
        activations,
        lax.all_gather(in_basis, "dp", axis=0, tiled=True),
        preferred_element_type=jnp.float32,
    ).astype(jnp.bfloat16)
    grad_proj = jnp.dot(
        out_grads,
        lax.all_gather(out_basis, "dp", axis=0, tiled=True),
        preferred_element_type=jnp.float32,
    ).astype(jnp.bfloat16)
    raw = dot(grad_proj, act_proj, TN).reshape(1, rank * rank) * (1.0 / math.sqrt(LEN))
    gathered = lax.all_gather(raw, "dp", axis=0, tiled=True)
    features = gathered.reshape(-1, LEN // rows, rank * rank).sum(axis=1).astype(jnp.bfloat16)
    conditioned = dot(features, preconditioner, NT).astype(jnp.bfloat16)
    scores = dot(lax.all_gather(conditioned, "dp", axis=1, tiled=True), queries, NT)
    return scores * (1.0 / rank)


def power_of_two(x):
    return x > 0 and x & (x - 1) == 0


def solution(mesh):
    n = mesh.shape["dp"]

    def body(activations, out_grads, in_basis, out_basis, preconditioner, queries):
        aligned = all(x.shape[0] % 128 == 0 for x in (in_basis, out_basis, preconditioner))
        split = LEN // activations.shape[0]
        regular = aligned and n >= 8 and power_of_two(n) and power_of_two(split) and 4 <= split <= n
        form = local if regular else local_gathered
        return form(activations, out_grads, in_basis, out_basis, preconditioner, queries)

    return jax.shard_map(
        body,
        mesh=mesh,
        in_specs=(
            P(("parts", "dp"), None),
            P(("parts", "dp"), None),
            P("dp", None),
            P("dp", None),
            P("dp", None),
            P("dp", None),
        ),
        out_specs=P("parts", "dp"),
        check_vma=False,
    )
```

```python
import functools
import math

import jax
import jax.numpy as jnp
from jax import lax
from jax.experimental import pallas as pl
from jax.experimental.pallas import tpu as pltpu
from jax.sharding import PartitionSpec as P

LEN = 1024
NT = (((1,), (1,)), ((), ()))
TN = (((0,), (0,)), ((), ()))
VMEM = pl.BlockSpec(memory_space=pltpu.VMEM)
HBM = pl.BlockSpec(memory_space=pltpu.HBM)


def held(space, *arrays):
    return [pltpu.with_memory_space_constraint(x, space) for x in arrays]


def dot(a, b, dims):
    return lax.dot_general(a, b, dims, preferred_element_type=jnp.float32)


def chip_behind(offset, chips):
    chip = lax.axis_index("dp") >> 1
    z, y = chip >> 1, chip & 1
    place = (jnp.where(y == 0, z, chips - 1 - z) - offset) & (chips - 1)
    return jnp.where(place < chips // 2, 2 * place, 2 * (chips - 1 - place) + 1)


def ring(x, step, chips):
    half = chips // 2
    chip = [2 * p if p < half else 2 * (chips - 1 - p) + 1 for p in range(chips)]
    pairs = [
        (chip[p] * 2 + c, chip[(p + step) % chips] * 2 + 1 - c) for p in range(chips) for c in range(2)
    ]
    return lax.ppermute(x, "dp", pairs)


def swap(x, bit, n):
    return lax.ppermute(x, "dp", [(i, i ^ bit) for i in range(n)])


def odd(chip):
    return (chip ^ (chip >> 1)) & 1


def column_copies(chip, ring_core, act, grad, out, sems, chips):
    block = 2 * chip + (ring_core ^ odd(lax.axis_index("dp") >> 1) ^ odd(chip))
    a_width, g_width = (x.shape[1] // (2 * chips) for x in (act, grad))
    return [
        pltpu.make_async_copy(
            ref.at[:, pl.ds(pl.multiple_of(block * width, 128), width)],
            out.at[:, pl.ds(at, width)],
            sems.at[k],
        )
        for k, (ref, at, width) in enumerate(((act, 0, a_width), (grad, a_width, g_width)))
    ]


def run_copies(copies):
    for copy in copies:
        copy.start()
    for copy in copies:
        copy.wait()


def start_kernel(chips, act, grad, in_rows, out_rows, first, second, send, sems, send_sems):
    core = lax.axis_index("dp") & 1
    a_width = in_rows.shape[1]
    cut = first.shape[1]
    pairs = [
        (in_rows, first.at[:, pl.ds(0, a_width)]),
        (out_rows.at[:, pl.ds(0, cut - a_width)], first.at[:, pl.ds(a_width, cut - a_width)]),
        (out_rows.at[:, pl.ds(cut - a_width, second.shape[1])], second),
    ]
    copies = [pltpu.make_async_copy(*pair, sems.at[i]) for i, pair in enumerate(pairs)]
    for chip in range(chips):
        copies += column_copies(chip, 1 - core, act, grad, send.at[chip], send_sems.at[chip], chips)
    run_copies(copies)


def start(act, grad, in_rows, out_rows, chips):
    rows = act.shape[0]
    rank, width = in_rows.shape[0], in_rows.shape[1] + out_rows.shape[1]
    cut = (width // 256 + 1) * 128
    shapes = (rank, cut), (rank, width - cut), (chips, rows, width)
    return pl.pallas_call(
        functools.partial(start_kernel, chips),
        out_shape=[pltpu.VMEM(shape, act.dtype) for shape in shapes],
        in_specs=[HBM] * 4,
        out_specs=[VMEM] * 3,
        scratch_shapes=[pltpu.SemaphoreType.DMA((3,)), pltpu.SemaphoreType.DMA((chips, 2))],
        compiler_params=pltpu.CompilerParams(vmem_limit_bytes=16 * 2**20),
        cost_estimate=pl.CostEstimate(
            flops=0, bytes_accessed=4 * (rank + chips * rows) * width, transcendentals=0
        ),
    )(*held(pltpu.HBM, act, grad, in_rows, out_rows))


def project_kernel(chips, items, a_width, cut, carry, act, grad, theirs, *refs):
    chunks, refs = refs[: len(items)], refs[len(items) :]
    out = refs[-1]
    rank = chunks[0].shape[0]
    g_width = theirs.shape[2] - a_width
    me = lax.axis_index("dp")
    if carry:
        a_sum, g_sum = refs[0][:, :rank], refs[0][:, rank:]
    else:
        a_sum = g_sum = jnp.zeros((out.shape[0], rank), jnp.float32)
    for (offset, part), chunk in zip(items, chunks):
        chip = chip_behind(offset, chips)
        block = 2 * chip + ((me & 1) ^ odd(me >> 1) ^ odd(chip))

        def tokens(ref, width, skip, first, last):
            at = pl.multiple_of(block * width, 128) + (first - skip)
            return jnp.concatenate(
                [ref[:, pl.ds(at, last - first)], theirs[chip, :, first:last]], axis=0
            )

        if part == 0:
            a_sum += dot(tokens(act, a_width, 0, 0, a_width), chunk[:, :a_width], NT)
            g_sum += dot(tokens(grad, g_width, a_width, a_width, cut), chunk[:, a_width:], NT)
        else:
            g_sum += dot(tokens(grad, g_width, a_width, cut, theirs.shape[2]), chunk[...], NT)
    out[:, :rank] = a_sum
    out[:, rank:] = g_sum


def project(tokens, items, chunks, a_width, cut, total=None):
    chips, rows, _ = tokens[2].shape
    rank = chunks[0].shape[0]
    columns = sum(x.shape[1] for x in chunks)
    carried = [] if total is None else [total]
    return pl.pallas_call(
        functools.partial(project_kernel, chips, items, a_width, cut, total is not None),
        out_shape=pltpu.VMEM((2 * rows, 2 * rank), jnp.float32),
        in_specs=[VMEM] * (3 + len(chunks) + len(carried)),
        out_specs=VMEM,
        compiler_params=pltpu.CompilerParams(vmem_limit_bytes=16 * 2**20),
        cost_estimate=pl.CostEstimate(
            flops=4 * rows * rank * columns,
            bytes_accessed=(2 * rows + rank) * columns * 2,
            transcendentals=0,
        ),
    )(*held(pltpu.VMEM, *tokens, *chunks, *carried))


def score_kernel(scale, conditioned, queries, out):
    width = conditioned.shape[2]
    total = jnp.zeros(out.shape, jnp.float32)
    for i in range(conditioned.shape[0]):
        total += dot(conditioned[i], queries[:, i * width : (i + 1) * width], NT)
    out[...] = total * scale


def score(conditioned, queries, scale):
    return pl.pallas_call(
        functools.partial(score_kernel, scale),
        out_shape=jax.ShapeDtypeStruct((conditioned.shape[1], queries.shape[0]), jnp.float32),
        in_specs=[VMEM] * 2,
        out_specs=VMEM,
        compiler_params=pltpu.CompilerParams(vmem_limit_bytes=16 * 2**20),
    )(*held(pltpu.VMEM, conditioned, queries))


def to_all(x, groups):
    copies = jnp.broadcast_to(x[None], (len(groups[0]),) + x.shape)
    return lax.all_to_all(copies, "dp", 0, 0, axis_index_groups=groups, tiled=True)


def local(activations, out_grads, in_basis, out_basis, preconditioner, queries):
    rows = activations.shape[0]
    a_width, rank = in_basis.shape
    n = activations.shape[1] // a_width
    chips = n // 2
    split = LEN // rows

    *own, send = start(activations, out_grads, in_basis.T, out_basis.T, chips)
    theirs = swap(send, 1, n)
    up, down = [own], [own]
    for _ in range(chips // 2 - 1):
        up.append([ring(x, 1, chips) for x in up[-1]])
        down.append([ring(x, -1, chips) for x in down[-1]])
    last = chips // 2 - 1
    far = (ring(up[last][0], 1, chips), ring(down[last][1], -1, chips))

    tokens = activations, out_grads, theirs
    run = functools.partial(project, tokens, a_width=a_width, cut=own[0].shape[1])
    near, items = [*own], [(0, 0), (0, 1)]
    for i in range(1, last):
        near += [*up[i], *down[i]]
        items += [(offset, part) for offset in (i, -i) for part in range(2)]
    total = run(items, near)
    items = [(offset, part) for offset in (last, -last) for part in range(2)]
    total = run(items, [*up[last], *down[last]], total=total)
    for part, chunk in enumerate(far):
        total = run([(chips // 2, part)], [chunk], total=total)
    theirs = swap(total, 1, n)
    total = (total + jnp.concatenate([theirs[rows:], theirs[:rows]], axis=0)).astype(jnp.bfloat16)

    raw = dot(total[:, rank:], total[:, :rank], TN)
    raw = (raw * (1.0 / math.sqrt(LEN))).reshape(-1, 128)
    planes = [[2 * i + c for i in range(chips)] for c in range(2)]
    raw = to_all(raw, planes)
    features = raw.reshape((-1, split // 2) + raw.shape[1:]).sum(axis=1)
    features = features.astype(jnp.bfloat16).reshape(-1, rank * rank)

    conditioned = dot(features, preconditioner, NT).astype(jnp.bfloat16)
    return score(to_all(conditioned, [list(range(n))]), queries, 1.0 / rank)


def local_gathered(activations, out_grads, in_basis, out_basis, preconditioner, queries):
    rows = activations.shape[0]
    rank = in_basis.shape[1]
    act_proj = jnp.dot(
        activations,
        lax.all_gather(in_basis, "dp", axis=0, tiled=True),
        preferred_element_type=jnp.float32,
    ).astype(jnp.bfloat16)
    grad_proj = jnp.dot(
        out_grads,
        lax.all_gather(out_basis, "dp", axis=0, tiled=True),
        preferred_element_type=jnp.float32,
    ).astype(jnp.bfloat16)
    raw = dot(grad_proj, act_proj, TN).reshape(1, rank * rank) * (1.0 / math.sqrt(LEN))
    gathered = lax.all_gather(raw, "dp", axis=0, tiled=True)
    features = gathered.reshape(-1, LEN // rows, rank * rank).sum(axis=1).astype(jnp.bfloat16)
    conditioned = dot(features, preconditioner, NT).astype(jnp.bfloat16)
    scores = dot(lax.all_gather(conditioned, "dp", axis=1, tiled=True), queries, NT)
    return scores * (1.0 / rank)


def power_of_two(x):
    return x > 0 and x & (x - 1) == 0


def solution(mesh):
    n = mesh.shape["dp"]

    def body(activations, out_grads, in_basis, out_basis, preconditioner, queries):
        aligned = all(x.shape[0] % 128 == 0 for x in (in_basis, out_basis, preconditioner))
        split = LEN // activations.shape[0]
        regular = aligned and n >= 8 and power_of_two(n) and power_of_two(split) and 4 <= split <= n
        form = local if regular else local_gathered
        return form(activations, out_grads, in_basis, out_basis, preconditioner, queries)

    return jax.shard_map(
        body,
        mesh=mesh,
        in_specs=(
            P(("parts", "dp"), None),
            P(("parts", "dp"), None),
            P("dp", None),
            P("dp", None),
            P("dp", None),
            P("dp", None),
        ),
        out_specs=P("parts", "dp"),
        check_vma=False,
    )
```

```python
import functools
import math

import jax
import jax.numpy as jnp
from jax import lax
from jax.experimental import pallas as pl
from jax.experimental.pallas import tpu as pltpu
from jax.sharding import PartitionSpec as P

LEN = 1024
HIDE = 10**11
NT = (((1,), (1,)), ((), ()))
TN = (((0,), (0,)), ((), ()))
VMEM = pl.BlockSpec(memory_space=pltpu.VMEM)
HBM = pl.BlockSpec(memory_space=pltpu.HBM)


def held(space, *arrays):
    return [pltpu.with_memory_space_constraint(x, space) for x in arrays]


def dot(a, b, dims):
    return lax.dot_general(a, b, dims, preferred_element_type=jnp.float32)


def chip_behind(offset, chips):
    chip = lax.axis_index("dp") >> 1
    z, y = chip >> 1, chip & 1
    place = (jnp.where(y == 0, z, chips - 1 - z) - offset) & (chips - 1)
    return jnp.where(place < chips // 2, 2 * place, 2 * (chips - 1 - place) + 1)


def ring(x, step, chips):
    half = chips // 2
    chip = [2 * p if p < half else 2 * (chips - 1 - p) + 1 for p in range(chips)]
    pairs = [
        (chip[p] * 2 + c, chip[(p + step) % chips] * 2 + 1 - c) for p in range(chips) for c in range(2)
    ]
    return lax.ppermute(x, "dp", pairs)


def swap(x, bit, n):
    return lax.ppermute(x, "dp", [(i, i ^ bit) for i in range(n)])


def odd(chip):
    return (chip ^ (chip >> 1)) & 1


def column_copies(chip, ring_core, act, grad, out, sems, chips):
    block = 2 * chip + (ring_core ^ odd(lax.axis_index("dp") >> 1) ^ odd(chip))
    a_width, g_width = (x.shape[1] // (2 * chips) for x in (act, grad))
    return [
        pltpu.make_async_copy(
            ref.at[:, pl.ds(pl.multiple_of(block * width, 128), width)],
            out.at[:, pl.ds(at, width)],
            sems.at[k],
        )
        for k, (ref, at, width) in enumerate(((act, 0, a_width), (grad, a_width, g_width)))
    ]


def run_copies(copies):
    for copy in copies:
        copy.start()
    for copy in copies:
        copy.wait()


def start_kernel(chips, act, grad, in_rows, out_rows, first, second, send, sems, send_sems):
    core = lax.axis_index("dp") & 1
    a_width = in_rows.shape[1]
    cut = first.shape[1]
    pairs = [
        (in_rows, first.at[:, pl.ds(0, a_width)]),
        (out_rows.at[:, pl.ds(0, cut - a_width)], first.at[:, pl.ds(a_width, cut - a_width)]),
        (out_rows.at[:, pl.ds(cut - a_width, second.shape[1])], second),
    ]
    copies = [pltpu.make_async_copy(*pair, sems.at[i]) for i, pair in enumerate(pairs)]
    for chip in range(chips):
        copies += column_copies(chip, 1 - core, act, grad, send.at[chip], send_sems.at[chip], chips)
    run_copies(copies)


def start(act, grad, in_rows, out_rows, chips):
    rows = act.shape[0]
    rank, width = in_rows.shape[0], in_rows.shape[1] + out_rows.shape[1]
    cut = width // 256 * 128
    shapes = (rank, cut), (rank, width - cut), (chips, rows, width)
    return pl.pallas_call(
        functools.partial(start_kernel, chips),
        out_shape=[pltpu.VMEM(shape, act.dtype) for shape in shapes],
        in_specs=[HBM] * 4,
        out_specs=[VMEM] * 3,
        scratch_shapes=[pltpu.SemaphoreType.DMA((3,)), pltpu.SemaphoreType.DMA((chips, 2))],
        compiler_params=pltpu.CompilerParams(vmem_limit_bytes=16 * 2**20),
        cost_estimate=pl.CostEstimate(
            flops=0, bytes_accessed=4 * (rank + chips * rows) * width, transcendentals=0
        ),
    )(*held(pltpu.HBM, act, grad, in_rows, out_rows))


def project_kernel(chips, items, a_width, cut, carry, act, grad, *refs):
    theirs = None
    if carry:
        theirs, refs = refs[0], refs[1:]
    chunks, refs = refs[: len(items)], refs[len(items) :]
    out = refs[-1]
    rows, rank = act.shape[0], chunks[0].shape[0]
    g_width = grad.shape[1] // (2 * chips)
    me = lax.axis_index("dp")
    if carry:
        a_sum, g_sum = refs[0][:, :rank], refs[0][:, rank:]
    else:
        a_sum = g_sum = jnp.zeros((2 * rows, rank), jnp.float32)
    for (offset, part, whose), chunk in zip(items, chunks):
        chip = chip_behind(offset, chips)
        block = 2 * chip + ((me & 1) ^ odd(me >> 1) ^ odd(chip))

        def product(ref, width, skip, first, last, basis):
            at = pl.multiple_of(block * width, 128) + (first - skip)
            tokens = []
            if whose != 1:
                tokens.append(ref[:, pl.ds(at, last - first)])
            if whose != 0:
                tokens.append(theirs[chip, :, first:last])
            value = dot(jnp.concatenate(tokens, axis=0), basis, NT)
            if whose == 2:
                return value
            none = jnp.zeros((rows, rank), jnp.float32)
            return jnp.concatenate([none, value] if whose == 1 else [value, none], axis=0)

        if part == 0:
            a_sum += product(act, a_width, 0, 0, a_width, chunk[:, :a_width])
            g_sum += product(grad, g_width, a_width, a_width, cut, chunk[:, a_width:])
        else:
            g_sum += product(grad, g_width, a_width, cut, a_width + g_width, chunk[...])
    out[:, :rank] = a_sum
    out[:, rank:] = g_sum


def project(tokens, items, chunks, a_width, cut, total=None, hide=0):
    rows = tokens[0].shape[0]
    chips = tokens[0].shape[1] // (2 * a_width)
    rank = chunks[0].shape[0]
    columns = sum(x.shape[1] for x in chunks)
    carried = [] if total is None else [total]
    operands = [*tokens, *chunks, *carried]
    return pl.pallas_call(
        functools.partial(project_kernel, chips, items, a_width, cut, total is not None),
        out_shape=pltpu.VMEM((2 * rows, 2 * rank), jnp.float32),
        in_specs=[VMEM] * len(operands),
        out_specs=VMEM,
        compiler_params=pltpu.CompilerParams(vmem_limit_bytes=16 * 2**20),
        cost_estimate=pl.CostEstimate(
            flops=4 * rows * rank * columns + hide,
            bytes_accessed=(2 * rows + rank) * columns * 2,
            transcendentals=0,
        ),
    )(*held(pltpu.VMEM, *operands))


def score_kernel(scale, conditioned, queries, out):
    width = conditioned.shape[2]
    total = jnp.zeros(out.shape, jnp.float32)
    for i in range(conditioned.shape[0]):
        total += dot(conditioned[i], queries[:, i * width : (i + 1) * width], NT)
    out[...] = total * scale


def score(conditioned, queries, scale):
    return pl.pallas_call(
        functools.partial(score_kernel, scale),
        out_shape=jax.ShapeDtypeStruct((conditioned.shape[1], queries.shape[0]), jnp.float32),
        in_specs=[VMEM] * 2,
        out_specs=VMEM,
        compiler_params=pltpu.CompilerParams(vmem_limit_bytes=16 * 2**20),
    )(*held(pltpu.VMEM, conditioned, queries))


def to_all(x, groups):
    copies = jnp.broadcast_to(x[None], (len(groups[0]),) + x.shape)
    return lax.all_to_all(copies, "dp", 0, 0, axis_index_groups=groups, tiled=True)


def local(activations, out_grads, in_basis, out_basis, preconditioner, queries):
    rows = activations.shape[0]
    a_width, rank = in_basis.shape
    n = activations.shape[1] // a_width
    chips = n // 2
    split = LEN // rows

    *own, send = start(activations, out_grads, in_basis.T, out_basis.T, chips)
    theirs = swap(send, 1, n)
    run = functools.partial(project, a_width=a_width, cut=own[0].shape[1])
    mine = activations, out_grads
    last = chips // 2 - 1
    up, down = [own], [own]
    for i in range(last):
        if i == 1:
            total = run(mine, [(0, 0, 0), (0, 1, 0)], own, hide=HIDE)
            total, up[i][1] = lax.optimization_barrier((total, up[i][1]))
        up.append([ring(x, 1, chips) for x in up[-1]])
        down.append([ring(x, -1, chips) for x in down[-1]])
    far = (ring(up[last][0], 1, chips), ring(down[last][1], -1, chips))

    run = functools.partial(run, (*mine, theirs))
    near, items = [*own], [(0, 0, 1), (0, 1, 1)]
    for i in range(1, last):
        near += [*up[i], *down[i]]
        items += [(offset, part, 2) for offset in (i, -i) for part in range(2)]
    total = run(items, near, total=total)
    items = [(offset, part, 2) for offset in (last, -last) for part in range(2)]
    total = run(items, [*up[last], *down[last]], total=total)
    for part, chunk in enumerate(far):
        total = run([(chips // 2, part, 2)], [chunk], total=total)
    theirs = swap(total, 1, n)
    total = (total + jnp.concatenate([theirs[rows:], theirs[:rows]], axis=0)).astype(jnp.bfloat16)

    raw = dot(total[:, rank:], total[:, :rank], TN)
    raw = (raw * (1.0 / math.sqrt(LEN))).reshape(-1, 128)
    planes = [[2 * i + c for i in range(chips)] for c in range(2)]
    raw = to_all(raw, planes)
    features = raw.reshape((-1, split // 2) + raw.shape[1:]).sum(axis=1)
    features = features.astype(jnp.bfloat16).reshape(-1, rank * rank)

    conditioned = dot(features, preconditioner, NT).astype(jnp.bfloat16)
    return score(to_all(conditioned, [list(range(n))]), queries, 1.0 / rank)


def local_gathered(activations, out_grads, in_basis, out_basis, preconditioner, queries):
    rows = activations.shape[0]
    rank = in_basis.shape[1]
    act_proj = jnp.dot(
        activations,
        lax.all_gather(in_basis, "dp", axis=0, tiled=True),
        preferred_element_type=jnp.float32,
    ).astype(jnp.bfloat16)
    grad_proj = jnp.dot(
        out_grads,
        lax.all_gather(out_basis, "dp", axis=0, tiled=True),
        preferred_element_type=jnp.float32,
    ).astype(jnp.bfloat16)
    raw = dot(grad_proj, act_proj, TN).reshape(1, rank * rank) * (1.0 / math.sqrt(LEN))
    gathered = lax.all_gather(raw, "dp", axis=0, tiled=True)
    features = gathered.reshape(-1, LEN // rows, rank * rank).sum(axis=1).astype(jnp.bfloat16)
    conditioned = dot(features, preconditioner, NT).astype(jnp.bfloat16)
    scores = dot(lax.all_gather(conditioned, "dp", axis=1, tiled=True), queries, NT)
    return scores * (1.0 / rank)


def power_of_two(x):
    return x > 0 and x & (x - 1) == 0


def solution(mesh):
    n = mesh.shape["dp"]

    def body(activations, out_grads, in_basis, out_basis, preconditioner, queries):
        aligned = all(x.shape[0] % 128 == 0 for x in (in_basis, out_basis, preconditioner))
        split = LEN // activations.shape[0]
        regular = aligned and n >= 8 and power_of_two(n) and power_of_two(split) and 4 <= split <= n
        form = local if regular else local_gathered
        return form(activations, out_grads, in_basis, out_basis, preconditioner, queries)

    return jax.shard_map(
        body,
        mesh=mesh,
        in_specs=(
            P(("parts", "dp"), None),
            P(("parts", "dp"), None),
            P("dp", None),
            P("dp", None),
            P("dp", None),
            P("dp", None),
        ),
        out_specs=P("parts", "dp"),
        check_vma=False,
    )
```

```python
import functools
import math

import jax
import jax.numpy as jnp
from jax import lax
from jax.experimental import pallas as pl
from jax.experimental.pallas import tpu as pltpu
from jax.sharding import PartitionSpec as P

LEN = 1024
HIDE = 10**11
NT = (((1,), (1,)), ((), ()))
TN = (((0,), (0,)), ((), ()))
VMEM = pl.BlockSpec(memory_space=pltpu.VMEM)
HBM = pl.BlockSpec(memory_space=pltpu.HBM)


def held(space, *arrays):
    return [pltpu.with_memory_space_constraint(x, space) for x in arrays]


def dot(a, b, dims):
    return lax.dot_general(a, b, dims, preferred_element_type=jnp.float32)


def chip_behind(offset, chips):
    chip = lax.axis_index("dp") >> 1
    z, y = chip >> 1, chip & 1
    place = (jnp.where(y == 0, z, chips - 1 - z) - offset) & (chips - 1)
    return jnp.where(place < chips // 2, 2 * place, 2 * (chips - 1 - place) + 1)


def ring(x, step, chips):
    half = chips // 2
    chip = [2 * p if p < half else 2 * (chips - 1 - p) + 1 for p in range(chips)]
    pairs = [
        (chip[p] * 2 + c, chip[(p + step) % chips] * 2 + 1 - c) for p in range(chips) for c in range(2)
    ]
    return lax.ppermute(x, "dp", pairs)


def swap(x, bit, n):
    return lax.ppermute(x, "dp", [(i, i ^ bit) for i in range(n)])


def odd(chip):
    return (chip ^ (chip >> 1)) & 1


def column_copies(chip, ring_core, act, grad, out, sems, chips):
    block = 2 * chip + (ring_core ^ odd(lax.axis_index("dp") >> 1) ^ odd(chip))
    a_width, g_width = (x.shape[1] // (2 * chips) for x in (act, grad))
    return [
        pltpu.make_async_copy(
            ref.at[:, pl.ds(pl.multiple_of(block * width, 128), width)],
            out.at[:, pl.ds(at, width)],
            sems.at[k],
        )
        for k, (ref, at, width) in enumerate(((act, 0, a_width), (grad, a_width, g_width)))
    ]


def run_copies(copies):
    for copy in copies:
        copy.start()
    for copy in copies:
        copy.wait()


def chunk_kernel(in_rows, out_rows, first, second, sems):
    a_width = in_rows.shape[1]
    cut = first.shape[1]
    pairs = [
        (in_rows, first.at[:, pl.ds(0, a_width)]),
        (out_rows.at[:, pl.ds(0, cut - a_width)], first.at[:, pl.ds(a_width, cut - a_width)]),
        (out_rows.at[:, pl.ds(cut - a_width, second.shape[1])], second),
    ]
    run_copies([pltpu.make_async_copy(*pair, sems.at[i]) for i, pair in enumerate(pairs)])


def chunks_of(in_rows, out_rows):
    rank, width = in_rows.shape[0], in_rows.shape[1] + out_rows.shape[1]
    cut = width // 256 * 128
    return pl.pallas_call(
        chunk_kernel,
        out_shape=[pltpu.VMEM((rank, w), in_rows.dtype) for w in (cut, width - cut)],
        in_specs=[HBM] * 2,
        out_specs=[VMEM] * 2,
        scratch_shapes=[pltpu.SemaphoreType.DMA((3,))],
        compiler_params=pltpu.CompilerParams(vmem_limit_bytes=16 * 2**20),
        cost_estimate=pl.CostEstimate(
            flops=0, bytes_accessed=4 * rank * width, transcendentals=0
        ),
    )(*held(pltpu.HBM, in_rows, out_rows))


def pack_kernel(chips, act, grad, send, sems):
    core = lax.axis_index("dp") & 1
    copies = []
    for chip in range(chips):
        copies += column_copies(chip, 1 - core, act, grad, send.at[chip], sems.at[chip], chips)
    run_copies(copies)


def pack(act, grad, chips):
    rows, width = act.shape[0], (act.shape[1] + grad.shape[1]) // (2 * chips)
    return pl.pallas_call(
        functools.partial(pack_kernel, chips),
        out_shape=pltpu.VMEM((chips, rows, width), act.dtype),
        in_specs=[HBM] * 2,
        out_specs=VMEM,
        scratch_shapes=[pltpu.SemaphoreType.DMA((chips, 2))],
        compiler_params=pltpu.CompilerParams(vmem_limit_bytes=16 * 2**20),
        cost_estimate=pl.CostEstimate(
            flops=0, bytes_accessed=4 * chips * rows * width, transcendentals=0
        ),
    )(*held(pltpu.HBM, act, grad))


def project_kernel(chips, items, a_width, cut, carry, act, grad, *refs):
    theirs = None
    if carry:
        theirs, refs = refs[0], refs[1:]
    chunks, refs = refs[: len(items)], refs[len(items) :]
    out = refs[-1]
    rows, rank = act.shape[0], chunks[0].shape[0]
    g_width = grad.shape[1] // (2 * chips)
    me = lax.axis_index("dp")
    if carry:
        a_sum, g_sum = refs[0][:, :rank], refs[0][:, rank:]
    else:
        a_sum = g_sum = jnp.zeros((2 * rows, rank), jnp.float32)
    for (offset, part, whose), chunk in zip(items, chunks):
        chip = chip_behind(offset, chips)
        block = 2 * chip + ((me & 1) ^ odd(me >> 1) ^ odd(chip))

        def product(ref, width, skip, first, last, basis):
            at = pl.multiple_of(block * width, 128) + (first - skip)
            tokens = []
            if whose != 1:
                tokens.append(ref[:, pl.ds(at, last - first)])
            if whose != 0:
                tokens.append(theirs[chip, :, first:last])
            value = dot(jnp.concatenate(tokens, axis=0), basis, NT)
            if whose == 2:
                return value
            none = jnp.zeros((rows, rank), jnp.float32)
            return jnp.concatenate([none, value] if whose == 1 else [value, none], axis=0)

        if part == 0:
            a_sum += product(act, a_width, 0, 0, a_width, chunk[:, :a_width])
            g_sum += product(grad, g_width, a_width, a_width, cut, chunk[:, a_width:])
        else:
            g_sum += product(grad, g_width, a_width, cut, a_width + g_width, chunk[...])
    out[:, :rank] = a_sum
    out[:, rank:] = g_sum


def project(tokens, items, chunks, a_width, cut, total=None, hide=0):
    rows = tokens[0].shape[0]
    chips = tokens[0].shape[1] // (2 * a_width)
    rank = chunks[0].shape[0]
    columns = sum(x.shape[1] for x in chunks)
    carried = [] if total is None else [total]
    operands = [*tokens, *chunks, *carried]
    return pl.pallas_call(
        functools.partial(project_kernel, chips, items, a_width, cut, total is not None),
        out_shape=pltpu.VMEM((2 * rows, 2 * rank), jnp.float32),
        in_specs=[VMEM] * len(operands),
        out_specs=VMEM,
        compiler_params=pltpu.CompilerParams(vmem_limit_bytes=16 * 2**20),
        cost_estimate=pl.CostEstimate(
            flops=4 * rows * rank * columns + hide,
            bytes_accessed=(2 * rows + rank) * columns * 2,
            transcendentals=0,
        ),
    )(*held(pltpu.VMEM, *operands))


def score_kernel(scale, conditioned, queries, out):
    width = conditioned.shape[2]
    total = jnp.zeros(out.shape, jnp.float32)
    for i in range(conditioned.shape[0]):
        total += dot(conditioned[i], queries[:, i * width : (i + 1) * width], NT)
    out[...] = total * scale


def score(conditioned, queries, scale):
    return pl.pallas_call(
        functools.partial(score_kernel, scale),
        out_shape=jax.ShapeDtypeStruct((conditioned.shape[1], queries.shape[0]), jnp.float32),
        in_specs=[VMEM] * 2,
        out_specs=VMEM,
        compiler_params=pltpu.CompilerParams(vmem_limit_bytes=16 * 2**20),
    )(*held(pltpu.VMEM, conditioned, queries))


def to_all(x, groups):
    copies = jnp.broadcast_to(x[None], (len(groups[0]),) + x.shape)
    return lax.all_to_all(copies, "dp", 0, 0, axis_index_groups=groups, tiled=True)


def local(activations, out_grads, in_basis, out_basis, preconditioner, queries):
    rows = activations.shape[0]
    a_width, rank = in_basis.shape
    n = activations.shape[1] // a_width
    chips = n // 2
    split = LEN // rows

    own = list(chunks_of(in_basis.T, out_basis.T))
    theirs = swap(pack(activations, out_grads, chips), 1, n)
    run = functools.partial(project, a_width=a_width, cut=own[0].shape[1])
    mine = activations, out_grads
    last = chips // 2 - 1
    up, down = [own], [own]
    for i in range(last):
        if i == 1:
            total = run(mine, [(0, 0, 0), (0, 1, 0)], own, hide=HIDE)
            total, up[i][1] = lax.optimization_barrier((total, up[i][1]))
        up.append([ring(x, 1, chips) for x in up[-1]])
        down.append([ring(x, -1, chips) for x in down[-1]])
    far = (ring(up[last][0], 1, chips), ring(down[last][1], -1, chips))

    run = functools.partial(run, (*mine, theirs))
    near, items = [*own], [(0, 0, 1), (0, 1, 1)]
    for i in range(1, last):
        near += [*up[i], *down[i]]
        items += [(offset, part, 2) for offset in (i, -i) for part in range(2)]
    total = run(items, near, total=total)
    items = [(offset, part, 2) for offset in (last, -last) for part in range(2)]
    total = run(items, [*up[last], *down[last]], total=total)
    for part, chunk in enumerate(far):
        total = run([(chips // 2, part, 2)], [chunk], total=total)
    theirs = swap(total, 1, n)
    total = (total + jnp.concatenate([theirs[rows:], theirs[:rows]], axis=0)).astype(jnp.bfloat16)

    raw = dot(total[:, rank:], total[:, :rank], TN)
    raw = (raw * (1.0 / math.sqrt(LEN))).reshape(-1, 128)
    planes = [[2 * i + c for i in range(chips)] for c in range(2)]
    raw = to_all(raw, planes)
    features = raw.reshape((-1, split // 2) + raw.shape[1:]).sum(axis=1)
    features = features.astype(jnp.bfloat16).reshape(-1, rank * rank)

    conditioned = dot(features, preconditioner, NT).astype(jnp.bfloat16)
    return score(to_all(conditioned, [list(range(n))]), queries, 1.0 / rank)


def local_gathered(activations, out_grads, in_basis, out_basis, preconditioner, queries):
    rows = activations.shape[0]
    rank = in_basis.shape[1]
    act_proj = jnp.dot(
        activations,
        lax.all_gather(in_basis, "dp", axis=0, tiled=True),
        preferred_element_type=jnp.float32,
    ).astype(jnp.bfloat16)
    grad_proj = jnp.dot(
        out_grads,
        lax.all_gather(out_basis, "dp", axis=0, tiled=True),
        preferred_element_type=jnp.float32,
    ).astype(jnp.bfloat16)
    raw = dot(grad_proj, act_proj, TN).reshape(1, rank * rank) * (1.0 / math.sqrt(LEN))
    gathered = lax.all_gather(raw, "dp", axis=0, tiled=True)
    features = gathered.reshape(-1, LEN // rows, rank * rank).sum(axis=1).astype(jnp.bfloat16)
    conditioned = dot(features, preconditioner, NT).astype(jnp.bfloat16)
    scores = dot(lax.all_gather(conditioned, "dp", axis=1, tiled=True), queries, NT)
    return scores * (1.0 / rank)


def power_of_two(x):
    return x > 0 and x & (x - 1) == 0


def solution(mesh):
    n = mesh.shape["dp"]

    def body(activations, out_grads, in_basis, out_basis, preconditioner, queries):
        aligned = all(x.shape[0] % 128 == 0 for x in (in_basis, out_basis, preconditioner))
        split = LEN // activations.shape[0]
        regular = aligned and n >= 8 and power_of_two(n) and power_of_two(split) and 4 <= split <= n
        form = local if regular else local_gathered
        return form(activations, out_grads, in_basis, out_basis, preconditioner, queries)

    return jax.shard_map(
        body,
        mesh=mesh,
        in_specs=(
            P(("parts", "dp"), None),
            P(("parts", "dp"), None),
            P("dp", None),
            P("dp", None),
            P("dp", None),
            P("dp", None),
        ),
        out_specs=P("parts", "dp"),
        check_vma=False,
    )
```

```python
import functools
import math

import jax
import jax.numpy as jnp
from jax import lax
from jax.experimental import pallas as pl
from jax.experimental.pallas import tpu as pltpu
from jax.sharding import PartitionSpec as P

LEN = 1024
HIDE = 10**11
NT = (((1,), (1,)), ((), ()))
TN = (((0,), (0,)), ((), ()))
VMEM = pl.BlockSpec(memory_space=pltpu.VMEM)
HBM = pl.BlockSpec(memory_space=pltpu.HBM)


def held(space, *arrays):
    return [pltpu.with_memory_space_constraint(x, space) for x in arrays]


def dot(a, b, dims):
    return lax.dot_general(a, b, dims, preferred_element_type=jnp.float32)


def chip_behind(offset, chips):
    chip = lax.axis_index("dp") >> 1
    z, y = chip >> 1, chip & 1
    place = (jnp.where(y == 0, z, chips - 1 - z) - offset) & (chips - 1)
    return jnp.where(place < chips // 2, 2 * place, 2 * (chips - 1 - place) + 1)


def ring(x, step, chips):
    half = chips // 2
    chip = [2 * p if p < half else 2 * (chips - 1 - p) + 1 for p in range(chips)]
    pairs = [
        (chip[p] * 2 + c, chip[(p + step) % chips] * 2 + 1 - c) for p in range(chips) for c in range(2)
    ]
    return lax.ppermute(x, "dp", pairs)


def swap(x, bit, n):
    return lax.ppermute(x, "dp", [(i, i ^ bit) for i in range(n)])


def odd(chip):
    return (chip ^ (chip >> 1)) & 1


def column_copies(chip, ring_core, act, grad, out, sems, chips):
    block = 2 * chip + (ring_core ^ odd(lax.axis_index("dp") >> 1) ^ odd(chip))
    a_width, g_width = (x.shape[1] // (2 * chips) for x in (act, grad))
    return [
        pltpu.make_async_copy(
            ref.at[:, pl.ds(pl.multiple_of(block * width, 128), width)],
            out.at[:, pl.ds(at, width)],
            sems.at[k],
        )
        for k, (ref, at, width) in enumerate(((act, 0, a_width), (grad, a_width, g_width)))
    ]


def run_copies(copies):
    for copy in copies:
        copy.start()
    for copy in copies:
        copy.wait()


def chunk_kernel(in_rows, out_rows, first, second, sems):
    a_width = in_rows.shape[1]
    cut = first.shape[1]
    pairs = [
        (in_rows, first.at[:, pl.ds(0, a_width)]),
        (out_rows.at[:, pl.ds(0, cut - a_width)], first.at[:, pl.ds(a_width, cut - a_width)]),
        (out_rows.at[:, pl.ds(cut - a_width, second.shape[1])], second),
    ]
    run_copies([pltpu.make_async_copy(*pair, sems.at[i]) for i, pair in enumerate(pairs)])


def chunks_of(in_rows, out_rows):
    rank, width = in_rows.shape[0], in_rows.shape[1] + out_rows.shape[1]
    cut = width // 256 * 128
    return pl.pallas_call(
        chunk_kernel,
        out_shape=[pltpu.VMEM((rank, w), in_rows.dtype) for w in (cut, width - cut)],
        in_specs=[HBM] * 2,
        out_specs=[VMEM] * 2,
        scratch_shapes=[pltpu.SemaphoreType.DMA((3,))],
        compiler_params=pltpu.CompilerParams(vmem_limit_bytes=16 * 2**20),
        cost_estimate=pl.CostEstimate(
            flops=0, bytes_accessed=4 * rank * width, transcendentals=0
        ),
    )(*held(pltpu.HBM, in_rows, out_rows))


def pack_kernel(chips, act, grad, send, sems):
    core = lax.axis_index("dp") & 1
    copies = []
    for chip in range(chips):
        copies += column_copies(chip, 1 - core, act, grad, send.at[chip], sems.at[chip], chips)
    run_copies(copies)


def pack(act, grad, chips):
    rows, width = act.shape[0], (act.shape[1] + grad.shape[1]) // (2 * chips)
    return pl.pallas_call(
        functools.partial(pack_kernel, chips),
        out_shape=pltpu.VMEM((chips, rows, width), act.dtype),
        in_specs=[HBM] * 2,
        out_specs=VMEM,
        scratch_shapes=[pltpu.SemaphoreType.DMA((chips, 2))],
        compiler_params=pltpu.CompilerParams(vmem_limit_bytes=16 * 2**20),
        cost_estimate=pl.CostEstimate(
            flops=0, bytes_accessed=4 * chips * rows * width, transcendentals=0
        ),
    )(*held(pltpu.HBM, act, grad))


def project_kernel(chips, items, a_width, cut, carry, act, grad, *refs):
    theirs = None
    if carry:
        theirs, refs = refs[0], refs[1:]
    chunks, refs = refs[: len(items)], refs[len(items) :]
    out = refs[-1]
    rows, rank = act.shape[0], chunks[0].shape[0]
    g_width = grad.shape[1] // (2 * chips)
    me = lax.axis_index("dp")
    if carry:
        a_sum, g_sum = refs[0][:, :rank], refs[0][:, rank:]
    else:
        a_sum = g_sum = jnp.zeros((2 * rows, rank), jnp.float32)
    for (offset, part, whose), chunk in zip(items, chunks):
        chip = chip_behind(offset, chips)
        block = 2 * chip + ((me & 1) ^ odd(me >> 1) ^ odd(chip))

        def product(ref, width, skip, first, last, basis):
            at = pl.multiple_of(block * width, 128) + (first - skip)
            tokens = []
            if whose != 1:
                tokens.append(ref[:, pl.ds(at, last - first)])
            if whose != 0:
                tokens.append(theirs[chip, :, first:last])
            value = dot(jnp.concatenate(tokens, axis=0), basis, NT)
            if whose == 2:
                return value
            none = jnp.zeros((rows, rank), jnp.float32)
            return jnp.concatenate([none, value] if whose == 1 else [value, none], axis=0)

        if part == 0:
            a_sum += product(act, a_width, 0, 0, a_width, chunk[:, :a_width])
            g_sum += product(grad, g_width, a_width, a_width, cut, chunk[:, a_width:])
        else:
            g_sum += product(grad, g_width, a_width, cut, a_width + g_width, chunk[...])
    out[:, :rank] = a_sum
    out[:, rank:] = g_sum


def project(tokens, items, chunks, a_width, cut, total=None, hide=0):
    rows = tokens[0].shape[0]
    chips = tokens[0].shape[1] // (2 * a_width)
    rank = chunks[0].shape[0]
    columns = sum(x.shape[1] for x in chunks)
    carried = [] if total is None else [total]
    operands = [*tokens, *chunks, *carried]
    return pl.pallas_call(
        functools.partial(project_kernel, chips, items, a_width, cut, total is not None),
        out_shape=pltpu.VMEM((2 * rows, 2 * rank), jnp.float32),
        in_specs=[VMEM] * len(operands),
        out_specs=VMEM,
        compiler_params=pltpu.CompilerParams(vmem_limit_bytes=16 * 2**20),
        cost_estimate=pl.CostEstimate(
            flops=4 * rows * rank * columns + hide,
            bytes_accessed=(2 * rows + rank) * columns * 2,
            transcendentals=0,
        ),
    )(*held(pltpu.VMEM, *operands))


def score_kernel(scale, conditioned, queries, out):
    width = conditioned.shape[2]
    total = jnp.zeros(out.shape, jnp.float32)
    for i in range(conditioned.shape[0]):
        total += dot(conditioned[i], queries[:, i * width : (i + 1) * width], NT)
    out[...] = total * scale


def score(conditioned, queries, scale):
    return pl.pallas_call(
        functools.partial(score_kernel, scale),
        out_shape=jax.ShapeDtypeStruct((conditioned.shape[1], queries.shape[0]), jnp.float32),
        in_specs=[VMEM] * 2,
        out_specs=VMEM,
        compiler_params=pltpu.CompilerParams(vmem_limit_bytes=16 * 2**20),
    )(*held(pltpu.VMEM, conditioned, queries))


def to_all(x, groups):
    copies = jnp.broadcast_to(x[None], (len(groups[0]),) + x.shape)
    return lax.all_to_all(copies, "dp", 0, 0, axis_index_groups=groups, tiled=True)


def local(activations, out_grads, in_basis, out_basis, preconditioner, queries):
    rows = activations.shape[0]
    a_width, rank = in_basis.shape
    n = activations.shape[1] // a_width
    chips = n // 2
    split = LEN // rows

    own = list(chunks_of(in_basis.T, out_basis.T))
    theirs = swap(pack(activations, out_grads, chips), 1, n)
    run = functools.partial(project, a_width=a_width, cut=own[0].shape[1])
    mine = activations, out_grads
    last = chips // 2 - 1
    up, down = [own], [own]
    for i in range(last):
        if i == 1:
            total = run(mine, [(0, 0, 0), (0, 1, 0)], own, hide=HIDE)
            total, up[i][1] = lax.optimization_barrier((total, up[i][1]))
        up.append([ring(x, 1, chips) for x in up[-1]])
        down.append([ring(x, -1, chips) for x in down[-1]])
    far = (ring(up[last][0], 1, chips), ring(down[last][1], -1, chips))

    run = functools.partial(run, (*mine, theirs))
    near, items = [*own], [(0, 0, 1), (0, 1, 1)]
    for i in range(1, last):
        near += [*up[i], *down[i]]
        items += [(offset, part, 2) for offset in (i, -i) for part in range(2)]
    total = run(items, near, total=total)
    items = [(offset, part, 2) for offset in (last, -last) for part in range(2)]
    total = run(items, [*up[last], *down[last]], total=total)
    for part, chunk in enumerate(far):
        total = run([(chips // 2, part, 2)], [chunk], total=total)
    theirs = swap(total, 1, n)
    total = (total + jnp.concatenate([theirs[rows:], theirs[:rows]], axis=0)).astype(jnp.bfloat16)

    raw = dot(total[:, rank:], total[:, :rank], TN)
    raw = (raw * (1.0 / math.sqrt(LEN))).astype(jnp.bfloat16).reshape(-1, 128)
    planes = [[2 * i + c for i in range(chips)] for c in range(2)]
    raw = to_all(raw, planes).astype(jnp.float32)
    features = raw.reshape((-1, split // 2) + raw.shape[1:]).sum(axis=1)
    features = features.astype(jnp.bfloat16).reshape(-1, rank * rank)

    conditioned = dot(features, preconditioner, NT).astype(jnp.bfloat16)
    return score(to_all(conditioned, [list(range(n))]), queries, 1.0 / rank)


def local_gathered(activations, out_grads, in_basis, out_basis, preconditioner, queries):
    rows = activations.shape[0]
    rank = in_basis.shape[1]
    act_proj = jnp.dot(
        activations,
        lax.all_gather(in_basis, "dp", axis=0, tiled=True),
        preferred_element_type=jnp.float32,
    ).astype(jnp.bfloat16)
    grad_proj = jnp.dot(
        out_grads,
        lax.all_gather(out_basis, "dp", axis=0, tiled=True),
        preferred_element_type=jnp.float32,
    ).astype(jnp.bfloat16)
    raw = dot(grad_proj, act_proj, TN).reshape(1, rank * rank) * (1.0 / math.sqrt(LEN))
    gathered = lax.all_gather(raw, "dp", axis=0, tiled=True)
    features = gathered.reshape(-1, LEN // rows, rank * rank).sum(axis=1).astype(jnp.bfloat16)
    conditioned = dot(features, preconditioner, NT).astype(jnp.bfloat16)
    scores = dot(lax.all_gather(conditioned, "dp", axis=1, tiled=True), queries, NT)
    return scores * (1.0 / rank)


def power_of_two(x):
    return x > 0 and x & (x - 1) == 0


def solution(mesh):
    n = mesh.shape["dp"]

    def body(activations, out_grads, in_basis, out_basis, preconditioner, queries):
        aligned = all(x.shape[0] % 128 == 0 for x in (in_basis, out_basis, preconditioner))
        split = LEN // activations.shape[0]
        regular = aligned and n >= 8 and power_of_two(n) and power_of_two(split) and 4 <= split <= n
        form = local if regular else local_gathered
        return form(activations, out_grads, in_basis, out_basis, preconditioner, queries)

    return jax.shard_map(
        body,
        mesh=mesh,
        in_specs=(
            P(("parts", "dp"), None),
            P(("parts", "dp"), None),
            P("dp", None),
            P("dp", None),
            P("dp", None),
            P("dp", None),
        ),
        out_specs=P("parts", "dp"),
        check_vma=False,
    )
```
